256 devices in a mesh: row: 16 (over y, x_hi, core), col: 16 (over x_lo, z).
Axes of the slice: x: 4 (x_hi: 2, x_lo: 2; x = x_hi * 2 + x_lo), y: 4, z: 8, core: 2. Of those that a mesh axis runs over, the one named last changes fastest.
Arguments:
- patch_tokens: bfloat16 [256, 256, 3072], P('row', 'col'), may hold values from -6 to 6
- queries: bfloat16 [256, 256, 1536], P('row', 'col'), may hold values from -6 to 6
- key_vectors: bfloat16 [256, 256, 1536], P('row', 'col'), may hold values from -6 to 6
- cotangent: bfloat16 [256, 256, 1536], P('row', 'col'), may hold values from -6 to 6
- value_weight: bfloat16 [3072, 1536], P(('row', 'col')), may hold values from -0.109375 to 0.109375
- adapter_down: bfloat16 [3072, 64], replicated, may hold values from -0.109375 to 0.109375
- adapter_up: bfloat16 [64, 1536], replicated, may hold values from -0.75 to 0.75
- radius: int32 [12], replicated, may hold values from 1 to 16, as said below
- tile_mask: int32 [16, 16, 9], P('row', 'col'), may hold values from 0 to 1, as said below
Outputs:
- attended: bfloat16 [256, 256, 1536], P('row', 'col')
- grad_down: float32 [3072, 64], P(('row', 'col'))
- grad_up: float32 [64, 1536], replicated
The draws below stay inside these ranges and needn't reach their ends.
Inputs may be any that keep to these rules, and one draw needn't show every extreme that they name: Some head has radius exactly 16. `tile_mask`: the centre entry (index 4) is 1 for every tile.
All inputs are finite; a program needn't handle non-finite values.
Results may differ from the reference program's by a relative error of at most 0.0061.
Values may be sent and summed in bfloat16 or wider, within the bound.
A program may use at most 128 MiB of HBM per device.

```python
import jax
import jax.numpy as jnp
from jax import lax

TILE = 16
D = 3072
H = 12
HEAD = 128
RANK = 64
HD = 1536
ROWS = 256
COLS = 256
TOKENS = 65536
N_ROW = 16
N_COL = 16


def shared_fields(key):
    first, second = jax.random.split(key, 2)
    shape = (ROWS, COLS, H, HEAD)
    query_base = jnp.clip(jax.random.normal(first, shape, jnp.float32), -6.0, 6.0)
    key_base = jnp.clip(jax.random.normal(second, shape, jnp.float32), -6.0, 6.0)
    return (query_base, key_base)


def draw_queries(key, part):
    query_base, key_base = shared_fields(key)
    return query_base.reshape(ROWS, COLS, H * HEAD).astype(jnp.bfloat16)


def draw_key_vectors(key, part):
    query_base, key_base = shared_fields(key)
    return key_base.reshape(ROWS, COLS, H * HEAD).astype(jnp.bfloat16)


def draw_radius(key, part):
    key = jax.random.fold_in(key, 7)
    first, second = jax.random.split(key)
    radii = jax.random.randint(first, (H,), 1, TILE + 1)
    chosen = jax.random.randint(second, (), 0, H)
    return jnp.where(jnp.arange(H) == chosen, TILE, radii).astype(jnp.int32)


def draw_tile_mask(key, part):
    key = jax.random.fold_in(key, 9)
    flags = (jax.random.randint(key, (N_ROW, N_COL, 9), 0, 4) > 0).astype(jnp.int32)
    centre = (jnp.arange(9) == 4)[None, None, :]
    return jnp.where(centre, 1, flags).astype(jnp.int32)


def strengthened(result, rng, source, target, parts, factor):
    owner, partner = [(jnp.arange(result.shape[position]) // (result.shape[position] // parts)).reshape([-1 if axis == position else 1 for axis in range(result.ndim)]) for position in (source, target)]
    chosen = jax.random.permutation(rng, parts)[partner]
    strong = (owner == chosen) | (owner == (partner + parts // 2) % parts)
    return jnp.where(strong, factor * result, result)


def level_of(rng, shape, cuts, low, top_value):
    loudness, own = 1.0, jax.random.fold_in(rng, 6)
    for position, shards_of in cuts:
        steps = jnp.exp(jax.random.uniform(jax.random.fold_in(own, position), (shards_of,), jnp.float32, low / len(cuts), top_value / len(cuts)))
        loudness = loudness * jnp.repeat(steps, shape[position] // shards_of).reshape([-1 if axis == position else 1 for axis in range(len(shape))])
    return loudness


def normal_values(stream_key, dims, spread, limit, cuts=(), kind=jnp.bfloat16):
    entries = spread * jax.random.normal(stream_key, dims, jnp.float32)
    if cuts:
        entries = entries * level_of(stream_key, dims, cuts, -0.22, 0.18)
    return jnp.clip(entries, -limit, limit).astype(kind)


def bell_draw_with(rng, extent, scale, bound, cuts, heavy, kind=jnp.bfloat16):
    values = scale * jax.random.normal(rng, extent, jnp.float32)
    if cuts:
        values = values * level_of(rng, extent, cuts, -0.22, 0.18)
    return jnp.clip(strengthened(values, jax.random.fold_in(rng, 3), *heavy), -bound, bound).astype(kind)


def setup_inputs(seed: int = 0) -> dict:
    splits = jax.random.split(jax.random.key(seed), 10)
    patch_tokens = bell_draw_with(splits[0], (ROWS, COLS, D), 1.0, 6.0, ((0, 16), (1, 16)), (0, 2, 16, 2.0))
    queries = draw_queries(jax.random.fold_in(splits[9], 71), 0)
    key_vectors = draw_key_vectors(jax.random.fold_in(splits[9], 71), 0)
    cotangent = normal_values(splits[3], (ROWS, COLS, HD), 1.0, 6.0, ((0, 16), (1, 16)))
    value_weight = normal_values(splits[4], (D, HD), D ** -0.5, 0.109375, ((0, 256),))
    adapter_down = normal_values(splits[5], (D, RANK), D ** -0.5, 0.109375)
    adapter_up = normal_values(splits[6], (RANK, HD), RANK ** -0.5, 0.75)
    radius = draw_radius(jax.random.fold_in(splits[9], 71), 0)
    tile_mask = draw_tile_mask(jax.random.fold_in(splits[9], 71), 0)
    return dict(patch_tokens=patch_tokens, queries=queries, key_vectors=key_vectors, cotangent=cotangent, value_weight=value_weight, adapter_down=adapter_down, adapter_up=adapter_up, radius=radius, tile_mask=tile_mask)


neg_fill = -1.0e30


def window_geometry(tile_side, row_tile, col_tile, rows_total, cols_total, mask_nine):
    window_side = 3 * tile_side
    query_pos = lax.iota(jnp.int32, tile_side * tile_side)
    query_row = query_pos // tile_side
    query_col = query_pos % tile_side
    key_pos = lax.iota(jnp.int32, window_side * window_side)
    key_row = key_pos // window_side
    key_col = key_pos % window_side
    row_gap = key_row[None, :] - tile_side - query_row[:, None]
    col_gap = key_col[None, :] - tile_side - query_col[:, None]
    distance = row_gap * row_gap + col_gap * col_gap
    global_row = row_tile * tile_side + key_row - tile_side
    global_col = col_tile * tile_side + key_col - tile_side
    in_image = (global_row >= 0) & (global_row < rows_total) & (global_col >= 0) & (global_col < cols_total)
    block_index = (key_row // tile_side) * 3 + key_col // tile_side
    nine = lax.iota(jnp.int32, 9)
    permitted = jnp.sum(jnp.where(block_index[:, None] == nine[None, :], mask_nine[None, :], 0), axis=1) > 0
    allowed = jnp.broadcast_to((in_image & permitted)[None, :], distance.shape)
    return allowed, distance


def window_heads(query_rows, key_rows, value_rows, cotangent_rows, allowed, distance, radius, head_size):
    head_count = radius.shape[0]

    def one_head(head_index):
        offset = head_index * head_size
        query_part = lax.dynamic_slice_in_dim(query_rows, offset, head_size, 1)
        key_part = lax.dynamic_slice_in_dim(key_rows, offset, head_size, 1)
        value_part = lax.dynamic_slice_in_dim(value_rows, offset, head_size, 1)
        cotangent_part = lax.dynamic_slice_in_dim(cotangent_rows, offset, head_size, 1)
        scores = lax.dot_general(query_part, key_part, (((1,), (1,)), ((), ())), preferred_element_type=jnp.float32)
        scores = scores * (head_size ** -0.5)
        inside = allowed & (distance <= radius[head_index] * radius[head_index])
        scores = jnp.where(inside, scores, neg_fill)
        row_max = jnp.max(scores, axis=1, keepdims=True)
        unnormed = jnp.where(inside, jnp.exp(scores - row_max), 0.0)
        weights = (unnormed / jnp.sum(unnormed, axis=1, keepdims=True)).astype(jnp.bfloat16)
        head_out = jnp.dot(weights, value_part, preferred_element_type=jnp.float32).astype(jnp.bfloat16)
        head_grad = lax.dot_general(weights, cotangent_part, (((0,), (0,)), ((), ())), preferred_element_type=jnp.float32).astype(jnp.bfloat16)
        return head_out, head_grad

    outputs, grads = lax.map(one_head, jnp.arange(head_count, dtype=jnp.int32))
    outputs = outputs.transpose(1, 0, 2).reshape(query_rows.shape[0], head_count * head_size)
    grads = grads.transpose(1, 0, 2).reshape(key_rows.shape[0], head_count * head_size)
    return outputs, grads


def reference(patch_tokens, queries, key_vectors, cotangent, value_weight, adapter_down, adapter_up, radius, tile_mask):
    flat_tokens = patch_tokens.reshape(TOKENS, D)
    lowrank = jnp.dot(flat_tokens, adapter_down, preferred_element_type=jnp.float32).astype(jnp.bfloat16)
    values = (jnp.dot(flat_tokens, value_weight, preferred_element_type=jnp.float32)
              + jnp.dot(lowrank, adapter_up, preferred_element_type=jnp.float32)).astype(jnp.bfloat16)
    packed = jnp.concatenate([key_vectors, values.reshape(ROWS, COLS, HD), lowrank.reshape(ROWS, COLS, RANK)], axis=2)
    padded = jnp.pad(packed, ((TILE, TILE), (TILE, TILE), (0, 0)))
    zero_index = jnp.zeros((), jnp.int32)

    def visit(carry, tile_number):
        back_pad, up_total = carry
        row_tile = (tile_number // N_COL).astype(jnp.int32)
        col_tile = (tile_number % N_COL).astype(jnp.int32)
        row_start = (row_tile * TILE).astype(jnp.int32)
        col_start = (col_tile * TILE).astype(jnp.int32)
        window = lax.dynamic_slice(padded, (row_start, col_start, zero_index), (3 * TILE, 3 * TILE, 2 * HD + RANK))
        window = window.reshape(9 * TILE * TILE, 2 * HD + RANK)
        query_rows = lax.dynamic_slice(queries, (row_start, col_start, zero_index), (TILE, TILE, HD)).reshape(TILE * TILE, HD)
        cotangent_rows = lax.dynamic_slice(cotangent, (row_start, col_start, zero_index), (TILE, TILE, HD)).reshape(TILE * TILE, HD)
        mask_nine = lax.dynamic_slice(tile_mask, (row_tile, col_tile, zero_index), (1, 1, 9)).reshape(9)
        allowed, distance = window_geometry(TILE, row_tile, col_tile, ROWS, COLS, mask_nine)
        head_out, value_grad = window_heads(query_rows, window[:, :HD], window[:, HD:2 * HD], cotangent_rows, allowed, distance, radius, HEAD)
        up_total = up_total + lax.dot_general(window[:, 2 * HD:], value_grad, (((0,), (0,)), ((), ())), preferred_element_type=jnp.float32)
        back_window = lax.dot_general(value_grad, adapter_up, (((1,), (1,)), ((), ())), preferred_element_type=jnp.float32)
        current = lax.dynamic_slice(back_pad, (row_start, col_start, zero_index), (3 * TILE, 3 * TILE, RANK))
        back_pad = lax.dynamic_update_slice(back_pad, current + back_window.reshape(3 * TILE, 3 * TILE, RANK), (row_start, col_start, zero_index))
        return (back_pad, up_total), head_out

    start = (jnp.zeros((ROWS + 2 * TILE, COLS + 2 * TILE, RANK), jnp.float32), jnp.zeros((RANK, HD), jnp.float32))
    (back_pad, up_total), tiles_out = lax.scan(visit, start, jnp.arange(N_ROW * N_COL, dtype=jnp.int32))
    attended = tiles_out.reshape(N_ROW, N_COL, TILE, TILE, HD).transpose(0, 2, 1, 3, 4).reshape(ROWS, COLS, HD)
    back = back_pad[TILE:TILE + ROWS, TILE:TILE + COLS].reshape(TOKENS, RANK)
    scale = TOKENS ** -0.5
    grad_down = lax.dot_general(flat_tokens.astype(jnp.float32), back, (((0,), (0,)), ((), ())), precision=lax.Precision.HIGHEST) * scale
    return attended, grad_down, up_total * scale
```

```python
import functools

import jax
import jax.numpy as jnp
import numpy as np
from jax import lax
from jax.experimental import pallas as pl
from jax.experimental.pallas import tpu as pltpu
from jax.sharding import PartitionSpec as P

MESH = pl.DeviceIdType.MESH
BF = jnp.bfloat16
F32 = jnp.float32
HALF = 768
MIB = 2**20


def place():
    row = lax.axis_index("row")
    col = lax.axis_index("col")
    return row, col


def grid_place():
    row, col = place()
    y = lax.div(row, 4)
    x = lax.rem(lax.div(row, 2), 2) * 2 + lax.div(col, 8)
    return y, x, lax.rem(col, 8), lax.rem(row, 2)


def at_grid(y, x, z, c):
    y = lax.rem(y + 4, 4)
    x = lax.rem(x + 4, 4)
    z = lax.rem(z + 8, 8)
    return (y * 4 + lax.div(x, 2) * 2 + c, lax.rem(x, 2) * 8 + z)


def at_chip(k, h, col):
    return (lax.rem(k + 8, 8) * 2 + h, lax.rem(col + 16, 16))


def greet(targets):
    barrier = pltpu.get_barrier_semaphore()
    for target in targets:
        pl.semaphore_signal(barrier, inc=1, device_id=target, device_id_type=MESH)
    pl.semaphore_wait(barrier, len(targets))


class Wire:
    def __init__(self, send, recv):
        self.send, self.recv, self.pending = send, recv, []

    def copy(self, src, dst, target, s, r):
        return pltpu.make_async_remote_copy(
            src_ref=src,
            dst_ref=dst,
            send_sem=self.send.at[s],
            recv_sem=self.recv.at[r],
            device_id=target,
            device_id_type=MESH,
        )

    def start(self, src, dst, target, s, r):
        copy = self.copy(src, dst, target, s, r)
        copy.start()
        self.pending.append(copy)

    def arrived(self, dst, r):
        row, col = place()
        self.copy(dst, dst, (row + 1 - 2 * lax.rem(row, 2), col), r, r).wait_recv()

    def drain(self):
        for copy in self.pending:
            copy.wait_send()
        self.pending = []


def chip_targets():
    row, col = place()
    k, c = lax.div(row, 2), lax.rem(row, 2)
    out = [at_chip(k, 1 - c, col)]
    for h in (0, 1):
        out += [at_chip(k + 1, h, col), at_chip(k - 1, h, col)]
        out += [at_chip(k, h, col + 1), at_chip(k, h, col - 1)]
    return out


def stretch(c):
    return pl.multiple_of(c * HALF, HALF)


def gather_kernel(
    q, kv, cot, x, low, wp, allow, q2, kwin, c2, lwin, x2, wout, allow2, zbuf, wblk, send, recv, local
):
    row, col = place()
    k, c = lax.div(row, 2), lax.rem(row, 2)
    y, xx, z, _ = grid_place()
    other = 1 - c
    mine = stretch(c)
    wire = Wire(send, recv)
    targets = chip_targets()
    for a in range(1, 8):
        targets += [at_grid(y, xx, z + a, 0), at_grid(y, xx, z + a, 1)]
    targets += [at_grid(y + 1, xx, z, c), at_grid(y - 1, xx, z, c)]
    targets += [at_grid(y, xx + 1, z, c), at_grid(y, xx - 1, z, c)]
    greet(targets)
    sib = at_chip(k, other, col)
    theirs = stretch(other)

    locals_ = []

    def local_copy(src, dst):
        copy = pltpu.make_async_copy(src, dst, local.at[len(locals_)])
        copy.start()
        locals_.append(copy)
        return copy

    slot = c * 8 + z
    own_w = local_copy(wp.at[:, pl.ds(mine, HALF)], zbuf.at[slot])
    wire.start(wp.at[:, pl.ds(theirs, HALF)], zbuf.at[slot], sib, 0, 0)
    for a in range(1, 8):
        for h in (0, 1):
            hh = c if h == 0 else other
            wire.start(
                wp.at[:, pl.ds(stretch(hh), HALF)],
                zbuf.at[slot],
                at_grid(y, xx, z + a, hh),
                2 * a + h,
                2 * a + h,
            )
    far = (3 - 3 * c) * 3 + 1
    up = 2 * c - 1
    for h in (0, 1):
        part = kv.at[:, pl.ds(h * HALF, HALF)]
        wire.start(part, kwin.at[far], at_chip(k + up, h, col), 16 + h, 16 + c)
        wire.start(low, lwin.at[far], at_chip(k + up, h, col), 18 + h, 18 + c)
    for h in (0, 1):
        part = kv.at[:, pl.ds(h * HALF, HALF)]
        for i, d in enumerate((1, -1)):
            wire.start(
                part, kwin.at[(1 + c) * 3 + 1 - d], at_chip(k, h, col + d), 20 + 2 * i + h, 20 + 2 * i + c
            )
            wire.start(
                low, lwin.at[(1 + c) * 3 + 1 - d], at_chip(k, h, col + d), 24 + 2 * i + h, 24 + 2 * i + c
            )
    centre = (1 + c) * 3 + 1
    wire.start(kv.at[:, pl.ds(theirs, HALF)], kwin.at[centre], sib, 28, 28)
    wire.start(low, lwin.at[centre], sib, 29, 29)
    wire.start(q.at[:, pl.ds(theirs, HALF)], q2.at[c], sib, 30, 30)
    wire.start(cot.at[:, pl.ds(theirs, HALF)], c2.at[c], sib, 31, 31)
    wire.start(x, x2.at[c], sib, 32, 32)
    wire.start(allow, allow2.at[c], sib, 33, 33)
    local_copy(kv.at[:, pl.ds(mine, HALF)], kwin.at[centre])
    local_copy(low, lwin.at[centre])
    local_copy(q.at[:, pl.ds(mine, HALF)], q2.at[c])
    local_copy(cot.at[:, pl.ds(mine, HALF)], c2.at[c])
    local_copy(x, x2.at[c])
    local_copy(allow, allow2.at[c])

    own_w.wait()
    wire.arrived(zbuf.at[0], 0)
    for a in range(1, 8):
        for h in (0, 1):
            wire.arrived(zbuf.at[0], 2 * a + h)
    r_out = lax.broadcasted_iota(jnp.int32, (96, 128), 0)
    r_in = lax.broadcasted_iota(jnp.int32, (96, 128), 1)
    pick = jnp.where(lax.div(r_out, 12) * 16 + lax.rem(r_out, 12) == r_in, 1.0, 0.0).astype(BF)
    for cc in (0, 1):
        part = zbuf[pl.ds(cc * 8, 8)].reshape(128, HALF)
        wblk[cc] = jnp.dot(pick, part, preferred_element_type=F32).astype(BF)

    xs = (at_grid(y, xx + 1, z, c), at_grid(y, xx - 1, z, c))
    ys = (at_grid(y + 1, xx, z, c), at_grid(y - 1, xx, z, c))

    def x_part(i):
        i = lax.rem(i + 4, 4)
        return lax.div(i, 2), lax.rem(i, 2)

    def y_part(i):
        return lax.rem(i + 4, 4)

    def small(yi, xi):
        a, b = x_part(xi)
        return wout.at[y_part(yi), a, :, b]

    def small_half(yi, xi, j):
        a, b = x_part(xi)
        return wout.at[y_part(yi), a, j, b]

    def strip(xi):
        a, b = x_part(xi)
        return wout.at[:, a, :, b]

    def strip_half(xi, j):
        a, b = x_part(xi)
        return wout.at[:, a, j, b]

    own_copy = pltpu.make_async_copy(wblk, small(y, xx), local.at[7])
    own_copy.start()

    def corners(wire):
        wire.arrived(kwin.at[1], 17)
        wire.arrived(lwin.at[1], 19)
        wire.arrived(kwin.at[10], 16)
        wire.arrived(lwin.at[10], 18)
        n = 44
        for rr in (0, 3):
            for d in (1, -1):
                dst = rr * 3 + 1 - d
                target = at_chip(k, c, col + d)
                wire.start(kwin.at[rr * 3 + 1], kwin.at[dst], target, n, n)
                wire.start(lwin.at[rr * 3 + 1], lwin.at[dst], target, n + 1, n + 1)
                n += 2

    def ring(wire, index, block, half, n, targets, src):
        nxt, prv = targets
        wire.start(src, block(index), nxt, n, n)
        wire.start(src, block(index), prv, n + 1, n + 1)

        def second():
            wire.arrived(block(index), n)
            wire.start(half(index - 1, 0), half(index - 1, 0), nxt, n + 2, n + 2)
            wire.arrived(block(index), n + 1)
            wire.start(half(index + 1, 1), half(index + 1, 1), prv, n + 3, n + 3)

        def last():
            wire.arrived(half(index, 0), n + 2)
            wire.arrived(half(index, 1), n + 3)

        return second, last

    def spread(along_x):
        sub = Wire(send, recv)
        x_small = (xx, lambda i: small(y, i), lambda i, j: small_half(y, i, j))
        y_small = (y, lambda i: small(i, xx), lambda i, j: small_half(i, xx, j))
        x_big = (xx, strip, strip_half)
        y_big = (y, lambda i: wout.at[y_part(i)], lambda i, j: wout.at[y_part(i), j])
        one, two = (x_small, y_big) if along_x else (y_small, x_big)
        first_to, second_to = (xs, ys) if along_x else (ys, xs)
        second, last = ring(sub, *one, 34, first_to, wblk)
        second()
        corners(sub)
        last()
        own_copy.wait()
        second, last = ring(sub, *two, 38, second_to, two[1](two[0]))
        second()
        last()
        sub.drain()

    @pl.when(c == 0)
    def _():
        spread(True)

    @pl.when(c == 1)
    def _():
        spread(False)

    for cc in (0, 1):
        for i in (0, 1):
            wire.arrived(kwin.at[0], 20 + 2 * i + cc)
            wire.arrived(lwin.at[0], 24 + 2 * i + cc)
    wire.arrived(kwin.at[0], 28)
    wire.arrived(lwin.at[0], 29)
    wire.arrived(q2.at[0], 30)
    wire.arrived(c2.at[0], 31)
    wire.arrived(x2.at[0], 32)
    wire.arrived(allow2.at[0], 33)
    for n in range(44, 52, 2):
        wire.arrived(kwin.at[0], n)
        wire.arrived(lwin.at[0], n + 1)
    for copy in locals_[1:]:
        copy.wait()
    wire.drain()


def any_spec(n):
    return [pl.BlockSpec(memory_space=pl.ANY)] * n


def gather(q, kv, cot, x, low, wp, allow):
    return pl.pallas_call(
        gather_kernel,
        out_shape=[
            jax.ShapeDtypeStruct((2, 256, HALF), BF),
            jax.ShapeDtypeStruct((12, 256, HALF), BF),
            jax.ShapeDtypeStruct((2, 256, HALF), BF),
            jax.ShapeDtypeStruct((12, 256, 128), BF),
            jax.ShapeDtypeStruct((2, 256, 3072), BF),
            jax.ShapeDtypeStruct((4, 2, 2, 2, 96, HALF), BF),
            jax.ShapeDtypeStruct((2,) + allow.shape, F32),
        ],
        in_specs=any_spec(7),
        out_specs=any_spec(7),
        scratch_shapes=[
            pltpu.VMEM((16, 16, HALF), BF),
            pltpu.VMEM((2, 96, HALF), BF),
            pltpu.SemaphoreType.DMA((52,)),
            pltpu.SemaphoreType.DMA((52,)),
            pltpu.SemaphoreType.DMA((8,)),
        ],
        compiler_params=pltpu.CompilerParams(collective_id=0, has_side_effects=True),
        name="gather",
    )(q, kv, cot, x, low, wp, allow)


def halo_kernel(v, vwin, send, recv, local):
    row, col = place()
    k, c = lax.div(row, 2), lax.rem(row, 2)
    wire = Wire(send, recv)
    up, down = at_chip(k - 1, c, col), at_chip(k + 1, c, col)
    sides = [at_chip(k, c, col + d) for d in (1, -1)]
    greet([up, down] + sides)
    wire.start(v.at[0], vwin.at[10], up, 0, 0)
    wire.start(v.at[1], vwin.at[1], down, 1, 1)
    for i, d in enumerate((1, -1)):
        for t in (0, 1):
            wire.start(v.at[t], vwin.at[(1 + t) * 3 + 1 - d], sides[i], 2 + 2 * i + t, 2 + 2 * i + t)
    copies = [pltpu.make_async_copy(v.at[t], vwin.at[4 + 3 * t], local.at[t]) for t in (0, 1)]
    for copy in copies:
        copy.start()
    n = 6
    for rr in (3, 0):
        wire.arrived(vwin.at[rr * 3 + 1], 0 if rr else 1)
        for i, d in enumerate((1, -1)):
            wire.start(vwin.at[rr * 3 + 1], vwin.at[rr * 3 + 1 - d], sides[i], n, n)
            n += 1
    for n in range(2, 10):
        wire.arrived(vwin.at[0], n)
    for copy in copies:
        copy.wait()
    wire.drain()


def halo(v):
    return pl.pallas_call(
        halo_kernel,
        out_shape=jax.ShapeDtypeStruct((12, 256, HALF), BF),
        in_specs=any_spec(1),
        out_specs=any_spec(1)[0],
        scratch_shapes=[
            pltpu.SemaphoreType.DMA((10,)),
            pltpu.SemaphoreType.DMA((10,)),
            pltpu.SemaphoreType.DMA((2,)),
        ],
        compiler_params=pltpu.CompilerParams(collective_id=1, has_side_effects=True),
        name="halo",
    )(v)


def attention_kernel(radius, q, kw, vw, cot, low, up, dist, allow, att, back, upt, s_ref, p_ref):
    h, t = pl.program_id(0), pl.program_id(1)
    keys = kw[pl.ds(t * 3, 9)].reshape(2304, 128)
    s_ref[...] = lax.dot_general(
        q[0], keys, (((1,), (1,)), ((), ())), preferred_element_type=F32
    )
    limit = allow[0, 0:1, :] * (radius[h] * radius[h] + 1.0) - 1.0
    scale = 128**-0.5

    @pl.loop(0, 8)
    def _(i):
        rows = pl.ds(pl.multiple_of(i * 32, 32), 32)
        s = jnp.where(dist[rows] <= limit, s_ref[rows] * scale, -1e30)
        e = jnp.exp(s - jnp.max(s, axis=1, keepdims=True))
        p_ref[rows] = (e * (1.0 / jnp.sum(e, axis=1, keepdims=True))).astype(BF)

    p = p_ref[...]
    vals = vw[pl.ds(t * 3, 9)].reshape(2304, 128)
    att[0] = jnp.dot(p, vals, preferred_element_type=F32).astype(BF)
    vgt = jnp.dot(cot[0].T, p, preferred_element_type=F32).astype(BF)

    @pl.when((h == 0) & (t == 0))
    def _():
        back[...] = jnp.zeros_like(back)

    bt = jnp.dot(up[...], vgt, preferred_element_type=F32)
    for n in range(9):
        back[t * 3 + n] += bt[:, n * 256 : (n + 1) * 256]
    lows = low[pl.ds(t * 3, 9)].reshape(2304, 128)
    ut = jnp.dot(vgt, lows, preferred_element_type=F32)

    @pl.when(t == 0)
    def _():
        upt[...] = ut

    @pl.when(t == 1)
    def _():
        upt[...] += ut


def distances():
    qp = np.arange(256)
    kp = np.arange(2304)
    kr = (kp // 768) * 16 + (kp % 256) // 16 - 16
    kc = (kp // 256 % 3) * 16 + kp % 16 - 16
    dr = kr[None] - (qp // 16)[:, None]
    dc = kc[None] - (qp % 16)[:, None]
    return (dr * dr + dc * dc).astype(np.float32)


def attention(radius, q2, kwin, vwin, c2, lwin, up, dist, allow2):
    return pl.pallas_call(
        attention_kernel,
        grid=(6, 2),
        out_shape=[
            jax.ShapeDtypeStruct((2, 256, HALF), BF),
            jax.ShapeDtypeStruct((12, 64, 256), F32),
            jax.ShapeDtypeStruct((HALF, 128), F32),
        ],
        in_specs=[
            pl.BlockSpec(memory_space=pltpu.SMEM),
            pl.BlockSpec((1, 256, 128), lambda h, t: (t, 0, h)),
            pl.BlockSpec((12, 256, 128), lambda h, t: (0, 0, h)),
            pl.BlockSpec((12, 256, 128), lambda h, t: (0, 0, h)),
            pl.BlockSpec((1, 256, 128), lambda h, t: (t, 0, h)),
            pl.BlockSpec((12, 256, 128), lambda h, t: (0, 0, 0)),
            pl.BlockSpec((64, 128), lambda h, t: (0, h)),
            pl.BlockSpec((256, 2304), lambda h, t: (0, 0)),
            pl.BlockSpec((1, 8, 2304), lambda h, t: (t, 0, 0)),
        ],
        out_specs=[
            pl.BlockSpec((1, 256, 128), lambda h, t: (t, 0, h)),
            pl.BlockSpec((12, 64, 256), lambda h, t: (0, 0, 0)),
            pl.BlockSpec((128, 128), lambda h, t: (h, 0)),
        ],
        scratch_shapes=[pltpu.VMEM((256, 2304), F32), pltpu.VMEM((256, 2304), BF)],
        compiler_params=pltpu.CompilerParams(vmem_limit_bytes=48 * MIB),
        name="attention",
    )(radius, q2, kwin, vwin, c2, lwin, up, dist, allow2)


def reduce_kernel(
    att_in, back, upt, x, att, gd, gu, bs, br, gs, gr, keep, xs_, xr, ys_, yr, zs, zr, send, recv, local
):
    row, col = place()
    k, c = lax.div(row, 2), lax.rem(row, 2)
    other = 1 - c
    y, xx, z, _ = grid_place()
    wire = Wire(send, recv)
    sib = at_chip(k, other, col)
    mine = stretch(c)
    xt = [at_grid(y, xx + a, z, c) for a in (1, 2, 3)]
    yt = [at_grid(y + a, xx, z, c) for a in (1, 2, 3)]
    zt = [at_grid(y, xx, z + a, c) for a in range(1, 8)]
    targets = [sib] + xt + yt + zt
    around = [(rr, cc) for rr in range(4) for cc in range(3)]
    for h in (0, 1):
        for d in (1, 0, -1):
            targets += [at_chip(k + 1, h, col + d), at_chip(k - 1, h, col + d)]
            if d:
                targets.append(at_chip(k, h, col + d))
    greet(targets)
    wire.start(att_in.at[other], att.at[:, pl.ds(mine, HALF)], sib, 0, 0)
    keep_att = pltpu.make_async_copy(att_in.at[c], att.at[:, pl.ds(mine, HALF)], local.at[0])
    keep_att.start()

    for n, (rr, cc) in enumerate(around):
        bs[n] = back[n].astype(BF)
    for n, (rr, cc) in enumerate(around):
        dk, h = ((-1, 1), (0, 0), (0, 1), (1, 0))[rr]
        adj = 0 if rr in (1, 2) else 1
        slot = adj * 6 + cc * 2
        if (rr, cc) in ((1, 1), (2, 1)):
            @pl.when(c != h)
            def _():
                copy = wire.copy(bs.at[n], br.at[slot + c], sib, 1, 2 + slot + c)
                copy.start()
                copy.wait_send()
        else:
            wire.start(
                bs.at[n], br.at[slot + c], at_chip(k + dk, h, col + cc - 1), 2 + n, 2 + slot + c
            )
    total = back[(1 + c) * 3 + 1]
    wire.arrived(br.at[0], 2 + 2 + other)
    total = total + br[2 + other].astype(F32)
    for slot in range(12):
        if slot not in (2, 3):
            wire.arrived(br.at[0], 2 + slot)
            total = total + br[slot].astype(F32)
    hi = total.astype(BF)
    lo = (total - hi.astype(F32)).astype(BF)
    both = jnp.concatenate([hi, lo], axis=0)

    @pl.loop(0, 8)
    def _(i):
        part = x[:, pl.ds(pl.multiple_of(i * 384, 384), 384)]
        g = jnp.dot(both, part, preferred_element_type=F32)
        g = (g[:64] + g[64:]).T
        yi, xhi = lax.div(i, 2), lax.rem(i, 2)
        for cc in (0, 1):
            for xl in (0, 1):
                rows = g[(cc * 2 + xl) * 96 : (cc * 2 + xl + 1) * 96]
                keep[cc, xhi * 2 + xl, yi] = rows
                gs[cc, xhi * 2 + xl, yi] = rows.astype(BF)

    wire.start(gs.at[other], gr, sib, 14, 14)
    wire.arrived(gr, 14)
    for a in range(4):
        for b in range(4):
            full = keep[c, a, b] + gr[a, b].astype(F32)
            keep[0, a, b] = full
            xs_[a, b, 0:96] = full.astype(BF)
            xs_[a, b, 96:144] = upt[a * 4 + b, :, 0:64].astype(BF)
    for i, a in enumerate((1, 2, 3)):
        wire.start(xs_.at[lax.rem(xx + a, 4)], xr.at[a - 1], xt[i], 15 + i, 15 + i)
    for i in range(3):
        wire.arrived(xr.at[0], 15 + i)
    for b in range(4):
        acc = keep[0, xx, b]
        ua = upt[xx * 4 + b, :, 0:64]
        for i in range(3):
            acc = acc + xr[i, b, 0:96].astype(F32)
            ua = ua + xr[i, b, 96:144].astype(F32)
        keep[1, 0, b] = acc
        keep[1, 1, b, 0:48] = ua
        ys_[b, 0:96] = acc.astype(BF)
        ys_[b, 96:144] = ua.astype(BF)
    for i, a in enumerate((1, 2, 3)):
        wire.start(ys_.at[lax.rem(y + a, 4)], yr.at[a - 1], yt[i], 18 + i, 18 + i)
    for i in range(3):
        wire.arrived(yr.at[0], 18 + i)
    acc = keep[1, 0, y]
    ua = keep[1, 1, y, 0:48]
    for i in range(3):
        acc = acc + yr[i, 0:96].astype(F32)
        ua = ua + yr[i, 96:144].astype(F32)
    zs[0:96] = acc.astype(BF)
    zs[96:144] = ua.astype(BF)
    for i in range(7):
        wire.start(zs, zr.at[z], zt[i], 21 + i, 21 + i)
    zr[z] = zs[...]
    for i in range(7):
        wire.arrived(zr.at[0], 21 + i)
    scale = 65536**-0.5
    acc = zr[0].astype(F32)
    for i in range(1, 8):
        acc = acc + zr[i].astype(F32)
    acc = acc * scale
    r_out = lax.broadcasted_iota(jnp.int32, (16, 96), 0)
    r_in = lax.broadcasted_iota(jnp.int32, (16, 96), 1)
    pick = jnp.where(z * 12 + r_out == r_in, 1.0, 0.0).astype(F32)
    gd[...] = jnp.dot(
        pick, acc[0:96], preferred_element_type=F32, precision=lax.Precision.HIGHEST
    )
    gu[c, xx, y] = acc[96:144]
    spot = gu.at[c, xx, y]
    for i in range(3):
        wire.start(spot, spot, yt[i], 28 + i, 28 + i)
    for i in range(3):
        wire.arrived(spot, 28 + i)
    for i in range(3):
        wire.start(gu.at[c, xx], gu.at[c, xx], xt[i], 31 + i, 31 + i)
    for i in range(3):
        wire.arrived(gu.at[c, xx], 31 + i)
    wire.start(gu.at[c], gu.at[c], sib, 34, 34)
    wire.arrived(gu.at[c], 34)
    wire.arrived(att.at[:, pl.ds(mine, HALF)], 0)
    keep_att.wait()
    wire.drain()


def reduce(att2, back, upt, x):
    vm = pl.BlockSpec(memory_space=pltpu.VMEM)
    hb = pl.BlockSpec(memory_space=pl.ANY)
    return pl.pallas_call(
        reduce_kernel,
        out_shape=[
            jax.ShapeDtypeStruct((256, 1536), BF),
            jax.ShapeDtypeStruct((16, 64), F32),
            jax.ShapeDtypeStruct((2, 4, 4, 48, 64), F32),
        ],
        in_specs=[hb, vm, vm, vm],
        out_specs=[hb, vm, vm],
        scratch_shapes=[
            pltpu.VMEM((12, 64, 256), BF),
            pltpu.VMEM((12, 64, 256), BF),
            pltpu.VMEM((2, 4, 4, 96, 64), BF),
            pltpu.VMEM((4, 4, 96, 64), BF),
            pltpu.VMEM((2, 4, 4, 96, 64), F32),
            pltpu.VMEM((4, 4, 144, 64), BF),
            pltpu.VMEM((3, 4, 144, 64), BF),
            pltpu.VMEM((4, 144, 64), BF),
            pltpu.VMEM((3, 144, 64), BF),
            pltpu.VMEM((144, 64), BF),
            pltpu.VMEM((8, 144, 64), BF),
            pltpu.SemaphoreType.DMA((35,)),
            pltpu.SemaphoreType.DMA((35,)),
            pltpu.SemaphoreType.DMA((1,)),
        ],
        compiler_params=pltpu.CompilerParams(
            collective_id=2, has_side_effects=True, vmem_limit_bytes=48 * MIB
        ),
        name="reduce",
    )(att2, back, upt, x)


def allowed_row(tile_mask):
    row, col = place()
    r = row + jnp.arange(3, dtype=jnp.int32) - 1
    s = col + jnp.arange(3, dtype=jnp.int32) - 1
    rows = lax.axis_size("row")
    cols = lax.axis_size("col")
    inside = ((r >= 0) & (r < rows))[:, None] & ((s >= 0) & (s < cols))[None, :]
    flags = jnp.where(inside.reshape(9) & (tile_mask.reshape(9) > 0), 1.0, 0.0).astype(F32)
    return jnp.broadcast_to(jnp.repeat(flags, 256)[None], (8, 2304))


def per_device(
    patch_tokens,
    queries,
    key_vectors,
    cotangent,
    value_weight,
    adapter_down,
    adapter_up,
    radius,
    tile_mask,
):
    core = lax.rem(lax.axis_index("row"), 2)
    x = patch_tokens.reshape(256, 3072)
    down = jnp.pad(adapter_down, ((0, 0), (0, 64)))
    low = jnp.dot(x, down, preferred_element_type=F32).astype(BF)
    wp = jnp.pad(value_weight, ((0, 4), (0, 0)))
    q2, kwin, c2, lwin, x2, w, allow2 = gather(
        queries.reshape(256, 1536),
        key_vectors.reshape(256, 1536),
        cotangent.reshape(256, 1536),
        x,
        low,
        wp,
        allowed_row(tile_mask),
    )
    up = lax.dynamic_slice_in_dim(adapter_up, core * HALF, HALF, 1)
    low2 = jnp.concatenate([lwin[4], lwin[7]], axis=0)[:, :64]
    values = (
        jnp.dot(x2.reshape(512, 3072), w.reshape(3072, HALF), preferred_element_type=F32)
        + jnp.dot(low2, up, preferred_element_type=F32)
    ).astype(BF)
    vwin = halo(values.reshape(2, 256, HALF))
    reach = lax.dynamic_slice_in_dim(radius, core * 6, 6, 0).astype(F32)
    att2, back, upt = attention(
        reach, q2, kwin, vwin, c2, lwin, up, jnp.asarray(distances()), allow2
    )
    att, gd, gu = reduce(att2, back, upt.reshape(16, 48, 128), x)
    return att.reshape(16, 16, 1536), gd[:12], gu.reshape(1536, 64).T


def solution(mesh):
    placed = (
        P("row", "col", None),
        P("row", "col", None),
        P("row", "col", None),
        P("row", "col", None),
        P(("row", "col"), None),
        P(),
        P(),
        P(),
        P("row", "col", None),
    )
    return jax.shard_map(
        per_device,
        mesh=mesh,
        in_specs=placed,
        out_specs=(P("row", "col", None), P(("row", "col"), None), P()),
        check_vma=False,
    )
```

```python
import jax
import jax.numpy as jnp
import numpy as np
from jax import lax
from jax.experimental import pallas as pl
from jax.experimental.pallas import tpu as pltpu
from jax.sharding import PartitionSpec as P

MESH = pl.DeviceIdType.MESH
BF = jnp.bfloat16
F32 = jnp.float32
HALF = 768
MIB = 2**20


def place():
    row = lax.axis_index("row")
    col = lax.axis_index("col")
    return row, col


def grid_place():
    row, col = place()
    y = lax.div(row, 4)
    x = lax.rem(lax.div(row, 2), 2) * 2 + lax.div(col, 8)
    return y, x, lax.rem(col, 8), lax.rem(row, 2)


def at_grid(y, x, z, c):
    y = lax.rem(y + 4, 4)
    x = lax.rem(x + 4, 4)
    z = lax.rem(z + 8, 8)
    return (y * 4 + lax.div(x, 2) * 2 + c, lax.rem(x, 2) * 8 + z)


def at_chip(k, h, col):
    return (lax.rem(k + 8, 8) * 2 + h, lax.rem(col + 16, 16))


def greet(targets):
    barrier = pltpu.get_barrier_semaphore()
    for target in targets:
        pl.semaphore_signal(barrier, inc=1, device_id=target, device_id_type=MESH)
    pl.semaphore_wait(barrier, len(targets))


class Wire:
    def __init__(self, send, recv):
        self.send, self.recv, self.pending = send, recv, []

    def copy(self, src, dst, target, s, r):
        return pltpu.make_async_remote_copy(
            src_ref=src,
            dst_ref=dst,
            send_sem=self.send.at[s],
            recv_sem=self.recv.at[r],
            device_id=target,
            device_id_type=MESH,
        )

    def start(self, src, dst, target, s, r):
        copy = self.copy(src, dst, target, s, r)
        copy.start()
        self.pending.append(copy)

    def arrived(self, dst, r):
        row, col = place()
        self.copy(dst, dst, (row + 1 - 2 * lax.rem(row, 2), col), r, r).wait_recv()

    def drain(self):
        for copy in self.pending:
            copy.wait_send()
        self.pending = []


def chip_targets():
    row, col = place()
    k, c = lax.div(row, 2), lax.rem(row, 2)
    out = [at_chip(k, 1 - c, col)]
    for h in (0, 1):
        out += [at_chip(k + 1, h, col), at_chip(k - 1, h, col)]
        out += [at_chip(k, h, col + 1), at_chip(k, h, col - 1)]
    return out


def stretch(c):
    return pl.multiple_of(c * HALF, HALF)


def kernel(
    radius, q, kv, cot, x, wp, allow, down, up, dist,
    att, gd, gu,
    q2, kwin, c2, lwin, x2, wout, allow2, zbuf, wblk, low,
    vwin, s_ref, p_ref, back, upt, att2,
    bs, br, gs, gr, keep, xs_, xr, ys_, yr, zs, zr,
    send, recv, local,
):
    row, col = place()
    k, c = lax.div(row, 2), lax.rem(row, 2)
    y, xx, z, _ = grid_place()
    other = 1 - c
    mine = stretch(c)
    wire = Wire(send, recv)
    targets = chip_targets()
    for a in range(1, 8):
        targets += [at_grid(y, xx, z + a, 0), at_grid(y, xx, z + a, 1)]
    xt = [at_grid(y, xx + a, z, c) for a in (1, 2, 3)]
    yt = [at_grid(y + a, xx, z, c) for a in (1, 2, 3)]
    zt = [at_grid(y, xx, z + a, c) for a in range(1, 8)]
    targets += xt + yt
    for h in (0, 1):
        for d in (1, -1):
            targets += [at_chip(k + 1, h, col + d), at_chip(k - 1, h, col + d)]
    sib = at_chip(k, other, col)
    theirs = stretch(other)

    locals_ = []

    def local_copy(src, dst):
        copy = pltpu.make_async_copy(src, dst, local.at[len(locals_)])
        copy.start()
        locals_.append(copy)
        return copy

    slot = c * 8 + z
    centre = (1 + c) * 3 + 1
    own_x = local_copy(x, x2.at[c])
    own_w = local_copy(wp.at[:, pl.ds(mine, HALF)], zbuf.at[slot])
    local_copy(kv.at[:, pl.ds(mine, HALF)], kwin.at[centre])
    local_copy(q.at[:, pl.ds(mine, HALF)], q2.at[c])
    local_copy(cot.at[:, pl.ds(mine, HALF)], c2.at[c])
    local_copy(allow, allow2.at[c])
    greet(targets)

    wire.start(wp.at[:, pl.ds(theirs, HALF)], zbuf.at[slot], sib, 0, 0)
    for a in range(1, 8):
        for h in (0, 1):
            hh = c if h == 0 else other
            wire.start(
                wp.at[:, pl.ds(stretch(hh), HALF)],
                zbuf.at[slot],
                at_grid(y, xx, z + a, hh),
                2 * a + h,
                2 * a + h,
            )
    far = (3 - 3 * c) * 3 + 1
    step = 2 * c - 1

    def spread_tile(src, win, n, split):
        part = lambda h: src.at[:, pl.ds(h * HALF, HALF)] if split else src
        for h in (0, 1):
            wire.start(part(h), win.at[far], at_chip(k + step, h, col), n + h, n + c)
        for h in (0, 1):
            for i, d in enumerate((1, -1)):
                m = n + 2 + 2 * i
                spot = win.at[(1 + c) * 3 + 1 - d]
                wire.start(part(h), spot, at_chip(k, h, col + d), m + h, m + c)
        full = src.at[:, pl.ds(theirs, HALF)] if split else src
        wire.start(full, win.at[centre], sib, n + 6, n + 6)

    spread_tile(kv, kwin, 16, True)
    wire.start(q.at[:, pl.ds(theirs, HALF)], q2.at[c], sib, 30, 30)
    wire.start(cot.at[:, pl.ds(theirs, HALF)], c2.at[c], sib, 31, 31)
    wire.start(x, x2.at[c], sib, 32, 32)
    wire.start(allow, allow2.at[c], sib, 33, 33)
    own_x.wait()
    low[...] = jnp.dot(x2[c], down[...], preferred_element_type=F32).astype(BF)
    lwin[centre] = low[...]
    spread_tile(low, lwin, 23, False)

    own_w.wait()
    wire.arrived(zbuf.at[0], 0)
    for a in range(1, 8):
        for h in (0, 1):
            wire.arrived(zbuf.at[0], 2 * a + h)
    r_out = lax.broadcasted_iota(jnp.int32, (96, 128), 0)
    r_in = lax.broadcasted_iota(jnp.int32, (96, 128), 1)
    pick = jnp.where(lax.div(r_out, 12) * 16 + lax.rem(r_out, 12) == r_in, 1.0, 0.0).astype(BF)
    for cc in (0, 1):
        part = zbuf[pl.ds(cc * 8, 8)].reshape(128, HALF)
        wblk[cc] = jnp.dot(pick, part, preferred_element_type=F32).astype(BF)

    xs = (at_grid(y, xx + 1, z, c), at_grid(y, xx - 1, z, c))
    ys = (at_grid(y + 1, xx, z, c), at_grid(y - 1, xx, z, c))

    def x_part(i):
        i = lax.rem(i + 4, 4)
        return lax.div(i, 2), lax.rem(i, 2)

    def y_part(i):
        return lax.rem(i + 4, 4)

    def small(yi, xi):
        a, b = x_part(xi)
        return wout.at[y_part(yi), a, :, b]

    def small_half(yi, xi, j):
        a, b = x_part(xi)
        return wout.at[y_part(yi), a, j, b]

    def strip(xi):
        a, b = x_part(xi)
        return wout.at[:, a, :, b]

    def strip_half(xi, j):
        a, b = x_part(xi)
        return wout.at[:, a, j, b]

    own_copy = pltpu.make_async_copy(wblk, small(y, xx), local.at[7])
    own_copy.start()

    def corners(wire, win, n, m):
        for rr, first in ((0, n + 1), (3, n)):
            wire.arrived(win.at[rr * 3 + 1], first)
            for d in (1, -1):
                spot = win.at[rr * 3 + 1 - d]
                wire.start(win.at[rr * 3 + 1], spot, at_chip(k, c, col + d), m, m)
                m += 1

    def ring(wire, index, block, half, n, targets, src):
        nxt, prv = targets
        wire.start(src, block(index), nxt, n, n)
        wire.start(src, block(index), prv, n + 1, n + 1)

        def second():
            wire.arrived(block(index), n)
            wire.start(half(index - 1, 0), half(index - 1, 0), nxt, n + 2, n + 2)
            wire.arrived(block(index), n + 1)
            wire.start(half(index + 1, 1), half(index + 1, 1), prv, n + 3, n + 3)

        def last():
            wire.arrived(half(index, 0), n + 2)
            wire.arrived(half(index, 1), n + 3)

        return second, last

    def spread(along_x):
        sub = Wire(send, recv)
        x_small = (xx, lambda i: small(y, i), lambda i, j: small_half(y, i, j))
        y_small = (y, lambda i: small(i, xx), lambda i, j: small_half(i, xx, j))
        x_big = (xx, strip, strip_half)
        y_big = (y, lambda i: wout.at[y_part(i)], lambda i, j: wout.at[y_part(i), j])
        one, two = (x_small, y_big) if along_x else (y_small, x_big)
        first_to, second_to = (xs, ys) if along_x else (ys, xs)
        second, last = ring(sub, *one, 34, first_to, wblk)
        second()
        corners(sub, kwin, 16, 42)
        corners(sub, lwin, 23, 46)
        last()
        own_copy.wait()
        second, last = ring(sub, *two, 38, second_to, two[1](two[0]))
        second()
        last()
        sub.drain()

    @pl.when(c == 0)
    def _():
        spread(True)

    @pl.when(c == 1)
    def _():
        spread(False)

    wire.arrived(x2.at[0], 32)
    wire.arrived(lwin.at[0], 29)
    low2 = jnp.concatenate([lwin[4][:, :64], lwin[7][:, :64]], axis=0)

    @pl.loop(0, 3)
    def _(n):
        lanes = pl.ds(pl.multiple_of(n * 256, 256), 256)
        acc = jnp.dot(low2, up[:, lanes], preferred_element_type=F32)
        for yi in range(4):
            rows = wout[yi, :, :, :, :, lanes].reshape(768, 256)
            part = x2[:, :, yi * 768 : (yi + 1) * 768].reshape(512, 768)
            acc = acc + jnp.dot(part, rows, preferred_element_type=F32)
        acc = acc.astype(BF)
        vwin[4, :, lanes] = acc[:256]
        vwin[7, :, lanes] = acc[256:]

    v0 = 50
    sides = [at_chip(k, c, col + d) for d in (1, -1)]
    wire.start(vwin.at[4], vwin.at[10], at_chip(k - 1, c, col), v0, v0)
    wire.start(vwin.at[7], vwin.at[1], at_chip(k + 1, c, col), v0 + 1, v0 + 1)
    for i, d in enumerate((1, -1)):
        for t in (0, 1):
            m = v0 + 2 + 2 * i + t
            wire.start(vwin.at[4 + 3 * t], vwin.at[(1 + t) * 3 + 1 - d], sides[i], m, m)

    for cc in (0, 1):
        for i in (0, 1):
            wire.arrived(kwin.at[0], 18 + 2 * i + cc)
            wire.arrived(lwin.at[0], 25 + 2 * i + cc)
    wire.arrived(kwin.at[0], 22)
    wire.arrived(q2.at[0], 30)
    wire.arrived(c2.at[0], 31)
    wire.arrived(allow2.at[0], 33)
    for n in range(4):
        wire.arrived(kwin.at[0], 42 + n)
        wire.arrived(lwin.at[0], 46 + n)
    for copy in locals_[2:]:
        copy.wait()

    back[...] = jnp.zeros_like(back)
    upt[...] = jnp.zeros_like(upt)

    def probs(lo, hi):
        @pl.loop(lo, hi)
        def _(i):
            h, t = lax.div(i, 2), lax.rem(i, 2)
            lanes = pl.ds(pl.multiple_of(h * 128, 128), 128)
            keys = kwin[pl.ds(t * 3, 9), :, lanes].reshape(2304, 128)
            s_ref[...] = lax.dot_general(
                q2[t, :, lanes], keys, (((1,), (1,)), ((), ())), preferred_element_type=F32
            )
            limit = allow2[t, 0:1, :] * (radius[h] * radius[h] + 1.0) - 1.0

            @pl.loop(0, 8)
            def _(j):
                rows = pl.ds(pl.multiple_of(j * 32, 32), 32)
                s = jnp.where(dist[rows] <= limit, s_ref[rows] * 128**-0.5, -1e30)
                e = jnp.exp(s - jnp.max(s, axis=1, keepdims=True))
                p_ref[i, rows] = (e * (1.0 / jnp.sum(e, axis=1, keepdims=True))).astype(BF)

            vgt = jnp.dot(c2[t, :, lanes].T, p_ref[i], preferred_element_type=F32).astype(BF)
            bt = jnp.dot(up[:, lanes], vgt, preferred_element_type=F32)
            for n in range(9):
                back[t * 3 + n] += bt[:, n * 256 : (n + 1) * 256]
            lows = lwin[pl.ds(t * 3, 9)].reshape(2304, 128)
            rows = pl.ds(pl.multiple_of(h * 128, 128), 128)
            upt[rows] += jnp.dot(vgt, lows, preferred_element_type=F32)

    def attend(lo, hi):
        @pl.loop(lo, hi)
        def _(i):
            h, t = lax.div(i, 2), lax.rem(i, 2)
            lanes = pl.ds(pl.multiple_of(h * 128, 128), 128)
            vals = vwin[pl.ds(t * 3, 9), :, lanes].reshape(2304, 128)
            att2[t, :, lanes] = jnp.dot(p_ref[i], vals, preferred_element_type=F32).astype(BF)

    probs(0, 6)
    n = v0 + 6
    for rr in (3, 0):
        wire.arrived(vwin.at[rr * 3 + 1], v0 if rr else v0 + 1)
        for i, d in enumerate((1, -1)):
            wire.start(vwin.at[rr * 3 + 1], vwin.at[rr * 3 + 1 - d], sides[i], n, n)
            n += 1
    probs(6, 12)

    def values_here():
        for n in range(2, 10):
            wire.arrived(vwin.at[0], v0 + n)

    r0 = 60
    around = [(rr, cc) for rr in range(4) for cc in range(3)]
    for n, (rr, cc) in enumerate(around):
        bs[n] = back[n].astype(BF)
    for n, (rr, cc) in enumerate(around):
        dk, h = ((-1, 1), (0, 0), (0, 1), (1, 0))[rr]
        adj = 0 if rr in (1, 2) else 1
        slot = adj * 6 + cc * 2
        if (rr, cc) in ((1, 1), (2, 1)):
            @pl.when(c != h)
            def _():
                copy = wire.copy(bs.at[n], br.at[slot + c], sib, r0 + 1, r0 + 2 + slot + c)
                copy.start()
                copy.wait_send()
        else:
            wire.start(
                bs.at[n], br.at[slot + c], at_chip(k + dk, h, col + cc - 1), r0 + 2 + n, r0 + 2 + slot + c
            )
    total = back[(1 + c) * 3 + 1]
    wire.arrived(br.at[0], r0 + 4 + other)
    total = total + br[2 + other].astype(F32)
    for slot in range(12):
        if slot not in (2, 3):
            wire.arrived(br.at[0], r0 + 2 + slot)
            total = total + br[slot].astype(F32)
    hi = total.astype(BF)
    lo = (total - hi.astype(F32)).astype(BF)
    both = jnp.concatenate([hi, lo], axis=0)

    @pl.loop(0, 8)
    def _(i):
        part = x2[c, :, pl.ds(pl.multiple_of(i * 384, 384), 384)]
        g = jnp.dot(both, part, preferred_element_type=F32)
        g = (g[:64] + g[64:]).T
        yi, xhi = lax.div(i, 2), lax.rem(i, 2)
        for cc in (0, 1):
            for xl in (0, 1):
                rows = g[(cc * 2 + xl) * 96 : (cc * 2 + xl + 1) * 96]
                keep[cc, xhi * 2 + xl, yi] = rows
                gs[cc, xhi * 2 + xl, yi] = rows.astype(BF)

    wire.start(gs.at[other], gr, sib, r0 + 14, r0 + 14)
    wire.arrived(gr, r0 + 14)
    for a in range(4):
        for b in range(4):
            full = keep[c, a, b] + gr[a, b].astype(F32)
            keep[0, a, b] = full
            xs_[a, b, 0:96] = full.astype(BF)
            xs_[a, b, 96:144] = upt[(a * 4 + b) * 48 : (a * 4 + b + 1) * 48, 0:64].astype(BF)
    for i, a in enumerate((1, 2, 3)):
        wire.start(xs_.at[lax.rem(xx + a, 4)], xr.at[a - 1], xt[i], r0 + 15 + i, r0 + 15 + i)
    for i in range(3):
        wire.arrived(xr.at[0], r0 + 15 + i)
    for b in range(4):
        acc = keep[0, xx, b]
        ua = upt[pl.ds(pl.multiple_of((xx * 4 + b) * 48, 16), 48), 0:64]
        for i in range(3):
            acc = acc + xr[i, b, 0:96].astype(F32)
            ua = ua + xr[i, b, 96:144].astype(F32)
        keep[1, 0, b] = acc
        keep[1, 1, b, 0:48] = ua
        ys_[b, 0:96] = acc.astype(BF)
        ys_[b, 96:144] = ua.astype(BF)
    for i, a in enumerate((1, 2, 3)):
        wire.start(ys_.at[lax.rem(y + a, 4)], yr.at[a - 1], yt[i], r0 + 18 + i, r0 + 18 + i)
    for i in range(3):
        wire.arrived(yr.at[0], r0 + 18 + i)
    acc = keep[1, 0, y]
    ua = keep[1, 1, y, 0:48]
    for i in range(3):
        acc = acc + yr[i, 0:96].astype(F32)
        ua = ua + yr[i, 96:144].astype(F32)
    zs[0:96] = acc.astype(BF)
    zs[96:144] = ua.astype(BF)
    for i in range(7):
        wire.start(zs, zr.at[z], zt[i], r0 + 21 + i, r0 + 21 + i)
    zr[z] = zs[...]
    for i in range(7):
        wire.arrived(zr.at[0], r0 + 21 + i)
    scale = 65536**-0.5
    acc = zr[0].astype(F32)
    for i in range(1, 8):
        acc = acc + zr[i].astype(F32)
    acc = acc * scale
    r_out = lax.broadcasted_iota(jnp.int32, (16, 96), 0)
    r_in = lax.broadcasted_iota(jnp.int32, (16, 96), 1)
    pick = jnp.where(z * 12 + r_out == r_in, 1.0, 0.0).astype(F32)
    gd[...] = jnp.dot(
        pick, acc[0:96], preferred_element_type=F32, precision=lax.Precision.HIGHEST
    )
    gu[c, xx, y] = acc[96:144]
    spot = gu.at[c, xx, y]
    for i in range(3):
        wire.start(spot, spot, yt[i], r0 + 28 + i, r0 + 28 + i)
    for i in range(3):
        wire.arrived(spot, r0 + 28 + i)
    for i in range(3):
        wire.start(gu.at[c, xx], gu.at[c, xx], xt[i], r0 + 31 + i, r0 + 31 + i)
    for i in range(3):
        wire.arrived(gu.at[c, xx], r0 + 31 + i)
    wire.start(gu.at[c], gu.at[c], sib, r0 + 34, r0 + 34)
    wire.arrived(gu.at[c], r0 + 34)
    values_here()
    attend(0, 12)
    wire.start(att2.at[other], att.at[:, pl.ds(mine, HALF)], sib, r0, r0)
    keep_att = pltpu.make_async_copy(att2.at[c], att.at[:, pl.ds(mine, HALF)], local.at[6])
    keep_att.start()
    wire.arrived(att.at[:, pl.ds(mine, HALF)], r0)
    keep_att.wait()
    wire.drain()


def distances():
    qp = np.arange(256)
    kp = np.arange(2304)
    kr = (kp // 768) * 16 + (kp % 256) // 16 - 16
    kc = (kp // 256 % 3) * 16 + kp % 16 - 16
    dr = kr[None] - (qp // 16)[:, None]
    dc = kc[None] - (qp % 16)[:, None]
    return (dr * dr + dc * dc).astype(np.float32)


def fused(*args):
    vm = pl.BlockSpec(memory_space=pltpu.VMEM)
    hb = pl.BlockSpec(memory_space=pl.ANY)
    return pl.pallas_call(
        kernel,
        out_shape=[
            jax.ShapeDtypeStruct((256, 1536), BF),
            jax.ShapeDtypeStruct((16, 64), F32),
            jax.ShapeDtypeStruct((2, 4, 4, 48, 64), F32),
        ],
        in_specs=[pl.BlockSpec(memory_space=pltpu.SMEM), hb, hb, hb, hb, hb, hb, vm, vm, vm],
        out_specs=[hb, vm, vm],
        scratch_shapes=[
            pltpu.VMEM((2, 256, HALF), BF),
            pltpu.VMEM((12, 256, HALF), BF),
            pltpu.VMEM((2, 256, HALF), BF),
            pltpu.VMEM((12, 256, 128), BF),
            pltpu.VMEM((2, 256, 3072), BF),
            pltpu.VMEM((4, 2, 2, 2, 96, HALF), BF),
            pltpu.VMEM((2, 8, 2304), F32),
            pltpu.VMEM((16, 16, HALF), BF),
            pltpu.VMEM((2, 96, HALF), BF),
            pltpu.VMEM((256, 128), BF),
            pltpu.VMEM((12, 256, HALF), BF),
            pltpu.VMEM((256, 2304), F32),
            pltpu.VMEM((12, 256, 2304), BF),
            pltpu.VMEM((12, 64, 256), F32),
            pltpu.VMEM((HALF, 128), F32),
            pltpu.VMEM((2, 256, HALF), BF),
            pltpu.VMEM((12, 64, 256), BF),
            pltpu.VMEM((12, 64, 256), BF),
            pltpu.VMEM((2, 4, 4, 96, 64), BF),
            pltpu.VMEM((4, 4, 96, 64), BF),
            pltpu.VMEM((2, 4, 4, 96, 64), F32),
            pltpu.VMEM((4, 4, 144, 64), BF),
            pltpu.VMEM((3, 4, 144, 64), BF),
            pltpu.VMEM((4, 144, 64), BF),
            pltpu.VMEM((3, 144, 64), BF),
            pltpu.VMEM((144, 64), BF),
            pltpu.VMEM((8, 144, 64), BF),
            pltpu.SemaphoreType.DMA((96,)),
            pltpu.SemaphoreType.DMA((96,)),
            pltpu.SemaphoreType.DMA((8,)),
        ],
        compiler_params=pltpu.CompilerParams(
            collective_id=0, has_side_effects=True, vmem_limit_bytes=60 * MIB
        ),
        name="fused",
    )(*args)


def allowed_row(tile_mask):
    row, col = place()
    r = row + jnp.arange(3, dtype=jnp.int32) - 1
    s = col + jnp.arange(3, dtype=jnp.int32) - 1
    rows = lax.axis_size("row")
    cols = lax.axis_size("col")
    inside = ((r >= 0) & (r < rows))[:, None] & ((s >= 0) & (s < cols))[None, :]
    flags = jnp.where(inside.reshape(9) & (tile_mask.reshape(9) > 0), 1.0, 0.0).astype(F32)
    return jnp.broadcast_to(jnp.repeat(flags, 256)[None], (8, 2304))


def per_device(
    patch_tokens,
    queries,
    key_vectors,
    cotangent,
    value_weight,
    adapter_down,
    adapter_up,
    radius,
    tile_mask,
):
    core = lax.rem(lax.axis_index("row"), 2)
    att, gd, gu = fused(
        lax.dynamic_slice_in_dim(radius, core * 6, 6, 0).astype(F32),
        queries.reshape(256, 1536),
        key_vectors.reshape(256, 1536),
        cotangent.reshape(256, 1536),
        patch_tokens.reshape(256, 3072),
        jnp.pad(value_weight, ((0, 4), (0, 0))),
        allowed_row(tile_mask),
        jnp.pad(adapter_down, ((0, 0), (0, 64))),
        lax.dynamic_slice_in_dim(adapter_up, core * HALF, HALF, 1),
        jnp.asarray(distances()),
    )
    return att.reshape(16, 16, 1536), gd[:12], gu.reshape(1536, 64).T


def solution(mesh):
    placed = (
        P("row", "col", None),
        P("row", "col", None),
        P("row", "col", None),
        P("row", "col", None),
        P(("row", "col"), None),
        P(),
        P(),
        P(),
        P("row", "col", None),
    )
    return jax.shard_map(
        per_device,
        mesh=mesh,
        in_specs=placed,
        out_specs=(P("row", "col", None), P(("row", "col"), None), P()),
        check_vma=False,
    )
```

```python
import jax
import jax.numpy as jnp
import numpy as np
from jax import lax
from jax.experimental import pallas as pl
from jax.experimental.pallas import tpu as pltpu
from jax.sharding import PartitionSpec as P

MESH = pl.DeviceIdType.MESH
BF = jnp.bfloat16
F32 = jnp.float32
HALF = 768
MIB = 2**20


def place():
    row = lax.axis_index("row")
    col = lax.axis_index("col")
    return row, col


def grid_place():
    row, col = place()
    y = lax.div(row, 4)
    x = lax.rem(lax.div(row, 2), 2) * 2 + lax.div(col, 8)
    return y, x, lax.rem(col, 8), lax.rem(row, 2)


def at_grid(y, x, z, c):
    y = lax.rem(y + 4, 4)
    x = lax.rem(x + 4, 4)
    z = lax.rem(z + 8, 8)
    return (y * 4 + lax.div(x, 2) * 2 + c, lax.rem(x, 2) * 8 + z)


def at_chip(k, h, col):
    return (lax.rem(k + 8, 8) * 2 + h, lax.rem(col + 16, 16))


def greet(targets):
    barrier = pltpu.get_barrier_semaphore()
    for target in targets:
        pl.semaphore_signal(barrier, inc=1, device_id=target, device_id_type=MESH)
    pl.semaphore_wait(barrier, len(targets))


class Wire:
    def __init__(self, send, recv):
        self.send, self.recv, self.pending = send, recv, []

    def copy(self, src, dst, target, s, r):
        return pltpu.make_async_remote_copy(
            src_ref=src,
            dst_ref=dst,
            send_sem=self.send.at[s],
            recv_sem=self.recv.at[r],
            device_id=target,
            device_id_type=MESH,
        )

    def start(self, src, dst, target, s, r):
        copy = self.copy(src, dst, target, s, r)
        copy.start()
        self.pending.append(copy)

    def arrived(self, dst, r):
        row, col = place()
        self.copy(dst, dst, (row + 1 - 2 * lax.rem(row, 2), col), r, r).wait_recv()

    def drain(self):
        for copy in self.pending:
            copy.wait_send()
        self.pending = []


def chip_targets():
    row, col = place()
    k, c = lax.div(row, 2), lax.rem(row, 2)
    out = [at_chip(k, 1 - c, col)]
    for h in (0, 1):
        out += [at_chip(k + 1, h, col), at_chip(k - 1, h, col)]
        out += [at_chip(k, h, col + 1), at_chip(k, h, col - 1)]
    return out


def stretch(c):
    return pl.multiple_of(c * HALF, HALF)


def kernel(
    radius, q, kv, cot, x, wp, allow, down, up, dist,
    att, gd, gu,
    q2, kwin, c2, lwin, x2, wout, allow2, zbuf, wblk, low,
    vwin, s_ref, p_ref, back, upt, att2,
    bs, br, gs, gr, keep, ux, uxr, ukeep, uy, uyr, uz, uzr, gx, gxr, gy, gyr, gz, gzr,
    send, recv, local,
):
    row, col = place()
    k, c = lax.div(row, 2), lax.rem(row, 2)
    y, xx, z, _ = grid_place()
    other = 1 - c
    mine = stretch(c)
    wire = Wire(send, recv)
    targets = chip_targets()
    for a in range(1, 8):
        targets += [at_grid(y, xx, z + a, 0), at_grid(y, xx, z + a, 1)]
    xt = [at_grid(y, xx + a, z, c) for a in (1, 2, 3)]
    yt = [at_grid(y + a, xx, z, c) for a in (1, 2, 3)]
    zt = [at_grid(y, xx, z + a, c) for a in range(1, 8)]
    targets += xt + yt
    targets += [(row, lax.rem(col + d, 16)) for d in (7, 8, 9)]
    for h in (0, 1):
        for d in (1, -1):
            targets += [at_chip(k + 1, h, col + d), at_chip(k - 1, h, col + d)]
    sib = at_chip(k, other, col)
    theirs = stretch(other)

    locals_ = []

    def local_copy(src, dst):
        copy = pltpu.make_async_copy(src, dst, local.at[len(locals_)])
        copy.start()
        locals_.append(copy)
        return copy

    slot = c * 8 + z
    centre = (1 + c) * 3 + 1
    own_x = local_copy(x, x2.at[c])
    own_w = local_copy(wp.at[:, pl.ds(mine, HALF)], zbuf.at[slot])
    local_copy(kv.at[:, pl.ds(mine, HALF)], kwin.at[centre])
    local_copy(q.at[:, pl.ds(mine, HALF)], q2.at[c])
    local_copy(cot.at[:, pl.ds(mine, HALF)], c2.at[c])
    local_copy(allow, allow2.at[c])
    greet(targets)

    wire.start(wp.at[:, pl.ds(theirs, HALF)], zbuf.at[slot], sib, 0, 0)
    for a in range(1, 8):
        for h in (0, 1):
            hh = c if h == 0 else other
            wire.start(
                wp.at[:, pl.ds(stretch(hh), HALF)],
                zbuf.at[slot],
                at_grid(y, xx, z + a, hh),
                2 * a + h,
                2 * a + h,
            )
    far = (3 - 3 * c) * 3 + 1
    step = 2 * c - 1

    def inner(d):
        return col != (15 if d == 1 else 0)

    def side_sends(parts, win, rr, n, m):
        for h, target_core, src in parts:
            for i, d in enumerate((1, -1)):

                @pl.when(inner(d))
                def _(h=h, i=i, d=d, src=src, target_core=target_core):
                    wire.copy(
                        src,
                        win.at[rr * 3 + 1 - d],
                        at_chip(k, target_core, col + d),
                        n + 2 * i + h,
                        m[i],
                    ).start()

    def side_drain(src, n, count):
        for h in range(count):
            for i, d in enumerate((1, -1)):

                @pl.when(inner(d))
                def _(h=h, i=i):
                    wire.copy(src, src, sib, n + 2 * i + h, n + 2 * i + h).wait_send()

    def side_arrivals(win, n):
        for i, d in enumerate((1, -1)):

            @pl.when(inner(-d))
            def _(i=i):
                wire.arrived(win.at[0], n + 2 * i)
                wire.arrived(win.at[0], n + 2 * i + 1)

    def clear_edges(win):
        for edge, cc in ((0, 0), (15, 2)):

            @pl.when(col == edge)
            def _(cc=cc):
                for rr in (1, 2):
                    win[rr * 3 + cc] = jnp.zeros(win.shape[1:], win.dtype)

    def corner(win, m, rr):
        base = m + (2 if rr else 0)
        src = win.at[rr * 3 + 1]
        for i, (d, hop, relay) in enumerate(((1, 7, 15), (-1, 8, 0))):
            spot, near = win.at[rr * 3 + 1 - d], win.at[rr * 3 + 1 + d]

            @pl.when((col != hop) & (col != relay))
            def _(d=d, i=i, spot=spot):
                wire.copy(src, spot, at_chip(k, c, col + d), base + i, base + i).start()

            @pl.when(col == hop)
            def _(i=i, near=near, relay=relay):
                wire.copy(src, near, (row, jnp.int32(relay)), base + i, base + 1 - i).start()

    def corner_relay(win, m, rr):
        base = m + (2 if rr else 0)
        for i, (d, hop, relay) in enumerate(((1, 7, 15), (-1, 8, 0))):
            spot, near = win.at[rr * 3 + 1 - d], win.at[rr * 3 + 1 + d]

            @pl.when(col == relay)
            def _(i=i, d=d, spot=spot, near=near, hop=hop):
                wire.arrived(near, base + 1 - i)
                wire.copy(near, spot, (row, jnp.int32(hop + d)), base + i, base + i).start()

    def corner_arrivals(win, m):
        for rr in (0, 3):
            base = m + (2 if rr else 0)
            for i, relay in enumerate((0, 15)):

                @pl.when(col != relay)
                def _(i=i):
                    wire.arrived(win.at[0], base + i)
        for n in range(4):
            wire.copy(win.at[0], win.at[0], sib, m + n, m + n).wait_send()

    def spread_tile(src, win, n, split):
        part = lambda h: src.at[:, pl.ds(h * HALF, HALF)] if split else src
        for h in (0, 1):
            wire.start(part(h), win.at[far], at_chip(k + step, h, col), n + h, n + c)
        parts = [(h, h, part(h)) for h in (0, 1)]
        side_sends(parts, win, 1 + c, n + 2, (n + 2 + c, n + 4 + c))
        full = src.at[:, pl.ds(theirs, HALF)] if split else src
        wire.start(full, win.at[centre], sib, n + 6, n + 6)

    for win in (kwin, lwin, vwin):
        clear_edges(win)
    spread_tile(kv, kwin, 16, True)
    wire.start(q.at[:, pl.ds(theirs, HALF)], q2.at[c], sib, 30, 30)
    wire.start(cot.at[:, pl.ds(theirs, HALF)], c2.at[c], sib, 31, 31)
    wire.start(x, x2.at[c], sib, 32, 32)
    wire.start(allow, allow2.at[c], sib, 33, 33)
    own_x.wait()
    low[...] = jnp.dot(x2[c], down[...], preferred_element_type=F32).astype(BF)
    lwin[centre] = low[...]
    spread_tile(low, lwin, 23, False)

    own_w.wait()
    wire.arrived(zbuf.at[0], 0)
    for a in range(1, 8):
        for h in (0, 1):
            wire.arrived(zbuf.at[0], 2 * a + h)
    r_out = lax.broadcasted_iota(jnp.int32, (96, 128), 0)
    r_in = lax.broadcasted_iota(jnp.int32, (96, 128), 1)
    pick = jnp.where(lax.div(r_out, 12) * 16 + lax.rem(r_out, 12) == r_in, 1.0, 0.0).astype(BF)
    for cc in (0, 1):
        part = zbuf[pl.ds(cc * 8, 8)].reshape(128, HALF)
        wblk[cc] = jnp.dot(pick, part, preferred_element_type=F32).astype(BF)

    xs = (at_grid(y, xx + 1, z, c), at_grid(y, xx - 1, z, c))
    ys = (at_grid(y + 1, xx, z, c), at_grid(y - 1, xx, z, c))

    def x_part(i):
        i = lax.rem(i + 4, 4)
        return lax.div(i, 2), lax.rem(i, 2)

    def y_part(i):
        return lax.rem(i + 4, 4)

    def small(yi, xi):
        a, b = x_part(xi)
        return wout.at[y_part(yi), a, :, b]

    def small_half(yi, xi, j):
        a, b = x_part(xi)
        return wout.at[y_part(yi), a, j, b]

    own_copy = pltpu.make_async_copy(wblk, small(y, xx), local.at[7])
    own_copy.start()

    def corners(win, n, m):
        for rr, first in ((0, n + 1), (3, n)):
            wire.arrived(win.at[rr * 3 + 1], first)
            corner(win, m, rr)

    def spread(along_x):
        sub = Wire(send, recv)
        w0 = 34
        if along_x:
            one, two = xs, ys
            full = lambda a, b: small(y + b, xx + a)
            half = lambda a, b, j: small_half(y + b, xx + a, j)
        else:
            one, two = ys, xs
            full = lambda a, b: small(y + a, xx + b)
            half = lambda a, b, j: small_half(y + a, xx + b, j)
        at = (0, -1, 1, 2)

        def across(n, src):
            for i in (0, 1):
                sub.start(src, full(at[n], 0), two[i], w0 + 4 + 2 * n + i, w0 + 4 + 2 * n + i)

        def pass_on(n):
            for i, d in enumerate((-1, 1)):
                sub.arrived(full(at[n], d), w0 + 4 + 2 * n + i)
                m = w0 + 12 + 2 * n + i
                sub.start(half(at[n], d, i), half(at[n], d, i), two[i], m, m)

        for i in (0, 1):
            sub.start(wblk, full(0, 0), one[i], w0 + i, w0 + i)
        across(0, wblk)
        for i, d in enumerate((-1, 1)):
            sub.arrived(full(d, 0), w0 + i)
            sub.start(half(d, 0, i), half(d, 0, i), one[i], w0 + 2 + i, w0 + 2 + i)
            across(1 + i, full(d, 0))
        corners(kwin, 16, 70)
        pass_on(0)
        for i in (0, 1):
            sub.arrived(half(2, 0, i), w0 + 2 + i)
        across(3, full(2, 0))
        corners(lwin, 23, 74)
        pass_on(1)
        pass_on(2)
        for win, m in ((kwin, 70), (lwin, 74)):
            for rr in (0, 3):
                corner_relay(win, m, rr)
        pass_on(3)
        for n in range(4):
            for i in (0, 1):
                sub.arrived(half(0, 2, i), w0 + 12 + 2 * n + i)
        own_copy.wait()
        sub.drain()

    @pl.when(c == 0)
    def _():
        spread(True)

    @pl.when(c == 1)
    def _():
        spread(False)

    wire.arrived(x2.at[0], 32)
    wire.arrived(lwin.at[0], 29)
    low2 = jnp.concatenate([lwin[4][:, :64], lwin[7][:, :64]], axis=0)

    @pl.loop(0, 3)
    def _(n):
        lanes = pl.ds(pl.multiple_of(n * 256, 256), 256)
        acc = jnp.dot(low2, up[:, lanes], preferred_element_type=F32)
        for yi in range(4):
            rows = wout[yi, :, :, :, :, lanes].reshape(768, 256)
            part = x2[:, :, yi * 768 : (yi + 1) * 768].reshape(512, 768)
            acc = acc + jnp.dot(part, rows, preferred_element_type=F32)
        acc = acc.astype(BF)
        vwin[4, :, lanes] = acc[:256]
        vwin[7, :, lanes] = acc[256:]

    v0 = 54
    wire.start(vwin.at[4], vwin.at[10], at_chip(k - 1, c, col), v0, v0)
    wire.start(vwin.at[7], vwin.at[1], at_chip(k + 1, c, col), v0 + 1, v0 + 1)
    for t in (0, 1):
        m = v0 + 2 + t
        side_sends([(t, c, vwin.at[4 + 3 * t])], vwin, 1 + t, v0 + 2, (m, m + 2))

    side_arrivals(kwin, 18)
    side_arrivals(lwin, 25)
    wire.arrived(kwin.at[0], 22)
    wire.arrived(q2.at[0], 30)
    wire.arrived(c2.at[0], 31)
    wire.arrived(allow2.at[0], 33)
    corner_arrivals(kwin, 70)
    corner_arrivals(lwin, 74)
    side_drain(kwin.at[0], 18, 2)
    side_drain(lwin.at[0], 25, 2)
    for copy in locals_[2:]:
        copy.wait()

    back[...] = jnp.zeros_like(back)
    upt[...] = jnp.zeros_like(upt)

    def probs(lo, hi):
        @pl.loop(lo, hi)
        def _(i):
            h, t = lax.div(i, 2), lax.rem(i, 2)
            lanes = pl.ds(pl.multiple_of(h * 128, 128), 128)
            keys = kwin[pl.ds(t * 3, 9), :, lanes].reshape(2304, 128)
            s_ref[...] = lax.dot_general(
                q2[t, :, lanes], keys, (((1,), (1,)), ((), ())), preferred_element_type=F32
            )
            limit = allow2[t, 0:1, :] * (radius[h] * radius[h] + 1.0) - 1.0

            @pl.loop(0, 8)
            def _(j):
                rows = pl.ds(pl.multiple_of(j * 32, 32), 32)
                s = jnp.where(dist[rows] <= limit, s_ref[rows] * 128**-0.5, -1e30)
                e = jnp.exp(s - jnp.max(s, axis=1, keepdims=True))
                p_ref[i, rows] = (e * (1.0 / jnp.sum(e, axis=1, keepdims=True))).astype(BF)

            vgt = jnp.dot(c2[t, :, lanes].T, p_ref[i], preferred_element_type=F32).astype(BF)
            bt = jnp.dot(up[:, lanes], vgt, preferred_element_type=F32)
            for n in range(9):
                back[t * 3 + n] += bt[:, n * 256 : (n + 1) * 256]
            lows = lwin[pl.ds(t * 3, 9)].reshape(2304, 128)
            rows = pl.ds(pl.multiple_of(h * 128, 128), 128)
            upt[rows] += jnp.dot(vgt, lows, preferred_element_type=F32)

    def attend(lo, hi):
        @pl.loop(lo, hi)
        def _(i):
            h, t = lax.div(i, 2), lax.rem(i, 2)
            lanes = pl.ds(pl.multiple_of(h * 128, 128), 128)
            vals = vwin[pl.ds(t * 3, 9), :, lanes].reshape(2304, 128)
            att2[t, :, lanes] = jnp.dot(p_ref[i], vals, preferred_element_type=F32).astype(BF)

    probs(0, 5)
    wire.arrived(vwin.at[10], v0)
    corner(vwin, 60, 3)
    wire.arrived(vwin.at[1], v0 + 1)
    corner(vwin, 60, 0)
    probs(5, 8)
    corner_relay(vwin, 60, 3)
    corner_relay(vwin, 60, 0)
    probs(8, 12)

    def values_here():
        side_arrivals(vwin, v0 + 2)
        corner_arrivals(vwin, 60)
        side_drain(vwin.at[0], v0 + 2, 2)

    b0 = 78
    for n in range(12):
        rr, cc = n // 3, n % 3
        bs[n] = back[n].astype(BF)
        dk, h = ((-1, 1), (0, 0), (0, 1), (1, 0))[rr]
        slot = (0 if rr in (1, 2) else 6) + cc * 2
        if n in (4, 7):

            @pl.when(c != h)
            def _():
                wire.copy(bs.at[n], br.at[slot + c], sib, b0 + 12, b0 + slot + c).start()
        else:
            target = at_chip(k + dk, h, col + cc - 1)
            wire.start(bs.at[n], br.at[slot + c], target, b0 + n, b0 + slot + c)

    u0, e0 = 92, 116
    for a in range(4):
        for b in range(4):
            ux[a, b] = upt[(a * 4 + b) * 48 : (a * 4 + b + 1) * 48, 0:64].astype(BF)
    for i in range(3):
        wire.start(ux.at[lax.rem(xx + i + 1, 4)], uxr.at[i], xt[i], u0 + i, u0 + i)

    total = back[(1 + c) * 3 + 1]
    wire.arrived(br.at[0], b0 + 2 + other)
    total = total + br[2 + other].astype(F32)
    for slot in range(12):
        if slot not in (2, 3):
            wire.arrived(br.at[0], b0 + slot)
            total = total + br[slot].astype(F32)
    hi = total.astype(BF)
    lo = (total - hi.astype(F32)).astype(BF)
    both = jnp.concatenate([hi, lo], axis=0)

    for i in range(3):
        wire.arrived(uxr.at[0], u0 + i)
    for b in range(4):
        ua = upt[pl.ds(pl.multiple_of((xx * 4 + b) * 48, 16), 48), 0:64]
        for i in range(3):
            ua = ua + uxr[i, b].astype(F32)
        ukeep[b] = ua
        uy[b] = ua.astype(BF)
    for i in range(3):
        wire.start(uy.at[lax.rem(y + i + 1, 4)], uyr.at[i], yt[i], u0 + 3 + i, u0 + 3 + i)

    @pl.loop(0, 8)
    def _(i):
        part = x2[c, :, pl.ds(pl.multiple_of(i * 384, 384), 384)]
        g = jnp.dot(both, part, preferred_element_type=F32)
        g = (g[:64] + g[64:]).T
        yi, xhi = lax.div(i, 2), lax.rem(i, 2)
        for cc in (0, 1):
            for xl in (0, 1):
                rows = g[(cc * 2 + xl) * 96 : (cc * 2 + xl + 1) * 96]
                keep[cc, xhi * 2 + xl, yi] = rows
                gs[cc, xhi * 2 + xl, yi] = rows.astype(BF)

    wire.start(gs.at[other], gr, sib, e0, e0)

    for i in range(3):
        wire.arrived(uyr.at[0], u0 + 3 + i)
    ua = ukeep[y]
    for i in range(3):
        ua = ua + uyr[i].astype(F32)
    uz[...] = ua.astype(BF)
    uzr[z] = ua.astype(BF)
    for i in range(7):
        wire.start(uz, uzr.at[z], zt[i], u0 + 6 + i, u0 + 6 + i)

    wire.arrived(gr, e0)
    for a in range(4):
        for b in range(4):
            full = keep[c, a, b] + gr[a, b].astype(F32)
            keep[0, a, b] = full
            gx[a, b] = full.astype(BF)
    for i in range(3):
        wire.start(gx.at[lax.rem(xx + i + 1, 4)], gxr.at[i], xt[i], e0 + 1 + i, e0 + 1 + i)

    scale = 65536**-0.5
    for i in range(7):
        wire.arrived(uz, u0 + 6 + i)
    ua = uzr[0].astype(F32)
    for i in range(1, 8):
        ua = ua + uzr[i].astype(F32)
    gu[c, xx, y] = ua * scale
    spot = gu.at[c, xx, y]
    for i in range(3):
        wire.start(spot, spot, yt[i], u0 + 13 + i, u0 + 13 + i)

    for i in range(3):
        wire.arrived(gxr.at[0], e0 + 1 + i)
    for b in range(4):
        acc = keep[0, xx, b]
        for i in range(3):
            acc = acc + gxr[i, b].astype(F32)
        keep[1, 0, b] = acc
        gy[b] = acc.astype(BF)
    for i in range(3):
        wire.start(gy.at[lax.rem(y + i + 1, 4)], gyr.at[i], yt[i], e0 + 4 + i, e0 + 4 + i)

    for i in range(3):
        wire.arrived(spot, u0 + 13 + i)
    for i in range(3):
        wire.start(gu.at[c, xx], gu.at[c, xx], xt[i], u0 + 16 + i, u0 + 16 + i)

    values_here()
    attend(0, 6)

    for i in range(3):
        wire.arrived(gyr.at[0], e0 + 4 + i)
    acc = keep[1, 0, y]
    for i in range(3):
        acc = acc + gyr[i].astype(F32)
    r_out = lax.broadcasted_iota(jnp.int32, (128, 96), 0)
    r_in = lax.broadcasted_iota(jnp.int32, (128, 96), 1)
    row_of = lax.div(r_out, 16) * 12 + lax.rem(r_out, 16)
    pick = jnp.where((row_of == r_in) & (lax.rem(r_out, 16) < 12), 1.0, 0.0).astype(BF)
    parts = jnp.dot(pick, acc.astype(BF), preferred_element_type=F32).astype(BF)
    for i in range(8):
        gz[i] = parts[i * 16 : (i + 1) * 16]
    for i in range(7):
        wire.start(gz.at[lax.rem(z + i + 1, 8)], gzr.at[i], zt[i], e0 + 7 + i, e0 + 7 + i)

    for i in range(3):
        wire.arrived(gu.at[c, xx], u0 + 16 + i)
    wire.start(gu.at[c], gu.at[c], sib, u0 + 19, u0 + 19)

    attend(6, 12)
    wire.start(att2.at[other], att.at[:, pl.ds(mine, HALF)], sib, e0 + 14, e0 + 14)
    keep_att = pltpu.make_async_copy(att2.at[c], att.at[:, pl.ds(mine, HALF)], local.at[6])
    keep_att.start()

    for i in range(7):
        wire.arrived(gzr.at[0], e0 + 7 + i)
    acc = gz[z].astype(F32)
    for i in range(7):
        acc = acc + gzr[i].astype(F32)
    gd[...] = acc * scale
    wire.arrived(gu.at[c], u0 + 19)
    wire.arrived(att.at[:, pl.ds(mine, HALF)], e0 + 14)
    keep_att.wait()
    wire.copy(bs.at[0], bs.at[0], sib, b0 + 12, b0 + 12).wait_send()
    wire.drain()


def distances():
    qp = np.arange(256)
    kp = np.arange(2304)
    kr = (kp // 768) * 16 + (kp % 256) // 16 - 16
    kc = (kp // 256 % 3) * 16 + kp % 16 - 16
    dr = kr[None] - (qp // 16)[:, None]
    dc = kc[None] - (qp % 16)[:, None]
    return (dr * dr + dc * dc).astype(np.float32)


def fused(*args):
    vm = pl.BlockSpec(memory_space=pltpu.VMEM)
    hb = pl.BlockSpec(memory_space=pl.ANY)
    return pl.pallas_call(
        kernel,
        out_shape=[
            jax.ShapeDtypeStruct((256, 1536), BF),
            jax.ShapeDtypeStruct((16, 64), F32),
            jax.ShapeDtypeStruct((2, 4, 4, 48, 64), F32),
        ],
        in_specs=[pl.BlockSpec(memory_space=pltpu.SMEM), hb, hb, hb, hb, hb, hb, vm, vm, vm],
        out_specs=[hb, vm, vm],
        scratch_shapes=[
            pltpu.VMEM((2, 256, HALF), BF),
            pltpu.VMEM((12, 256, HALF), BF),
            pltpu.VMEM((2, 256, HALF), BF),
            pltpu.VMEM((12, 256, 128), BF),
            pltpu.VMEM((2, 256, 3072), BF),
            pltpu.VMEM((4, 2, 2, 2, 96, HALF), BF),
            pltpu.VMEM((2, 8, 2304), F32),
            pltpu.VMEM((16, 16, HALF), BF),
            pltpu.VMEM((2, 96, HALF), BF),
            pltpu.VMEM((256, 128), BF),
            pltpu.VMEM((12, 256, HALF), BF),
            pltpu.VMEM((256, 2304), F32),
            pltpu.VMEM((12, 256, 2304), BF),
            pltpu.VMEM((12, 64, 256), F32),
            pltpu.VMEM((HALF, 128), F32),
            pltpu.VMEM((2, 256, HALF), BF),
            pltpu.VMEM((12, 64, 256), BF),
            pltpu.VMEM((12, 64, 256), BF),
            pltpu.VMEM((2, 4, 4, 96, 64), BF),
            pltpu.VMEM((4, 4, 96, 64), BF),
            pltpu.VMEM((2, 4, 4, 96, 64), F32),
            pltpu.VMEM((4, 4, 48, 64), BF),
            pltpu.VMEM((3, 4, 48, 64), BF),
            pltpu.VMEM((4, 48, 64), F32),
            pltpu.VMEM((4, 48, 64), BF),
            pltpu.VMEM((3, 48, 64), BF),
            pltpu.VMEM((48, 64), BF),
            pltpu.VMEM((8, 48, 64), BF),
            pltpu.VMEM((4, 4, 96, 64), BF),
            pltpu.VMEM((3, 4, 96, 64), BF),
            pltpu.VMEM((4, 96, 64), BF),
            pltpu.VMEM((3, 96, 64), BF),
            pltpu.VMEM((8, 16, 64), BF),
            pltpu.VMEM((7, 16, 64), BF),
            pltpu.SemaphoreType.DMA((136,)),
            pltpu.SemaphoreType.DMA((136,)),
            pltpu.SemaphoreType.DMA((8,)),
        ],
        compiler_params=pltpu.CompilerParams(
            collective_id=0, has_side_effects=True, vmem_limit_bytes=60 * MIB
        ),
        name="fused",
    )(*args)


def allowed_row(tile_mask):
    row, col = place()
    r = row + jnp.arange(3, dtype=jnp.int32) - 1
    s = col + jnp.arange(3, dtype=jnp.int32) - 1
    rows = lax.axis_size("row")
    cols = lax.axis_size("col")
    inside = ((r >= 0) & (r < rows))[:, None] & ((s >= 0) & (s < cols))[None, :]
    flags = jnp.where(inside.reshape(9) & (tile_mask.reshape(9) > 0), 1.0, 0.0).astype(F32)
    return jnp.broadcast_to(jnp.repeat(flags, 256)[None], (8, 2304))


def per_device(
    patch_tokens,
    queries,
    key_vectors,
    cotangent,
    value_weight,
    adapter_down,
    adapter_up,
    radius,
    tile_mask,
):
    core = lax.rem(lax.axis_index("row"), 2)
    att, gd, gu = fused(
        lax.dynamic_slice_in_dim(radius, core * 6, 6, 0).astype(F32),
        queries.reshape(256, 1536),
        key_vectors.reshape(256, 1536),
        cotangent.reshape(256, 1536),
        patch_tokens.reshape(256, 3072),
        jnp.pad(value_weight, ((0, 4), (0, 0))),
        allowed_row(tile_mask),
        jnp.pad(adapter_down, ((0, 0), (0, 64))),
        lax.dynamic_slice_in_dim(adapter_up, core * HALF, HALF, 1),
        jnp.asarray(distances()),
    )
    return att.reshape(16, 16, 1536), gd[:12], gu.reshape(1536, 64).T


def solution(mesh):
    placed = (
        P("row", "col", None),
        P("row", "col", None),
        P("row", "col", None),
        P("row", "col", None),
        P(("row", "col"), None),
        P(),
        P(),
        P(),
        P("row", "col", None),
    )
    return jax.shard_map(
        per_device,
        mesh=mesh,
        in_specs=placed,
        out_specs=(P("row", "col", None), P(("row", "col"), None), P()),
        check_vma=False,
    )
```

```python
import jax
import jax.numpy as jnp
import numpy as np
from jax import lax
from jax.experimental import pallas as pl
from jax.experimental.pallas import tpu as pltpu
from jax.sharding import PartitionSpec as P

MESH = pl.DeviceIdType.MESH
BF = jnp.bfloat16
F32 = jnp.float32
HALF = 768
MIB = 2**20


def place():
    row = lax.axis_index("row")
    col = lax.axis_index("col")
    return row, col


def grid_place():
    row, col = place()
    y = lax.div(row, 4)
    x = lax.rem(lax.div(row, 2), 2) * 2 + lax.div(col, 8)
    return y, x, lax.rem(col, 8), lax.rem(row, 2)


def at_grid(y, x, z, c):
    y = lax.rem(y + 4, 4)
    x = lax.rem(x + 4, 4)
    z = lax.rem(z + 8, 8)
    return (y * 4 + lax.div(x, 2) * 2 + c, lax.rem(x, 2) * 8 + z)


def at_chip(k, h, col):
    return (lax.rem(k + 8, 8) * 2 + h, lax.rem(col + 16, 16))


def greet(targets):
    barrier = pltpu.get_barrier_semaphore()
    for target in targets:
        pl.semaphore_signal(barrier, inc=1, device_id=target, device_id_type=MESH)
    pl.semaphore_wait(barrier, len(targets))


class Wire:
    def __init__(self, send, recv):
        self.send, self.recv, self.pending = send, recv, []

    def copy(self, src, dst, target, s, r):
        return pltpu.make_async_remote_copy(
            src_ref=src,
            dst_ref=dst,
            send_sem=self.send.at[s],
            recv_sem=self.recv.at[r],
            device_id=target,
            device_id_type=MESH,
        )

    def start(self, src, dst, target, s, r):
        copy = self.copy(src, dst, target, s, r)
        copy.start()
        self.pending.append(copy)

    def arrived(self, dst, r):
        row, col = place()
        self.copy(dst, dst, (row + 1 - 2 * lax.rem(row, 2), col), r, r).wait_recv()

    def drain(self):
        for copy in self.pending:
            copy.wait_send()
        self.pending = []


def chip_targets():
    row, col = place()
    k, c = lax.div(row, 2), lax.rem(row, 2)
    out = [at_chip(k, 1 - c, col)]
    for h in (0, 1):
        out += [at_chip(k + 1, h, col), at_chip(k - 1, h, col)]
        out += [at_chip(k, h, col + 1), at_chip(k, h, col - 1)]
    return out


def stretch(c):
    return pl.multiple_of(c * HALF, HALF)


def kernel(
    radius, mask, q, kv, cot, x, w, down, up, dist,
    att, gd, gu,
    q2, kwin, c2, lwin, x2, wout, allow2, zbuf, wblk, low, wp, gun,
    vwin, s_ref, p_ref, back, upt, att2,
    bs, br, gs, gr, keep, ux, uxr, ukeep, uy, uyr, uz, uzr, gx, gxr, gy, gyr, gz, gzr,
    send, recv, local,
):
    row, col = place()
    k, c = lax.div(row, 2), lax.rem(row, 2)
    y, xx, z, _ = grid_place()
    other = 1 - c
    mine = stretch(c)
    wire = Wire(send, recv)
    targets = chip_targets()
    for a in range(1, 8):
        targets += [at_grid(y, xx, z + a, 0), at_grid(y, xx, z + a, 1)]
    xt = [at_grid(y, xx + a, z, c) for a in (1, 2, 3)]
    yt = [at_grid(y + a, xx, z, c) for a in (1, 2, 3)]
    zt = [at_grid(y, xx, z + a, c) for a in range(1, 8)]
    targets += xt + yt
    targets += [at_chip(k, h, col + d) for d in (7, 8, 9) for h in (0, 1)]
    for h in (0, 1):
        for d in (1, -1):
            targets += [at_chip(k + 1, h, col + d), at_chip(k - 1, h, col + d)]
    sib = at_chip(k, other, col)
    theirs = stretch(other)

    locals_ = []

    def local_copy(src, dst):
        copy = pltpu.make_async_copy(src, dst, local.at[len(locals_)])
        copy.start()
        locals_.append(copy)
        return copy

    slot = c * 8 + z
    centre = (1 + c) * 3 + 1
    own_x = local_copy(x, x2.at[c])
    local_copy(kv.at[:, pl.ds(mine, HALF)], kwin.at[centre])
    local_copy(q.at[:, pl.ds(mine, HALF)], q2.at[c])
    local_copy(cot.at[:, pl.ds(mine, HALF)], c2.at[c])
    for n in range(9):
        r, t = row + n // 3 - 1, col + n % 3 - 1
        seen = (r >= 0) & (r < 16) & (t >= 0) & (t < 16) & (mask[0, 0, n] > 0)
        allow2[c, :, n * 256 : (n + 1) * 256] = jnp.full((8, 256), jnp.where(seen, 1.0, 0.0))
    r_out = lax.broadcasted_iota(jnp.int32, (16, 12), 0)
    r_in = lax.broadcasted_iota(jnp.int32, (16, 12), 1)
    wp[...] = jnp.dot(
        jnp.where(r_out == r_in, 1.0, 0.0).astype(BF), w[...], preferred_element_type=F32
    ).astype(BF)
    local_copy(wp.at[:, pl.ds(mine, HALF)], zbuf.at[slot])
    greet(targets)

    wire.start(wp.at[:, pl.ds(theirs, HALF)], zbuf.at[slot], sib, 0, 0)
    for a in range(1, 8):
        for h in (0, 1):
            hh = c if h == 0 else other
            wire.start(
                wp.at[:, pl.ds(stretch(hh), HALF)],
                zbuf.at[slot],
                at_grid(y, xx, z + a, hh),
                2 * a + h,
                2 * a + h,
            )
    far = (3 - 3 * c) * 3 + 1
    step = 2 * c - 1

    crossing = ((0, 1, 7, 15), (1, -1, 8, 0))

    def side_sends(parts, win, rr, n, which):
        for h, target_core, src in parts:
            for i, d, hop, relay in crossing:
                spot, near = win.at[rr * 3 + 1 - d], win.at[rr * 3 + 1 + d]

                @pl.when((col != hop) & (col != relay))
                def _(h=h, i=i, d=d, src=src, target_core=target_core, spot=spot):
                    target = at_chip(k, target_core, col + d)
                    wire.copy(src, spot, target, n + 2 * i + h, n + 2 * i + which).start()

                @pl.when(col == hop)
                def _(h=h, i=i, src=src, target_core=target_core, near=near, relay=relay):
                    target = at_chip(k, target_core, jnp.int32(relay))
                    wire.copy(src, near, target, n + 2 * i + h, n + 2 * (1 - i) + which).start()

    def side_relay(win, n):
        for i, d, hop, relay in crossing:

            @pl.when(col == relay)
            def _(i=i, d=d, hop=hop):
                for t in (0, 1):
                    spot, near = win.at[(1 + t) * 3 + 1 - d], win.at[(1 + t) * 3 + 1 + d]
                    wire.arrived(near, n + 2 * (1 - i) + t)
                    m = n + 2 * i + t
                    wire.copy(near, spot, (row, jnp.int32(hop + d)), m, m).start()

    def side_arrivals(win, n):
        for i, edge in enumerate((0, 15)):

            @pl.when(col != edge)
            def _(i=i):
                wire.arrived(win.at[0], n + 2 * i)
                wire.arrived(win.at[0], n + 2 * i + 1)

        for m in range(4):
            wire.copy(win.at[0], win.at[0], sib, n + m, n + m).wait_send()

    def clear_edges(win):
        for edge, cc in ((0, 0), (15, 2)):

            @pl.when(col == edge)
            def _(cc=cc):
                for rr in (0, 3):
                    win[rr * 3 + cc] = jnp.zeros(win.shape[1:], win.dtype)

    def corner(win, m, rr):
        src = win.at[rr * 3 + 1]
        for i, d, _, edge in crossing:

            @pl.when(col != edge)
            def _(i=i, d=d):
                n = m + (2 if rr else 0) + i
                wire.copy(src, win.at[rr * 3 + 1 - d], at_chip(k, c, col + d), n, n).start()

    def corner_arrivals(win, m):
        for n in (m, m + 2):
            for i, edge in enumerate((0, 15)):

                @pl.when(col != edge)
                def _(n=n, i=i):
                    wire.arrived(win.at[0], n + i)

                @pl.when(col != 15 - edge)
                def _(n=n, i=i):
                    wire.copy(win.at[0], win.at[0], sib, n + i, n + i).wait_send()

    def spread_tile(src, win, n, split):
        part = lambda h: src.at[:, pl.ds(h * HALF, HALF)] if split else src
        for h in (0, 1):
            wire.start(part(h), win.at[far], at_chip(k + step, h, col), n + h, n + c)
        side_sends([(h, h, part(h)) for h in (0, 1)], win, 1 + c, n + 2, c)
        full = src.at[:, pl.ds(theirs, HALF)] if split else src
        wire.start(full, win.at[centre], sib, n + 6, n + 6)

    for win in (kwin, lwin, vwin):
        clear_edges(win)
    spread_tile(kv, kwin, 16, True)
    wire.start(q.at[:, pl.ds(theirs, HALF)], q2.at[c], sib, 30, 30)
    wire.start(cot.at[:, pl.ds(theirs, HALF)], c2.at[c], sib, 31, 31)
    wire.start(x, x2.at[c], sib, 32, 32)
    wire.start(allow2.at[c], allow2.at[c], sib, 33, 33)
    own_x.wait()
    low[:, 0:64] = lax.dot_general(
        x2[c], down[...], (((1,), (1,)), ((), ())), preferred_element_type=F32
    ).astype(BF)
    low[:, 64:128] = jnp.zeros((256, 64), BF)
    lwin[centre] = low[...]
    spread_tile(low, lwin, 23, False)

    locals_.pop().wait()
    wire.arrived(zbuf.at[0], 0)
    for a in range(1, 8):
        for h in (0, 1):
            wire.arrived(zbuf.at[0], 2 * a + h)
    r_out = lax.broadcasted_iota(jnp.int32, (96, 128), 0)
    r_in = lax.broadcasted_iota(jnp.int32, (96, 128), 1)
    pick = jnp.where(lax.div(r_out, 12) * 16 + lax.rem(r_out, 12) == r_in, 1.0, 0.0).astype(BF)
    for cc in (0, 1):
        part = zbuf[pl.ds(cc * 8, 8)].reshape(128, HALF)
        wblk[cc] = jnp.dot(pick, part, preferred_element_type=F32).astype(BF)

    xs = (at_grid(y, xx + 1, z, c), at_grid(y, xx - 1, z, c))
    ys = (at_grid(y + 1, xx, z, c), at_grid(y - 1, xx, z, c))

    def x_part(i):
        i = lax.rem(i + 4, 4)
        return lax.div(i, 2), lax.rem(i, 2)

    def y_part(i):
        return lax.rem(i + 4, 4)

    def small(yi, xi):
        a, b = x_part(xi)
        return wout.at[y_part(yi), a, :, b]

    def small_half(yi, xi, j):
        a, b = x_part(xi)
        return wout.at[y_part(yi), a, j, b]

    own_copy = pltpu.make_async_copy(wblk, small(y, xx), local.at[7])
    own_copy.start()

    def corners(win, n, m):
        for rr, first in ((0, n + 1), (3, n)):
            wire.arrived(win.at[rr * 3 + 1], first)
            corner(win, m, rr)

    def spread(along_x):
        sub = Wire(send, recv)
        w0 = 34
        if along_x:
            one, two = xs, ys
            full = lambda a, b: small(y + b, xx + a)
            half = lambda a, b, j: small_half(y + b, xx + a, j)
        else:
            one, two = ys, xs
            full = lambda a, b: small(y + a, xx + b)
            half = lambda a, b, j: small_half(y + a, xx + b, j)
        at = (0, -1, 1, 2)

        def across(n, src):
            for i in (0, 1):
                sub.start(src, full(at[n], 0), two[i], w0 + 4 + 2 * n + i, w0 + 4 + 2 * n + i)

        def pass_on(n):
            for i, d in enumerate((-1, 1)):
                sub.arrived(full(at[n], d), w0 + 4 + 2 * n + i)
                m = w0 + 12 + 2 * n + i
                sub.start(half(at[n], d, i), half(at[n], d, i), two[i], m, m)

        for i in (0, 1):
            sub.start(wblk, full(0, 0), one[i], w0 + i, w0 + i)
        across(0, wblk)
        for i, d in enumerate((-1, 1)):
            sub.arrived(full(d, 0), w0 + i)
            sub.start(half(d, 0, i), half(d, 0, i), one[i], w0 + 2 + i, w0 + 2 + i)
            across(1 + i, full(d, 0))
        corners(kwin, 16, 70)
        side_relay(kwin, 18)
        pass_on(0)
        for i in (0, 1):
            sub.arrived(half(2, 0, i), w0 + 2 + i)
        across(3, full(2, 0))
        corners(lwin, 23, 74)
        side_relay(lwin, 25)
        pass_on(1)
        pass_on(2)
        pass_on(3)
        for n in range(4):
            for i in (0, 1):
                sub.arrived(half(0, 2, i), w0 + 12 + 2 * n + i)
        own_copy.wait()
        sub.drain()

    busy = lax.rem(z + 1, 8) < 2

    @pl.when((c == 0) | busy)
    def _():
        spread(True)

    @pl.when((c == 1) & jnp.logical_not(busy))
    def _():
        spread(False)

    def heads(start, width):
        return pl.ds(pl.multiple_of(mine + start, 128), width)

    wire.arrived(x2.at[0], 32)
    wire.arrived(lwin.at[0], 29)
    low2 = jnp.concatenate([lwin[4][:, :64], lwin[7][:, :64]], axis=0)

    @pl.loop(0, 3)
    def _(n):
        lanes = pl.ds(pl.multiple_of(n * 256, 256), 256)
        acc = jnp.dot(low2, up[:, heads(n * 256, 256)], preferred_element_type=F32)
        for yi in range(4):
            rows = wout[yi, :, :, :, :, lanes].reshape(768, 256)
            part = x2[:, :, yi * 768 : (yi + 1) * 768].reshape(512, 768)
            acc = acc + jnp.dot(part, rows, preferred_element_type=F32)
        acc = acc.astype(BF)
        vwin[4, :, lanes] = acc[:256]
        vwin[7, :, lanes] = acc[256:]

    v0 = 54
    wire.start(vwin.at[4], vwin.at[10], at_chip(k - 1, c, col), v0, v0)
    wire.start(vwin.at[7], vwin.at[1], at_chip(k + 1, c, col), v0 + 1, v0 + 1)
    for t in (0, 1):
        side_sends([(t, c, vwin.at[4 + 3 * t])], vwin, 1 + t, v0 + 2, t)

    side_arrivals(kwin, 18)
    side_arrivals(lwin, 25)
    wire.arrived(kwin.at[0], 22)
    wire.arrived(q2.at[0], 30)
    wire.arrived(c2.at[0], 31)
    wire.arrived(allow2.at[0], 33)
    corner_arrivals(kwin, 70)
    corner_arrivals(lwin, 74)
    for copy in locals_[1:]:
        copy.wait()

    back[...] = jnp.zeros_like(back)
    upt[...] = jnp.zeros_like(upt)

    def probs(lo, hi):
        @pl.loop(lo, hi)
        def _(i):
            h, t = lax.div(i, 2), lax.rem(i, 2)
            lanes = pl.ds(pl.multiple_of(h * 128, 128), 128)
            keys = kwin[pl.ds(t * 3, 9), :, lanes].reshape(2304, 128)
            s_ref[...] = lax.dot_general(
                q2[t, :, lanes], keys, (((1,), (1,)), ((), ())), preferred_element_type=F32
            )
            reach = radius[c * 6 + h]
            limit = allow2[t, 0:1, :] * (reach * reach + 1).astype(F32) - 1.0

            @pl.loop(0, 8)
            def _(j):
                rows = pl.ds(pl.multiple_of(j * 32, 32), 32)
                s = jnp.where(dist[rows] <= limit, s_ref[rows] * 128**-0.5, -1e30)
                e = jnp.exp(s - jnp.max(s, axis=1, keepdims=True))
                p_ref[i, rows] = (e * (1.0 / jnp.sum(e, axis=1, keepdims=True))).astype(BF)

            vgt = jnp.dot(c2[t, :, lanes].T, p_ref[i], preferred_element_type=F32).astype(BF)
            bt = jnp.dot(up[:, heads(h * 128, 128)], vgt, preferred_element_type=F32)
            for n in range(9):
                back[t * 3 + n] += bt[:, n * 256 : (n + 1) * 256]
            lows = lwin[pl.ds(t * 3, 9)].reshape(2304, 128)
            rows = pl.ds(pl.multiple_of(h * 128, 128), 128)
            upt[rows] += jnp.dot(vgt, lows, preferred_element_type=F32)

    def attend(lo, hi):
        @pl.loop(lo, hi)
        def _(i):
            h, t = lax.div(i, 2), lax.rem(i, 2)
            lanes = pl.ds(pl.multiple_of(h * 128, 128), 128)
            vals = vwin[pl.ds(t * 3, 9), :, lanes].reshape(2304, 128)
            att2[t, :, lanes] = jnp.dot(p_ref[i], vals, preferred_element_type=F32).astype(BF)

    probs(0, 5)
    wire.arrived(vwin.at[10], v0)
    corner(vwin, 60, 3)
    wire.arrived(vwin.at[1], v0 + 1)
    corner(vwin, 60, 0)
    side_relay(vwin, v0 + 2)
    probs(5, 12)

    def values_here():
        side_arrivals(vwin, v0 + 2)
        corner_arrivals(vwin, 60)

    b0 = 78
    for n in range(12):
        rr, cc = n // 3, n % 3
        bs[n] = back[n].astype(BF)
        dk, h = ((-1, 1), (0, 0), (0, 1), (1, 0))[rr]
        slot = (0 if rr in (1, 2) else 6) + cc * 2
        if n in (4, 7):

            @pl.when(c != h)
            def _():
                wire.copy(bs.at[n], br.at[slot + c], sib, b0 + 12, b0 + slot + c).start()
        else:
            target = at_chip(k + dk, h, col + cc - 1)
            wire.start(bs.at[n], br.at[slot + c], target, b0 + n, b0 + slot + c)

    u0, e0 = 92, 116
    for a in range(4):
        for b in range(4):
            ux[a, b] = upt[(a * 4 + b) * 48 : (a * 4 + b + 1) * 48, 0:64].astype(BF)
    for i in range(3):
        wire.start(ux.at[lax.rem(xx + i + 1, 4)], uxr.at[i], xt[i], u0 + i, u0 + i)

    total = back[(1 + c) * 3 + 1]
    wire.arrived(br.at[0], b0 + 2 + other)
    total = total + br[2 + other].astype(F32)
    for slot in range(12):
        if slot not in (2, 3):
            wire.arrived(br.at[0], b0 + slot)
            total = total + br[slot].astype(F32)
    hi = total.astype(BF)
    lo = (total - hi.astype(F32)).astype(BF)
    both = jnp.concatenate([hi, lo], axis=0)

    for i in range(3):
        wire.arrived(uxr.at[0], u0 + i)
    for b in range(4):
        ua = upt[pl.ds(pl.multiple_of((xx * 4 + b) * 48, 16), 48), 0:64]
        for i in range(3):
            ua = ua + uxr[i, b].astype(F32)
        ukeep[b] = ua
        uy[b] = ua.astype(BF)
    for i in range(3):
        wire.start(uy.at[lax.rem(y + i + 1, 4)], uyr.at[i], yt[i], u0 + 3 + i, u0 + 3 + i)

    @pl.loop(0, 8)
    def _(i):
        part = x2[c, :, pl.ds(pl.multiple_of(i * 384, 384), 384)]
        g = jnp.dot(both, part, preferred_element_type=F32)
        g = (g[:64] + g[64:]).T
        yi, xhi = lax.div(i, 2), lax.rem(i, 2)
        for cc in (0, 1):
            for xl in (0, 1):
                rows = g[(cc * 2 + xl) * 96 : (cc * 2 + xl + 1) * 96]
                keep[cc, xhi * 2 + xl, yi] = rows
                gs[cc, xhi * 2 + xl, yi] = rows.astype(BF)

    wire.start(gs.at[other], gr, sib, e0, e0)

    for i in range(3):
        wire.arrived(uyr.at[0], u0 + 3 + i)
    ua = ukeep[y]
    for i in range(3):
        ua = ua + uyr[i].astype(F32)
    uz[...] = ua.astype(BF)
    uzr[z] = ua.astype(BF)
    for i in range(7):
        wire.start(uz, uzr.at[z], zt[i], u0 + 6 + i, u0 + 6 + i)

    wire.arrived(gr, e0)
    for a in range(4):
        for b in range(4):
            full = keep[c, a, b] + gr[a, b].astype(F32)
            keep[0, a, b] = full
            gx[a, b] = full.astype(BF)
    for i in range(3):
        wire.start(gx.at[lax.rem(xx + i + 1, 4)], gxr.at[i], xt[i], e0 + 1 + i, e0 + 1 + i)

    scale = 65536**-0.5
    for i in range(7):
        wire.arrived(uz, u0 + 6 + i)
    ua = uzr[0].astype(F32)
    for i in range(1, 8):
        ua = ua + uzr[i].astype(F32)
    gun[c, xx, y] = ua * scale
    spot = gun.at[c, xx, y]
    for i in range(3):
        wire.start(spot, spot, yt[i], u0 + 13 + i, u0 + 13 + i)

    for i in range(3):
        wire.arrived(gxr.at[0], e0 + 1 + i)
    for b in range(4):
        acc = keep[0, xx, b]
        for i in range(3):
            acc = acc + gxr[i, b].astype(F32)
        keep[1, 0, b] = acc
        gy[b] = acc.astype(BF)
    for i in range(3):
        wire.start(gy.at[lax.rem(y + i + 1, 4)], gyr.at[i], yt[i], e0 + 4 + i, e0 + 4 + i)

    for i in range(3):
        wire.arrived(spot, u0 + 13 + i)
    for i in range(3):
        wire.start(gun.at[c, xx], gun.at[c, xx], xt[i], u0 + 16 + i, u0 + 16 + i)

    values_here()
    attend(0, 6)

    for i in range(3):
        wire.arrived(gyr.at[0], e0 + 4 + i)
    acc = keep[1, 0, y]
    for i in range(3):
        acc = acc + gyr[i].astype(F32)
    r_out = lax.broadcasted_iota(jnp.int32, (128, 96), 0)
    r_in = lax.broadcasted_iota(jnp.int32, (128, 96), 1)
    row_of = lax.div(r_out, 16) * 12 + lax.rem(r_out, 16)
    pick = jnp.where((row_of == r_in) & (lax.rem(r_out, 16) < 12), 1.0, 0.0).astype(BF)
    parts = jnp.dot(pick, acc.astype(BF), preferred_element_type=F32).astype(BF)
    for i in range(8):
        gz[i] = parts[i * 16 : (i + 1) * 16]
    for i in range(7):
        wire.start(gz.at[lax.rem(z + i + 1, 8)], gzr.at[i], zt[i], e0 + 7 + i, e0 + 7 + i)

    for i in range(3):
        wire.arrived(gun.at[c, xx], u0 + 16 + i)
    wire.start(gun.at[c], gun.at[c], sib, u0 + 19, u0 + 19)

    attend(6, 12)
    wire.start(att2.at[other], att.at[:, pl.ds(mine, HALF)], sib, e0 + 14, e0 + 14)
    keep_att = pltpu.make_async_copy(att2.at[c], att.at[:, pl.ds(mine, HALF)], local.at[6])
    keep_att.start()

    for i in range(7):
        wire.arrived(gzr.at[0], e0 + 7 + i)
    acc = gz[z].astype(F32)
    for i in range(7):
        acc = acc + gzr[i].astype(F32)
    gd[...] = (acc * scale)[0:12]
    wire.arrived(gun.at[c], u0 + 19)
    for cc in (0, 1):
        for i in (0, 2):
            lanes = pl.ds(cc * HALF + i * 192, 384)
            gu[:, lanes] = gun[cc, i : i + 2].reshape(384, 64).T
    wire.arrived(att.at[:, pl.ds(mine, HALF)], e0 + 14)
    keep_att.wait()
    wire.copy(bs.at[0], bs.at[0], sib, b0 + 12, b0 + 12).wait_send()
    wire.drain()


def distances():
    qp = np.arange(256)
    kp = np.arange(2304)
    kr = (kp // 768) * 16 + (kp % 256) // 16 - 16
    kc = (kp // 256 % 3) * 16 + kp % 16 - 16
    dr = kr[None] - (qp // 16)[:, None]
    dc = kc[None] - (qp % 16)[:, None]
    return (dr * dr + dc * dc).astype(np.float32)


def fused(*args):
    vm = pl.BlockSpec(memory_space=pltpu.VMEM)
    hb = pl.BlockSpec(memory_space=pl.ANY)
    return pl.pallas_call(
        kernel,
        out_shape=[
            jax.ShapeDtypeStruct((256, 1536), BF),
            jax.ShapeDtypeStruct((12, 64), F32),
            jax.ShapeDtypeStruct((64, 1536), F32),
        ],
        in_specs=[pl.BlockSpec(memory_space=pltpu.SMEM)] * 2 + [hb] * 4 + [vm] * 4,
        out_specs=[hb, vm, vm],
        scratch_shapes=[
            pltpu.VMEM((2, 256, HALF), BF),
            pltpu.VMEM((12, 256, HALF), BF),
            pltpu.VMEM((2, 256, HALF), BF),
            pltpu.VMEM((12, 256, 128), BF),
            pltpu.VMEM((2, 256, 3072), BF),
            pltpu.VMEM((4, 2, 2, 2, 96, HALF), BF),
            pltpu.VMEM((2, 8, 2304), F32),
            pltpu.VMEM((16, 16, HALF), BF),
            pltpu.VMEM((2, 96, HALF), BF),
            pltpu.VMEM((256, 128), BF),
            pltpu.VMEM((16, 1536), BF),
            pltpu.VMEM((2, 4, 4, 48, 64), F32),
            pltpu.VMEM((12, 256, HALF), BF),
            pltpu.VMEM((256, 2304), F32),
            pltpu.VMEM((12, 256, 2304), BF),
            pltpu.VMEM((12, 64, 256), F32),
            pltpu.VMEM((HALF, 128), F32),
            pltpu.VMEM((2, 256, HALF), BF),
            pltpu.VMEM((12, 64, 256), BF),
            pltpu.VMEM((12, 64, 256), BF),
            pltpu.VMEM((2, 4, 4, 96, 64), BF),
            pltpu.VMEM((4, 4, 96, 64), BF),
            pltpu.VMEM((2, 4, 4, 96, 64), F32),
            pltpu.VMEM((4, 4, 48, 64), BF),
            pltpu.VMEM((3, 4, 48, 64), BF),
            pltpu.VMEM((4, 48, 64), F32),
            pltpu.VMEM((4, 48, 64), BF),
            pltpu.VMEM((3, 48, 64), BF),
            pltpu.VMEM((48, 64), BF),
            pltpu.VMEM((8, 48, 64), BF),
            pltpu.VMEM((4, 4, 96, 64), BF),
            pltpu.VMEM((3, 4, 96, 64), BF),
            pltpu.VMEM((4, 96, 64), BF),
            pltpu.VMEM((3, 96, 64), BF),
            pltpu.VMEM((8, 16, 64), BF),
            pltpu.VMEM((7, 16, 64), BF),
            pltpu.SemaphoreType.DMA((136,)),
            pltpu.SemaphoreType.DMA((136,)),
            pltpu.SemaphoreType.DMA((8,)),
        ],
        compiler_params=pltpu.CompilerParams(
            collective_id=0, has_side_effects=True, vmem_limit_bytes=60 * MIB
        ),
        name="fused",
    )(*args)


def per_device(
    patch_tokens,
    queries,
    key_vectors,
    cotangent,
    value_weight,
    adapter_down,
    adapter_up,
    radius,
    tile_mask,
):
    att, gd, gu = fused(
        radius,
        tile_mask,
        queries.reshape(256, 1536),
        key_vectors.reshape(256, 1536),
        cotangent.reshape(256, 1536),
        patch_tokens.reshape(256, 3072),
        value_weight,
        adapter_down.T,
        adapter_up,
        jnp.asarray(distances()),
    )
    return att.reshape(16, 16, 1536), gd, gu


def solution(mesh):
    placed = (
        P("row", "col", None),
        P("row", "col", None),
        P("row", "col", None),
        P("row", "col", None),
        P(("row", "col"), None),
        P(),
        P(),
        P(),
        P("row", "col", None),
    )
    return jax.shard_map(
        per_device,
        mesh=mesh,
        in_specs=placed,
        out_specs=(P("row", "col", None), P(("row", "col"), None), P()),
        check_vma=False,
    )
```

```python
import jax
import jax.numpy as jnp
import numpy as np
from jax import lax
from jax.experimental import pallas as pl
from jax.experimental.pallas import tpu as pltpu
from jax.sharding import PartitionSpec as P

MESH = pl.DeviceIdType.MESH
BF = jnp.bfloat16
F32 = jnp.float32
HALF = 768
MIB = 2**20


def place():
    row = lax.axis_index("row")
    col = lax.axis_index("col")
    return row, col


def grid_place():
    row, col = place()
    y = lax.div(row, 4)
    x = lax.rem(lax.div(row, 2), 2) * 2 + lax.div(col, 8)
    return y, x, lax.rem(col, 8), lax.rem(row, 2)


def at_grid(y, x, z, c):
    y = lax.rem(y + 4, 4)
    x = lax.rem(x + 4, 4)
    z = lax.rem(z + 8, 8)
    return (y * 4 + lax.div(x, 2) * 2 + c, lax.rem(x, 2) * 8 + z)


def at_chip(k, h, col):
    return (lax.rem(k + 8, 8) * 2 + h, lax.rem(col + 16, 16))


def greet(targets):
    barrier = pltpu.get_barrier_semaphore()
    for target in targets:
        pl.semaphore_signal(barrier, inc=1, device_id=target, device_id_type=MESH)
    pl.semaphore_wait(barrier, len(targets))


class Wire:
    def __init__(self, send, recv):
        self.send, self.recv, self.pending = send, recv, []

    def copy(self, src, dst, target, s, r):
        return pltpu.make_async_remote_copy(
            src_ref=src,
            dst_ref=dst,
            send_sem=self.send.at[s],
            recv_sem=self.recv.at[r],
            device_id=target,
            device_id_type=MESH,
        )

    def start(self, src, dst, target, s, r):
        copy = self.copy(src, dst, target, s, r)
        copy.start()
        self.pending.append(copy)

    def arrived(self, dst, r):
        row, col = place()
        self.copy(dst, dst, (row + 1 - 2 * lax.rem(row, 2), col), r, r).wait_recv()

    def drain(self):
        for copy in self.pending:
            copy.wait_send()
        self.pending = []


def chip_targets():
    row, col = place()
    k, c = lax.div(row, 2), lax.rem(row, 2)
    out = [at_chip(k, 1 - c, col)]
    for h in (0, 1):
        out += [at_chip(k + 1, h, col), at_chip(k - 1, h, col)]
        out += [at_chip(k, h, col + 1), at_chip(k, h, col - 1)]
    return out


def stretch(c):
    return pl.multiple_of(c * HALF, HALF)


def kernel(
    radius, mask, q, kv, cot, x, w, down, up, dist,
    att, gd, gu,
    q2, kwin, c2, lwin, x2, wout, allow2, zbuf, wblk, low, wp, gun,
    vwin, s_one, s_two, p_ref, back, upt, att2,
    bs, br, gs, gr, keep, ux, uxr, ukeep, uy, uyr, uz, uzr, gx, gxr, gy, gyr, gz, gzr,
    send, recv, local,
):
    row, col = place()
    k, c = lax.div(row, 2), lax.rem(row, 2)
    y, xx, z, _ = grid_place()
    other = 1 - c
    mine = stretch(c)
    wire = Wire(send, recv)
    targets = chip_targets()
    for a in range(1, 8):
        targets += [at_grid(y, xx, z + a, 0), at_grid(y, xx, z + a, 1)]
    xt = [at_grid(y, xx + a, z, c) for a in (1, 2, 3)]
    yt = [at_grid(y + a, xx, z, c) for a in (1, 2, 3)]
    zt = [at_grid(y, xx, z + a, c) for a in range(1, 8)]
    targets += xt + yt
    targets += [at_chip(k, h, col + d) for d in (7, 8, 9) for h in (0, 1)]
    for h in (0, 1):
        for d in (1, -1):
            targets += [at_chip(k + 1, h, col + d), at_chip(k - 1, h, col + d)]
    sib = at_chip(k, other, col)
    theirs = stretch(other)

    locals_ = []

    def local_copy(src, dst):
        copy = pltpu.make_async_copy(src, dst, local.at[len(locals_)])
        copy.start()
        locals_.append(copy)
        return copy

    slot = c * 8 + z
    centre = (1 + c) * 3 + 1
    own_x = local_copy(x, x2.at[c])
    local_copy(kv.at[:, pl.ds(mine, HALF)], kwin.at[centre])
    local_copy(q.at[:, pl.ds(mine, HALF)], q2.at[c])
    local_copy(cot.at[:, pl.ds(mine, HALF)], c2.at[c])
    for n in range(9):
        r, t = row + n // 3 - 1, col + n % 3 - 1
        seen = (r >= 0) & (r < 16) & (t >= 0) & (t < 16) & (mask[0, 0, n] > 0)
        allow2[c, :, n * 256 : (n + 1) * 256] = jnp.full((8, 256), jnp.where(seen, 1.0, 0.0))
    r_out = lax.broadcasted_iota(jnp.int32, (16, 12), 0)
    r_in = lax.broadcasted_iota(jnp.int32, (16, 12), 1)
    wp[...] = jnp.dot(
        jnp.where(r_out == r_in, 1.0, 0.0).astype(BF), w[...], preferred_element_type=F32
    ).astype(BF)
    local_copy(wp.at[:, pl.ds(mine, HALF)], zbuf.at[slot])
    greet(targets)

    wire.start(wp.at[:, pl.ds(theirs, HALF)], zbuf.at[slot], sib, 0, 0)
    for a in range(1, 8):
        for h in (0, 1):
            hh = c if h == 0 else other
            wire.start(
                wp.at[:, pl.ds(stretch(hh), HALF)],
                zbuf.at[slot],
                at_grid(y, xx, z + a, hh),
                2 * a + h,
                2 * a + h,
            )
    far = (3 - 3 * c) * 3 + 1
    step = 2 * c - 1

    crossing = ((0, 1, 7, 15), (1, -1, 8, 0))

    def side_sends(parts, win, rr, n, which, far_ones):
        for h, target_core, src in parts:
            for i, d, hop, relay in crossing:
                spot, near = win.at[rr * 3 + 1 - d], win.at[rr * 3 + 1 + d]

                if False in far_ones:

                    @pl.when((col != hop) & (col != relay))
                    def _(h=h, i=i, d=d, src=src, target_core=target_core, spot=spot):
                        target = at_chip(k, target_core, col + d)
                        wire.copy(src, spot, target, n + 2 * i + h, n + 2 * i + which).start()

                if True in far_ones:

                    @pl.when(col == hop)
                    def _(h=h, i=i, src=src, target_core=target_core, near=near, relay=relay):
                        target = at_chip(k, target_core, jnp.int32(relay))
                        m = n + 2 * (1 - i) + which
                        wire.copy(src, near, target, n + 2 * i + h, m).start()

    def side_relay(win, n):
        for i, d, hop, relay in crossing:

            @pl.when(col == relay)
            def _(i=i, d=d, hop=hop):
                for t in (0, 1):
                    spot, near = win.at[(1 + t) * 3 + 1 - d], win.at[(1 + t) * 3 + 1 + d]
                    wire.arrived(near, n + 2 * (1 - i) + t)
                    m = n + 2 * i + t
                    wire.copy(near, spot, (row, jnp.int32(hop + d)), m, m).start()

    def side_arrivals(win, n):
        for i, edge in enumerate((0, 15)):

            @pl.when(col != edge)
            def _(i=i):
                wire.arrived(win.at[0], n + 2 * i)
                wire.arrived(win.at[0], n + 2 * i + 1)

        for m in range(4):
            wire.copy(win.at[0], win.at[0], sib, n + m, n + m).wait_send()

    def clear_edges(win):
        for edge, cc in ((0, 0), (15, 2)):

            @pl.when(col == edge)
            def _(cc=cc):
                for rr in (0, 3):
                    win[rr * 3 + cc] = jnp.zeros(win.shape[1:], win.dtype)

    def corner(win, m, rr):
        src = win.at[rr * 3 + 1]
        for i, d, _, edge in crossing:

            @pl.when(col != edge)
            def _(i=i, d=d):
                n = m + (2 if rr else 0) + i
                wire.copy(src, win.at[rr * 3 + 1 - d], at_chip(k, c, col + d), n, n).start()

    def corner_arrivals(win, m):
        for n in (m, m + 2):
            for i, edge in enumerate((0, 15)):

                @pl.when(col != edge)
                def _(n=n, i=i):
                    wire.arrived(win.at[0], n + i)

                @pl.when(col != 15 - edge)
                def _(n=n, i=i):
                    wire.copy(win.at[0], win.at[0], sib, n + i, n + i).wait_send()

    def halves(src, split):
        return [src.at[:, pl.ds(h * HALF, HALF)] if split else src for h in (0, 1)]

    def tile_up(src, win, n, split, by):
        for h, part in enumerate(halves(src, split)):
            by.start(part, win.at[far], at_chip(k + step, h, col), n + h, n + c)

    def tile_sides(src, win, n, split, far_ones):
        parts = [(h, h, part) for h, part in enumerate(halves(src, split))]
        side_sends(parts, win, 1 + c, n, c, far_ones)

    for win in (kwin, lwin, vwin):
        clear_edges(win)
    tile_up(kv, kwin, 16, True, wire)
    wire.start(kv.at[:, pl.ds(theirs, HALF)], kwin.at[centre], sib, 22, 22)
    wire.start(q.at[:, pl.ds(theirs, HALF)], q2.at[c], sib, 30, 30)
    wire.start(cot.at[:, pl.ds(theirs, HALF)], c2.at[c], sib, 31, 31)
    wire.start(x, x2.at[c], sib, 32, 32)
    wire.start(allow2.at[c], allow2.at[c], sib, 33, 33)
    own_x.wait()
    low[:, 0:64] = lax.dot_general(
        x2[c], down[...], (((1,), (1,)), ((), ())), preferred_element_type=F32
    ).astype(BF)
    low[:, 64:128] = jnp.zeros((256, 64), BF)
    lwin[centre] = low[...]
    wire.start(low, lwin.at[centre], sib, 29, 29)

    locals_.pop().wait()
    wire.arrived(zbuf.at[0], 0)
    for a in range(1, 8):
        for h in (0, 1):
            wire.arrived(zbuf.at[0], 2 * a + h)
    r_out = lax.broadcasted_iota(jnp.int32, (96, 128), 0)
    r_in = lax.broadcasted_iota(jnp.int32, (96, 128), 1)
    pick = jnp.where(lax.div(r_out, 12) * 16 + lax.rem(r_out, 12) == r_in, 1.0, 0.0).astype(BF)
    for cc in (0, 1):
        part = zbuf[pl.ds(cc * 8, 8)].reshape(128, HALF)
        wblk[cc] = jnp.dot(pick, part, preferred_element_type=F32).astype(BF)

    xs = (at_grid(y, xx + 1, z, c), at_grid(y, xx - 1, z, c))
    ys = (at_grid(y + 1, xx, z, c), at_grid(y - 1, xx, z, c))

    def x_part(i):
        i = lax.rem(i + 4, 4)
        return lax.div(i, 2), lax.rem(i, 2)

    def y_part(i):
        return lax.rem(i + 4, 4)

    def small(yi, xi):
        a, b = x_part(xi)
        return wout.at[y_part(yi), a, :, b]

    def small_half(yi, xi, j):
        a, b = x_part(xi)
        return wout.at[y_part(yi), a, j, b]

    own_copy = pltpu.make_async_copy(wblk, small(y, xx), local.at[7])
    own_copy.start()

    def corners(win, n, m):
        for rr, first in ((0, n + 1), (3, n)):
            wire.arrived(win.at[rr * 3 + 1], first)
            corner(win, m, rr)

    def spread(along_x):
        sub = Wire(send, recv)
        w0 = 34
        if along_x:
            one, two = xs, ys
            full = lambda a, b: small(y + b, xx + a)
            half = lambda a, b, j: small_half(y + b, xx + a, j)
        else:
            one, two = ys, xs
            full = lambda a, b: small(y + a, xx + b)
            half = lambda a, b, j: small_half(y + a, xx + b, j)
        at = (0, -1, 1, 2)

        def across(n, src):
            for i in (0, 1):
                sub.start(src, full(at[n], 0), two[i], w0 + 4 + 2 * n + i, w0 + 4 + 2 * n + i)

        def pass_on(n):
            for i, d in enumerate((-1, 1)):
                sub.arrived(full(at[n], d), w0 + 4 + 2 * n + i)
                m = w0 + 12 + 2 * n + i
                sub.start(half(at[n], d, i), half(at[n], d, i), two[i], m, m)

        for i in (0, 1):
            sub.start(wblk, full(0, 0), one[i], w0 + i, w0 + i)
        across(0, wblk)
        tile_sides(kv, kwin, 18, True, (False,))
        for i, d in enumerate((-1, 1)):
            sub.arrived(full(d, 0), w0 + i)
            sub.start(half(d, 0, i), half(d, 0, i), one[i], w0 + 2 + i, w0 + 2 + i)
            across(1 + i, full(d, 0))
        tile_sides(kv, kwin, 18, True, (True,))
        corners(kwin, 16, 70)
        pass_on(0)
        for i in (0, 1):
            sub.arrived(half(2, 0, i), w0 + 2 + i)
        across(3, full(2, 0))
        tile_up(low, lwin, 23, False, sub)
        tile_sides(low, lwin, 25, False, (True, False))
        pass_on(1)
        pass_on(2)
        pass_on(3)
        for n in range(4):
            for i in (0, 1):
                sub.arrived(half(0, 2, i), w0 + 12 + 2 * n + i)
        own_copy.wait()
        sub.drain()

    busy = lax.rem(z + 1, 8) < 2

    @pl.when((c == 0) | busy)
    def _():
        spread(True)

    @pl.when((c == 1) & jnp.logical_not(busy))
    def _():
        spread(False)

    def heads(start, width):
        return pl.ds(pl.multiple_of(mine + start, 128), width)

    wire.arrived(x2.at[0], 32)
    wire.arrived(lwin.at[0], 29)
    low2 = jnp.concatenate([lwin[4][:, :64], lwin[7][:, :64]], axis=0)

    @pl.loop(0, 3)
    def _(n):
        lanes = pl.ds(pl.multiple_of(n * 256, 256), 256)
        acc = jnp.dot(low2, up[:, heads(n * 256, 256)], preferred_element_type=F32)
        for yi in range(4):
            rows = wout[yi, :, :, :, :, lanes].reshape(768, 256)
            part = x2[:, :, yi * 768 : (yi + 1) * 768].reshape(512, 768)
            acc = acc + jnp.dot(part, rows, preferred_element_type=F32)
        acc = acc.astype(BF)
        vwin[4, :, lanes] = acc[:256]
        vwin[7, :, lanes] = acc[256:]

    v0 = 54
    wire.start(vwin.at[4], vwin.at[10], at_chip(k - 1, c, col), v0, v0)
    wire.start(vwin.at[7], vwin.at[1], at_chip(k + 1, c, col), v0 + 1, v0 + 1)
    for t in (0, 1):
        side_sends([(t, c, vwin.at[4 + 3 * t])], vwin, 1 + t, v0 + 2, t, (True, False))

    side_relay(kwin, 18)
    corners(lwin, 23, 74)
    side_relay(lwin, 25)

    side_arrivals(kwin, 18)
    side_arrivals(lwin, 25)
    wire.arrived(kwin.at[0], 22)
    wire.arrived(q2.at[0], 30)
    wire.arrived(c2.at[0], 31)
    wire.arrived(allow2.at[0], 33)
    corner_arrivals(kwin, 70)
    corner_arrivals(lwin, 74)
    for copy in locals_[1:]:
        copy.wait()

    back[...] = jnp.zeros_like(back)
    upt[...] = jnp.zeros_like(upt)

    def place_of(i):
        h, t = lax.div(i, 2), lax.rem(i, 2)
        return h, t, pl.ds(pl.multiple_of(h * 128, 128), 128)

    def score(i, to):
        h, t, lanes = place_of(i)
        keys = kwin[pl.ds(t * 3, 9), :, lanes].reshape(2304, 128)
        to[...] = lax.dot_general(
            q2[t, :, lanes], keys, (((1,), (1,)), ((), ())), preferred_element_type=F32
        )

    log_scale = 128**-0.5 * 1.4426950408889634

    def soften(i, s_ref):
        h, t, _ = place_of(i)
        reach = radius[c * 6 + h]
        limit = allow2[t, 0:1, :] * (reach * reach + 1).astype(F32) - 1.0
        for j in range(8):
            rows = slice(j * 32, (j + 1) * 32)
            s = jnp.where(dist[rows] <= limit, s_ref[rows], -1e30)
            e = jnp.exp2((s - jnp.max(s, axis=1, keepdims=True)) * log_scale)
            p_ref[i, rows] = (e * (1.0 / jnp.sum(e, axis=1, keepdims=True))).astype(BF)

    def gradient(i):
        h, t, lanes = place_of(i)
        vgt = jnp.dot(c2[t, :, lanes].T, p_ref[i], preferred_element_type=F32).astype(BF)
        bt = jnp.dot(up[:, heads(h * 128, 128)], vgt, preferred_element_type=F32)
        for n in range(9):
            back[t * 3 + n] += bt[:, n * 256 : (n + 1) * 256]
        lows = lwin[pl.ds(t * 3, 9)].reshape(2304, 128)
        upt[lanes] += jnp.dot(vgt, lows, preferred_element_type=F32)

    def probs(lo, hi):
        @pl.loop(lo, hi)
        def _(m):
            score(2 * m, s_one)
            score(2 * m + 1, s_two)
            soften(2 * m, s_one)
            soften(2 * m + 1, s_two)
            gradient(2 * m)
            gradient(2 * m + 1)

    def attend(lo, hi):
        for i in range(lo, hi):
            h, t = i // 2, i % 2
            lanes = slice(h * 128, (h + 1) * 128)
            vals = vwin[t * 3 : t * 3 + 9, :, lanes].reshape(2304, 128)
            att2[t, :, lanes] = jnp.dot(p_ref[i], vals, preferred_element_type=F32).astype(BF)

    probs(0, 4)
    wire.arrived(vwin.at[10], v0)
    corner(vwin, 60, 3)
    wire.arrived(vwin.at[1], v0 + 1)
    corner(vwin, 60, 0)
    probs(4, 6)
    side_relay(vwin, v0 + 2)

    def values_here():
        side_arrivals(vwin, v0 + 2)
        corner_arrivals(vwin, 60)

    b0 = 78
    for n in range(12):
        rr, cc = n // 3, n % 3
        bs[n] = back[n].astype(BF)
        dk, h = ((-1, 1), (0, 0), (0, 1), (1, 0))[rr]
        slot = (0 if rr in (1, 2) else 6) + cc * 2
        if n in (4, 7):

            @pl.when(c != h)
            def _():
                wire.copy(bs.at[n], br.at[slot + c], sib, b0 + 12, b0 + slot + c).start()
        else:
            target = at_chip(k + dk, h, col + cc - 1)
            wire.start(bs.at[n], br.at[slot + c], target, b0 + n, b0 + slot + c)

    u0, e0 = 92, 116
    for a in range(4):
        for b in range(4):
            ux[a, b] = upt[(a * 4 + b) * 48 : (a * 4 + b + 1) * 48, 0:64].astype(BF)
    for i in range(3):
        wire.start(ux.at[lax.rem(xx + i + 1, 4)], uxr.at[i], xt[i], u0 + i, u0 + i)

    total = back[(1 + c) * 3 + 1]
    wire.arrived(br.at[0], b0 + 2 + other)
    total = total + br[2 + other].astype(F32)
    for slot in range(12):
        if slot not in (2, 3):
            wire.arrived(br.at[0], b0 + slot)
            total = total + br[slot].astype(F32)
    hi = total.astype(BF)
    lo = (total - hi.astype(F32)).astype(BF)
    both = jnp.concatenate([hi, lo], axis=0)

    for i in range(3):
        wire.arrived(uxr.at[0], u0 + i)
    for b in range(4):
        ua = upt[pl.ds(pl.multiple_of((xx * 4 + b) * 48, 16), 48), 0:64]
        for i in range(3):
            ua = ua + uxr[i, b].astype(F32)
        ukeep[b] = ua
        uy[b] = ua.astype(BF)
    for i in range(3):
        wire.start(uy.at[lax.rem(y + i + 1, 4)], uyr.at[i], yt[i], u0 + 3 + i, u0 + 3 + i)

    @pl.loop(0, 8)
    def _(i):
        part = x2[c, :, pl.ds(pl.multiple_of(i * 384, 384), 384)]
        g = jnp.dot(both, part, preferred_element_type=F32)
        g = (g[:64] + g[64:]).T
        yi, xhi = lax.div(i, 2), lax.rem(i, 2)
        for cc in (0, 1):
            for xl in (0, 1):
                rows = g[(cc * 2 + xl) * 96 : (cc * 2 + xl + 1) * 96]
                keep[cc, xhi * 2 + xl, yi] = rows
                gs[cc, xhi * 2 + xl, yi] = rows.astype(BF)

    wire.start(gs.at[other], gr, sib, e0, e0)

    for i in range(3):
        wire.arrived(uyr.at[0], u0 + 3 + i)
    ua = ukeep[y]
    for i in range(3):
        ua = ua + uyr[i].astype(F32)
    uz[...] = ua.astype(BF)
    uzr[z] = ua.astype(BF)
    for i in range(7):
        wire.start(uz, uzr.at[z], zt[i], u0 + 6 + i, u0 + 6 + i)

    wire.arrived(gr, e0)
    for a in range(4):
        for b in range(4):
            full = keep[c, a, b] + gr[a, b].astype(F32)
            keep[0, a, b] = full
            gx[a, b] = full.astype(BF)
    for i in range(3):
        wire.start(gx.at[lax.rem(xx + i + 1, 4)], gxr.at[i], xt[i], e0 + 1 + i, e0 + 1 + i)

    scale = 65536**-0.5
    for i in range(7):
        wire.arrived(uz, u0 + 6 + i)
    ua = uzr[0].astype(F32)
    for i in range(1, 8):
        ua = ua + uzr[i].astype(F32)
    gun[c, xx, y] = ua * scale
    spot = gun.at[c, xx, y]
    for i in range(3):
        wire.start(spot, spot, yt[i], u0 + 13 + i, u0 + 13 + i)

    for i in range(3):
        wire.arrived(gxr.at[0], e0 + 1 + i)
    for b in range(4):
        acc = keep[0, xx, b]
        for i in range(3):
            acc = acc + gxr[i, b].astype(F32)
        keep[1, 0, b] = acc
        gy[b] = acc.astype(BF)
    for i in range(3):
        wire.start(gy.at[lax.rem(y + i + 1, 4)], gyr.at[i], yt[i], e0 + 4 + i, e0 + 4 + i)

    for i in range(3):
        wire.arrived(spot, u0 + 13 + i)
    for i in range(3):
        wire.start(gun.at[c, xx], gun.at[c, xx], xt[i], u0 + 16 + i, u0 + 16 + i)

    values_here()
    attend(0, 6)

    for i in range(3):
        wire.arrived(gyr.at[0], e0 + 4 + i)
    acc = keep[1, 0, y]
    for i in range(3):
        acc = acc + gyr[i].astype(F32)
    r_out = lax.broadcasted_iota(jnp.int32, (128, 96), 0)
    r_in = lax.broadcasted_iota(jnp.int32, (128, 96), 1)
    row_of = lax.div(r_out, 16) * 12 + lax.rem(r_out, 16)
    pick = jnp.where((row_of == r_in) & (lax.rem(r_out, 16) < 12), 1.0, 0.0).astype(BF)
    parts = jnp.dot(pick, acc.astype(BF), preferred_element_type=F32).astype(BF)
    for i in range(8):
        gz[i] = parts[i * 16 : (i + 1) * 16]
    for i in range(7):
        wire.start(gz.at[lax.rem(z + i + 1, 8)], gzr.at[i], zt[i], e0 + 7 + i, e0 + 7 + i)

    for i in range(3):
        wire.arrived(gun.at[c, xx], u0 + 16 + i)
    wire.start(gun.at[c], gun.at[c], sib, u0 + 19, u0 + 19)

    attend(6, 12)
    wire.start(att2.at[other], att.at[:, pl.ds(mine, HALF)], sib, e0 + 14, e0 + 14)
    keep_att = pltpu.make_async_copy(att2.at[c], att.at[:, pl.ds(mine, HALF)], local.at[6])
    keep_att.start()

    for i in range(7):
        wire.arrived(gzr.at[0], e0 + 7 + i)
    acc = gz[z].astype(F32)
    for i in range(7):
        acc = acc + gzr[i].astype(F32)
    gd[...] = (acc * scale)[0:12]
    wire.arrived(gun.at[c], u0 + 19)
    for cc in (0, 1):
        for i in (0, 2):
            lanes = pl.ds(cc * HALF + i * 192, 384)
            gu[:, lanes] = gun[cc, i : i + 2].reshape(384, 64).T
    wire.arrived(att.at[:, pl.ds(mine, HALF)], e0 + 14)
    keep_att.wait()
    wire.copy(bs.at[0], bs.at[0], sib, b0 + 12, b0 + 12).wait_send()
    wire.drain()


def distances():
    qp = np.arange(256)
    kp = np.arange(2304)
    kr = (kp // 768) * 16 + (kp % 256) // 16 - 16
    kc = (kp // 256 % 3) * 16 + kp % 16 - 16
    dr = kr[None] - (qp // 16)[:, None]
    dc = kc[None] - (qp % 16)[:, None]
    return (dr * dr + dc * dc).astype(np.float32)


def fused(*args):
    vm = pl.BlockSpec(memory_space=pltpu.VMEM)
    hb = pl.BlockSpec(memory_space=pl.ANY)
    return pl.pallas_call(
        kernel,
        out_shape=[
            jax.ShapeDtypeStruct((256, 1536), BF),
            jax.ShapeDtypeStruct((12, 64), F32),
            jax.ShapeDtypeStruct((64, 1536), F32),
        ],
        in_specs=[pl.BlockSpec(memory_space=pltpu.SMEM)] * 2 + [hb] * 4 + [vm] * 4,
        out_specs=[hb, vm, vm],
        scratch_shapes=[
            pltpu.VMEM((2, 256, HALF), BF),
            pltpu.VMEM((12, 256, HALF), BF),
            pltpu.VMEM((2, 256, HALF), BF),
            pltpu.VMEM((12, 256, 128), BF),
            pltpu.VMEM((2, 256, 3072), BF),
            pltpu.VMEM((4, 2, 2, 2, 96, HALF), BF),
            pltpu.VMEM((2, 8, 2304), F32),
            pltpu.VMEM((16, 16, HALF), BF),
            pltpu.VMEM((2, 96, HALF), BF),
            pltpu.VMEM((256, 128), BF),
            pltpu.VMEM((16, 1536), BF),
            pltpu.VMEM((2, 4, 4, 48, 64), F32),
            pltpu.VMEM((12, 256, HALF), BF),
            pltpu.VMEM((256, 2304), F32),
            pltpu.VMEM((256, 2304), F32),
            pltpu.VMEM((12, 256, 2304), BF),
            pltpu.VMEM((12, 64, 256), F32),
            pltpu.VMEM((HALF, 128), F32),
            pltpu.VMEM((2, 256, HALF), BF),
            pltpu.VMEM((12, 64, 256), BF),
            pltpu.VMEM((12, 64, 256), BF),
            pltpu.VMEM((2, 4, 4, 96, 64), BF),
            pltpu.VMEM((4, 4, 96, 64), BF),
            pltpu.VMEM((2, 4, 4, 96, 64), F32),
            pltpu.VMEM((4, 4, 48, 64), BF),
            pltpu.VMEM((3, 4, 48, 64), BF),
            pltpu.VMEM((4, 48, 64), F32),
            pltpu.VMEM((4, 48, 64), BF),
            pltpu.VMEM((3, 48, 64), BF),
            pltpu.VMEM((48, 64), BF),
            pltpu.VMEM((8, 48, 64), BF),
            pltpu.VMEM((4, 4, 96, 64), BF),
            pltpu.VMEM((3, 4, 96, 64), BF),
            pltpu.VMEM((4, 96, 64), BF),
            pltpu.VMEM((3, 96, 64), BF),
            pltpu.VMEM((8, 16, 64), BF),
            pltpu.VMEM((7, 16, 64), BF),
            pltpu.SemaphoreType.DMA((136,)),
            pltpu.SemaphoreType.DMA((136,)),
            pltpu.SemaphoreType.DMA((8,)),
        ],
        compiler_params=pltpu.CompilerParams(
            collective_id=0, has_side_effects=True, vmem_limit_bytes=60 * MIB
        ),
        name="fused",
    )(*args)


def per_device(
    patch_tokens,
    queries,
    key_vectors,
    cotangent,
    value_weight,
    adapter_down,
    adapter_up,
    radius,
    tile_mask,
):
    att, gd, gu = fused(
        radius,
        tile_mask,
        queries.reshape(256, 1536),
        key_vectors.reshape(256, 1536),
        cotangent.reshape(256, 1536),
        patch_tokens.reshape(256, 3072),
        value_weight,
        adapter_down.T,
        adapter_up,
        jnp.asarray(distances()),
    )
    return att.reshape(16, 16, 1536), gd, gu


def solution(mesh):
    placed = (
        P("row", "col", None),
        P("row", "col", None),
        P("row", "col", None),
        P("row", "col", None),
        P(("row", "col"), None),
        P(),
        P(),
        P(),
        P("row", "col", None),
    )
    return jax.shard_map(
        per_device,
        mesh=mesh,
        in_specs=placed,
        out_specs=(P("row", "col", None), P(("row", "col"), None), P()),
        check_vma=False,
    )
```

```python
import jax
import jax.numpy as jnp
import numpy as np
from jax import lax
from jax.experimental import pallas as pl
from jax.experimental.pallas import tpu as pltpu
from jax.sharding import PartitionSpec as P

MESH = pl.DeviceIdType.MESH
BF = jnp.bfloat16
F32 = jnp.float32
HALF = 768
WIDE = 896
MIB = 2**20


def place():
    row = lax.axis_index("row")
    col = lax.axis_index("col")
    return row, col


def grid_place():
    row, col = place()
    y = lax.div(row, 4)
    x = lax.rem(lax.div(row, 2), 2) * 2 + lax.div(col, 8)
    return y, x, lax.rem(col, 8), lax.rem(row, 2)


def at_grid(y, x, z, c):
    y = lax.rem(y + 4, 4)
    x = lax.rem(x + 4, 4)
    z = lax.rem(z + 8, 8)
    return (y * 4 + lax.div(x, 2) * 2 + c, lax.rem(x, 2) * 8 + z)


def at_chip(k, h, col):
    return (lax.rem(k + 8, 8) * 2 + h, lax.rem(col + 16, 16))


def greet(targets):
    barrier = pltpu.get_barrier_semaphore()
    for target in targets:
        pl.semaphore_signal(barrier, inc=1, device_id=target, device_id_type=MESH)
    return lambda: pl.semaphore_wait(barrier, len(targets))


class Wire:
    def __init__(self, send, recv):
        self.send, self.recv, self.pending = send, recv, []

    def copy(self, src, dst, target, s, r):
        return pltpu.make_async_remote_copy(
            src_ref=src,
            dst_ref=dst,
            send_sem=self.send.at[s],
            recv_sem=self.recv.at[r],
            device_id=target,
            device_id_type=MESH,
        )

    def start(self, src, dst, target, s, r):
        copy = self.copy(src, dst, target, s, r)
        copy.start()
        self.pending.append(copy)

    def arrived(self, dst, r):
        row, col = place()
        self.copy(dst, dst, (row + 1 - 2 * lax.rem(row, 2), col), r, r).wait_recv()

    def drain(self):
        for copy in self.pending:
            copy.wait_send()
        self.pending = []


def chip_targets():
    row, col = place()
    k, c = lax.div(row, 2), lax.rem(row, 2)
    out = [at_chip(k, 1 - c, col)]
    for h in (0, 1):
        out += [at_chip(k + 1, h, col), at_chip(k - 1, h, col)]
        out += [at_chip(k, h, col + 1), at_chip(k, h, col - 1)]
    return out


def stretch(c):
    return pl.multiple_of(c * HALF, HALF)


def kernel(
    radius, mask, q, kv, cot, x, w, down, up, dist,
    att, gd, gu,
    q2, kwin, c2, keys_out, x2, wout, allow2, zbuf, wblk, wp, gun,
    vwin, s_one, s_two, p_ref, back, upt, att2,
    bs, br, gs, gr, keep, ux, uxr, ukeep, uy, uyr, uz, uzr, gx, gxr, gy, gyr, gz, gzr,
    send, recv, local,
):
    row, col = place()
    k, c = lax.div(row, 2), lax.rem(row, 2)
    y, xx, z, _ = grid_place()
    other = 1 - c
    mine = stretch(c)
    wire = Wire(send, recv)
    targets = chip_targets()
    for a in range(1, 8):
        targets += [at_grid(y, xx, z + a, 0), at_grid(y, xx, z + a, 1)]
    xt = [at_grid(y, xx + a, z, c) for a in (1, 2, 3)]
    yt = [at_grid(y + a, xx, z, c) for a in (1, 2, 3)]
    zt = [at_grid(y, xx, z + a, c) for a in range(1, 8)]
    targets += xt + yt
    targets += [at_chip(k, h, col + d) for d in (7, 8, 9) for h in (0, 1)]
    for h in (0, 1):
        for d in (1, -1):
            targets += [at_chip(k + 1, h, col + d), at_chip(k - 1, h, col + d)]
    sib = at_chip(k, other, col)
    theirs = stretch(other)

    locals_ = []

    def local_copy(src, dst):
        copy = pltpu.make_async_copy(src, dst, local.at[len(locals_)])
        copy.start()
        locals_.append(copy)
        return copy

    slot = c * 8 + z
    centre = (1 + c) * 3 + 1
    far = (3 - 3 * c) * 3 + 1
    step = 2 * c - 1

    crossing = ((0, 1, 7, 15), (1, -1, 8, 0))

    def side_sends(parts, win, rr, n, which):
        for h, target_core, src in parts:
            for i, d, hop, relay in crossing:
                spot, near = win.at[rr * 3 + 1 - d], win.at[rr * 3 + 1 + d]

                @pl.when((col != hop) & (col != relay))
                def _(h=h, i=i, d=d, src=src, target_core=target_core, spot=spot):
                    target = at_chip(k, target_core, col + d)
                    wire.copy(src, spot, target, n + 2 * i + h, n + 2 * i + which).start()

                @pl.when(col == hop)
                def _(h=h, i=i, src=src, target_core=target_core, near=near, relay=relay):
                    target = at_chip(k, target_core, jnp.int32(relay))
                    wire.copy(src, near, target, n + 2 * i + h, n + 2 * (1 - i) + which).start()

    def side_relay(win, n):
        for i, d, hop, relay in crossing:

            @pl.when(col == relay)
            def _(i=i, d=d, hop=hop):
                for t in (0, 1):
                    spot, near = win.at[(1 + t) * 3 + 1 - d], win.at[(1 + t) * 3 + 1 + d]
                    wire.arrived(near, n + 2 * (1 - i) + t)
                    m = n + 2 * i + t
                    wire.copy(near, spot, (row, jnp.int32(hop + d)), m, m).start()

    def side_arrivals(win, n):
        for i, edge in enumerate((0, 15)):

            @pl.when(col != edge)
            def _(i=i):
                wire.arrived(win.at[0], n + 2 * i)
                wire.arrived(win.at[0], n + 2 * i + 1)

        for m in range(4):
            wire.copy(win.at[0], win.at[0], sib, n + m, n + m).wait_send()

    def clear_edges(win):
        for edge, cc in ((0, 0), (15, 2)):

            @pl.when(col == edge)
            def _(cc=cc):
                for rr in (0, 3):
                    win[rr * 3 + cc] = jnp.zeros(win.shape[1:], win.dtype)

    def corner(win, m, rr):
        src = win.at[rr * 3 + 1]
        for i, d, _, edge in crossing:

            @pl.when(col != edge)
            def _(i=i, d=d):
                n = m + (2 if rr else 0) + i
                wire.copy(src, win.at[rr * 3 + 1 - d], at_chip(k, c, col + d), n, n).start()

    def corner_arrivals(win, m):
        for n in (m, m + 2):
            for i, edge in enumerate((0, 15)):

                @pl.when(col != edge)
                def _(n=n, i=i):
                    wire.arrived(win.at[0], n + i)

                @pl.when(col != 15 - edge)
                def _(n=n, i=i):
                    wire.copy(win.at[0], win.at[0], sib, n + i, n + i).wait_send()

    def keys_up():
        for h in (0, 1):
            wire.start(keys_out.at[h], kwin.at[far], at_chip(k + step, h, col), 16 + h, 16 + c)

    def keys_aside():
        parts = [(h, h, keys_out.at[h]) for h in (0, 1)]
        side_sends(parts, kwin, 1 + c, 18, c)

    met = greet(targets)
    own_x = local_copy(x, x2.at[c])
    own_k = local_copy(kv.at[:, pl.ds(mine, HALF)], kwin.at[centre, :, pl.ds(0, HALF)])
    for h in (0, 1):
        local_copy(kv.at[:, pl.ds(h * HALF, HALF)], keys_out.at[h, :, pl.ds(0, HALF)])
    local_copy(q.at[:, pl.ds(mine, HALF)], q2.at[c])
    local_copy(cot.at[:, pl.ds(mine, HALF)], c2.at[c])
    for n in range(9):
        r, t = row + n // 3 - 1, col + n % 3 - 1
        seen = (r >= 0) & (r < 16) & (t >= 0) & (t < 16) & (mask[0, 0, n] > 0)
        allow2[c, :, n * 256 : (n + 1) * 256] = jnp.full((8, 256), jnp.where(seen, 1.0, 0.0))
    r_out = lax.broadcasted_iota(jnp.int32, (16, 12), 0)
    r_in = lax.broadcasted_iota(jnp.int32, (16, 12), 1)
    wp[...] = jnp.dot(
        jnp.where(r_out == r_in, 1.0, 0.0).astype(BF), w[...], preferred_element_type=F32
    ).astype(BF)
    own_w = local_copy(wp.at[:, pl.ds(mine, HALF)], zbuf.at[slot])
    own_x.wait()
    low = lax.dot_general(
        x2[c], down[...], (((1,), (1,)), ((), ())), preferred_element_type=F32
    ).astype(BF)
    low = jnp.concatenate([low, jnp.zeros((256, 64), BF)], axis=1)
    for h in (0, 1):
        keys_out[h, :, HALF:WIDE] = low
    clear_edges(kwin)
    clear_edges(vwin)
    kwin[centre, :, HALF:WIDE] = low
    for copy in locals_[1:]:
        copy.wait()
    met()

    wire.start(wp.at[:, pl.ds(theirs, HALF)], zbuf.at[slot], sib, 0, 0)
    for a in range(1, 8):
        for h in (0, 1):
            hh = c if h == 0 else other
            wire.start(
                wp.at[:, pl.ds(stretch(hh), HALF)],
                zbuf.at[slot],
                at_grid(y, xx, z + a, hh),
                2 * a + h,
                2 * a + h,
            )
    keys_up()
    wire.start(keys_out.at[other], kwin.at[centre], sib, 22, 22)
    wire.start(q.at[:, pl.ds(theirs, HALF)], q2.at[c], sib, 30, 30)
    wire.start(cot.at[:, pl.ds(theirs, HALF)], c2.at[c], sib, 31, 31)
    wire.start(x, x2.at[c], sib, 32, 32)
    wire.start(allow2.at[c], allow2.at[c], sib, 33, 33)
    wire.arrived(zbuf.at[0], 0)
    for a in range(1, 8):
        for h in (0, 1):
            wire.arrived(zbuf.at[0], 2 * a + h)
    r_out = lax.broadcasted_iota(jnp.int32, (96, 128), 0)
    r_in = lax.broadcasted_iota(jnp.int32, (96, 128), 1)
    pick = jnp.where(lax.div(r_out, 12) * 16 + lax.rem(r_out, 12) == r_in, 1.0, 0.0).astype(BF)
    for cc in (0, 1):
        part = zbuf[pl.ds(cc * 8, 8)].reshape(128, HALF)
        wblk[cc] = jnp.dot(pick, part, preferred_element_type=F32).astype(BF)

    def x_part(i):
        i = lax.rem(i + 4, 4)
        return lax.div(i, 2), lax.rem(i, 2)

    def y_part(i):
        return lax.rem(i + 4, 4)

    def small(yi, xi):
        a, b = x_part(xi)
        return wout.at[y_part(yi), a, :, b]

    def small_half(yi, xi, j):
        a, b = x_part(xi)
        return wout.at[y_part(yi), a, j, b]

    own_copy = pltpu.make_async_copy(wblk, small(y, xx), local.at[7])
    own_copy.start()

    def corners(win, n, m):
        for rr, first in ((0, n + 1), (3, n)):
            wire.arrived(win.at[rr * 3 + 1], first)
            corner(win, m, rr)

    fx, fy = 1 - c, c
    ring = Wire(send, recv)
    one = [at_grid(y + d * fy, xx + d * fx, z, c) for d in (1, -1)]
    two = [at_grid(y + d * fx, xx + d * fy, z, c) for d in (1, -1)]
    w0 = 34
    at = (0, -1, 1, 2)

    def full(a, b):
        return small(y + a * fy + b * fx, xx + a * fx + b * fy)

    def half(a, b, j):
        return small_half(y + a * fy + b * fx, xx + a * fx + b * fy, j)

    def across(n, src):
        for i in (0, 1):
            m = w0 + 4 + 2 * n + i
            ring.start(src, full(at[n], 0), two[i], m, m)

    def pass_on(n):
        for i, d in enumerate((-1, 1)):
            ring.arrived(full(at[n], d), w0 + 4 + 2 * n + i)
            m = w0 + 12 + 2 * n + i
            ring.start(half(at[n], d, i), half(at[n], d, i), two[i], m, m)

    for i in (0, 1):
        ring.start(wblk, full(0, 0), one[i], w0 + i, w0 + i)
    across(0, wblk)
    keys_aside()
    for i, d in enumerate((-1, 1)):
        ring.arrived(full(d, 0), w0 + i)
        ring.start(half(d, 0, i), half(d, 0, i), one[i], w0 + 2 + i, w0 + 2 + i)
        across(1 + i, full(d, 0))
    corners(kwin, 16, 70)
    pass_on(0)
    for i in (0, 1):
        ring.arrived(half(2, 0, i), w0 + 2 + i)
    across(3, full(2, 0))
    side_relay(kwin, 18)
    pass_on(1)

    def heads(start, width):
        return pl.ds(pl.multiple_of(mine + start, 128), width)

    def keys_here():
        side_arrivals(kwin, 18)
        wire.arrived(q2.at[0], 30)
        wire.arrived(c2.at[0], 31)
        wire.arrived(allow2.at[0], 33)
        corner_arrivals(kwin, 70)

    back[...] = jnp.zeros_like(back)
    upt[...] = jnp.zeros_like(upt)

    def place_of(i):
        h, t = lax.div(i, 2), lax.rem(i, 2)
        return h, t, pl.ds(pl.multiple_of(h * 128, 128), 128)

    def score(i, to):
        h, t, lanes = place_of(i)
        keys = kwin[pl.ds(t * 3, 9), :, lanes].reshape(2304, 128)
        to[...] = lax.dot_general(
            q2[t, :, lanes], keys, (((1,), (1,)), ((), ())), preferred_element_type=F32
        )

    log_scale = 128**-0.5 * 1.4426950408889634

    def soften(i, s_ref):
        h, t, _ = place_of(i)
        reach = radius[c * 6 + h]
        limit = allow2[t, 0:1, :] * (reach * reach + 1).astype(F32) - 1.0
        for j in range(8):
            rows = slice(j * 32, (j + 1) * 32)
            s = jnp.where(dist[rows] <= limit, s_ref[rows], -1e30)
            e = jnp.exp2((s - jnp.max(s, axis=1, keepdims=True)) * log_scale)
            p_ref[i, rows] = (e * (1.0 / jnp.sum(e, axis=1, keepdims=True))).astype(BF)

    def gradient(i):
        h, t, lanes = place_of(i)
        vgt = jnp.dot(c2[t, :, lanes].T, p_ref[i], preferred_element_type=F32).astype(BF)
        bt = jnp.dot(up[:, heads(h * 128, 128)], vgt, preferred_element_type=F32)
        for n in range(9):
            back[t * 3 + n] += bt[:, n * 256 : (n + 1) * 256]
        lows = kwin[pl.ds(t * 3, 9), :, HALF:WIDE].reshape(2304, 128)
        upt[lanes] += jnp.dot(vgt, lows, preferred_element_type=F32)

    def probs(lo, hi):
        @pl.loop(lo, hi)
        def _(m):
            score(2 * m, s_one)
            score(2 * m + 1, s_two)
            soften(2 * m, s_one)
            soften(2 * m + 1, s_two)
            gradient(2 * m)
            gradient(2 * m + 1)

    def attend(lo, hi):
        for i in range(lo, hi):
            h, t = i // 2, i % 2
            lanes = slice(h * 128, (h + 1) * 128)
            vals = vwin[t * 3 : t * 3 + 9, :, lanes].reshape(2304, 128)
            att2[t, :, lanes] = jnp.dot(p_ref[i], vals, preferred_element_type=F32).astype(BF)

    pass_on(2)
    pass_on(3)
    for n in range(4):
        for i in (0, 1):
            ring.arrived(half(0, 2, i), w0 + 12 + 2 * n + i)
    own_copy.wait()

    wire.arrived(x2.at[0], 32)
    wire.arrived(kwin.at[0], 22)
    low2 = jnp.concatenate([kwin[4, :, HALF : HALF + 64], kwin[7, :, HALF : HALF + 64]], axis=0)

    @pl.loop(0, 3)
    def _(n):
        lanes = pl.ds(pl.multiple_of(n * 256, 256), 256)
        acc = jnp.dot(low2, up[:, heads(n * 256, 256)], preferred_element_type=F32)
        for yi in range(4):
            rows = wout[yi, :, :, :, :, lanes].reshape(768, 256)
            part = x2[:, :, yi * 768 : (yi + 1) * 768].reshape(512, 768)
            acc = acc + jnp.dot(part, rows, preferred_element_type=F32)
        acc = acc.astype(BF)
        vwin[4, :, lanes] = acc[:256]
        vwin[7, :, lanes] = acc[256:]

    v0 = 54
    wire.start(vwin.at[4], vwin.at[10], at_chip(k - 1, c, col), v0, v0)
    wire.start(vwin.at[7], vwin.at[1], at_chip(k + 1, c, col), v0 + 1, v0 + 1)
    for t in (0, 1):
        side_sends([(t, c, vwin.at[4 + 3 * t])], vwin, 1 + t, v0 + 2, t)

    keys_here()

    probs(0, 6)
    wire.arrived(vwin.at[10], v0)
    corner(vwin, 60, 3)
    wire.arrived(vwin.at[1], v0 + 1)
    corner(vwin, 60, 0)

    def values_here():
        side_arrivals(vwin, v0 + 2)
        corner_arrivals(vwin, 60)

    b0 = 78
    for n in range(12):
        rr, cc = n // 3, n % 3
        bs[n] = back[n].astype(BF)
        dk, h = ((-1, 1), (0, 0), (0, 1), (1, 0))[rr]
        slot = (0 if rr in (1, 2) else 6) + cc * 2
        if n in (4, 7):

            @pl.when(c != h)
            def _():
                wire.copy(bs.at[n], br.at[slot + c], sib, b0 + 12, b0 + slot + c).start()
        else:
            target = at_chip(k + dk, h, col + cc - 1)
            wire.start(bs.at[n], br.at[slot + c], target, b0 + n, b0 + slot + c)

    u0, e0 = 92, 116
    for a in range(4):
        for b in range(4):
            ux[a, b] = upt[(a * 4 + b) * 48 : (a * 4 + b + 1) * 48, 0:64].astype(BF)
    for i in range(3):
        wire.start(ux.at[lax.rem(xx + i + 1, 4)], uxr.at[i], xt[i], u0 + i, u0 + i)

    side_relay(vwin, v0 + 2)
    total = back[(1 + c) * 3 + 1]
    wire.arrived(br.at[0], b0 + 2 + other)
    total = total + br[2 + other].astype(F32)
    for slot in range(12):
        if slot not in (2, 3):
            wire.arrived(br.at[0], b0 + slot)
            total = total + br[slot].astype(F32)
    hi = total.astype(BF)
    lo = (total - hi.astype(F32)).astype(BF)
    both = jnp.concatenate([hi, lo], axis=0)

    for i in range(3):
        wire.arrived(uxr.at[0], u0 + i)
    for b in range(4):
        ua = upt[pl.ds(pl.multiple_of((xx * 4 + b) * 48, 16), 48), 0:64]
        for i in range(3):
            ua = ua + uxr[i, b].astype(F32)
        ukeep[b] = ua
        uy[b] = ua.astype(BF)
    for i in range(3):
        wire.start(uy.at[lax.rem(y + i + 1, 4)], uyr.at[i], yt[i], u0 + 3 + i, u0 + 3 + i)

    for i in range(8):
        part = x2[c, :, i * 384 : (i + 1) * 384]
        g = jnp.dot(both, part, preferred_element_type=F32)
        g = (g[:64] + g[64:]).T
        yi, xhi = i // 2, i % 2
        for cc in (0, 1):
            for xl in (0, 1):
                rows = g[(cc * 2 + xl) * 96 : (cc * 2 + xl + 1) * 96]
                keep[cc, xhi * 2 + xl, yi] = rows
                gs[cc, xhi * 2 + xl, yi] = rows.astype(BF)

    wire.start(gs.at[other], gr, sib, e0, e0)

    for i in range(3):
        wire.arrived(uyr.at[0], u0 + 3 + i)
    ua = ukeep[y]
    for i in range(3):
        ua = ua + uyr[i].astype(F32)
    uz[...] = ua.astype(BF)
    uzr[z] = ua.astype(BF)
    for i in range(7):
        wire.start(uz, uzr.at[z], zt[i], u0 + 6 + i, u0 + 6 + i)

    wire.arrived(gr, e0)
    for a in range(4):
        for b in range(4):
            full = keep[c, a, b] + gr[a, b].astype(F32)
            keep[0, a, b] = full
            gx[a, b] = full.astype(BF)
    for i in range(3):
        wire.start(gx.at[lax.rem(xx + i + 1, 4)], gxr.at[i], xt[i], e0 + 1 + i, e0 + 1 + i)
    values_here()
    attend(0, 4)

    scale = 65536**-0.5
    for i in range(7):
        wire.arrived(uz, u0 + 6 + i)
    ua = uzr[0].astype(F32)
    for i in range(1, 8):
        ua = ua + uzr[i].astype(F32)
    gun[c, xx, y] = ua * scale
    spot = gun.at[c, xx, y]
    for i in range(3):
        wire.start(spot, spot, yt[i], u0 + 13 + i, u0 + 13 + i)

    for i in range(3):
        wire.arrived(gxr.at[0], e0 + 1 + i)
    for b in range(4):
        acc = keep[0, xx, b]
        for i in range(3):
            acc = acc + gxr[i, b].astype(F32)
        keep[1, 0, b] = acc
        gy[b] = acc.astype(BF)
    for i in range(3):
        wire.start(gy.at[lax.rem(y + i + 1, 4)], gyr.at[i], yt[i], e0 + 4 + i, e0 + 4 + i)
    attend(4, 8)

    for i in range(3):
        wire.arrived(spot, u0 + 13 + i)
    for i in range(3):
        wire.start(gun.at[c, xx], gun.at[c, xx], xt[i], u0 + 16 + i, u0 + 16 + i)

    for i in range(3):
        wire.arrived(gyr.at[0], e0 + 4 + i)
    acc = keep[1, 0, y]
    for i in range(3):
        acc = acc + gyr[i].astype(F32)
    r_out = lax.broadcasted_iota(jnp.int32, (128, 96), 0)
    r_in = lax.broadcasted_iota(jnp.int32, (128, 96), 1)
    row_of = lax.div(r_out, 16) * 12 + lax.rem(r_out, 16)
    pick = jnp.where((row_of == r_in) & (lax.rem(r_out, 16) < 12), 1.0, 0.0).astype(BF)
    parts = jnp.dot(pick, acc.astype(BF), preferred_element_type=F32).astype(BF)
    for i in range(8):
        gz[i] = parts[i * 16 : (i + 1) * 16]
    for i in range(7):
        wire.start(gz.at[lax.rem(z + i + 1, 8)], gzr.at[i], zt[i], e0 + 7 + i, e0 + 7 + i)

    for i in range(3):
        wire.arrived(gun.at[c, xx], u0 + 16 + i)
    wire.start(gun.at[c], gun.at[c], sib, u0 + 19, u0 + 19)

    attend(8, 12)
    wire.start(att2.at[other], att.at[:, pl.ds(mine, HALF)], sib, e0 + 14, e0 + 14)
    keep_att = pltpu.make_async_copy(att2.at[c], att.at[:, pl.ds(mine, HALF)], local.at[6])
    keep_att.start()

    for i in range(7):
        wire.arrived(gzr.at[0], e0 + 7 + i)
    acc = gz[z].astype(F32)
    for i in range(7):
        acc = acc + gzr[i].astype(F32)
    gd[...] = (acc * scale)[0:12]
    wire.arrived(gun.at[c], u0 + 19)
    for cc in (0, 1):
        for i in (0, 2):
            lanes = pl.ds(cc * HALF + i * 192, 384)
            gu[:, lanes] = gun[cc, i : i + 2].reshape(384, 64).T
    wire.arrived(att.at[:, pl.ds(mine, HALF)], e0 + 14)
    keep_att.wait()
    wire.copy(bs.at[0], bs.at[0], sib, b0 + 12, b0 + 12).wait_send()
    ring.drain()
    wire.drain()


def distances():
    qp = np.arange(256)
    kp = np.arange(2304)
    kr = (kp // 768) * 16 + (kp % 256) // 16 - 16
    kc = (kp // 256 % 3) * 16 + kp % 16 - 16
    dr = kr[None] - (qp // 16)[:, None]
    dc = kc[None] - (qp % 16)[:, None]
    return (dr * dr + dc * dc).astype(np.float32)


def fused(*args):
    vm = pl.BlockSpec(memory_space=pltpu.VMEM)
    hb = pl.BlockSpec(memory_space=pl.ANY)
    return pl.pallas_call(
        kernel,
        out_shape=[
            jax.ShapeDtypeStruct((256, 1536), BF),
            jax.ShapeDtypeStruct((12, 64), F32),
            jax.ShapeDtypeStruct((64, 1536), F32),
        ],
        in_specs=[pl.BlockSpec(memory_space=pltpu.SMEM)] * 2 + [hb] * 4 + [vm] * 4,
        out_specs=[hb, vm, vm],
        scratch_shapes=[
            pltpu.VMEM((2, 256, HALF), BF),
            pltpu.VMEM((12, 256, WIDE), BF),
            pltpu.VMEM((2, 256, HALF), BF),
            pltpu.VMEM((2, 256, WIDE), BF),
            pltpu.VMEM((2, 256, 3072), BF),
            pltpu.VMEM((4, 2, 2, 2, 96, HALF), BF),
            pltpu.VMEM((2, 8, 2304), F32),
            pltpu.VMEM((16, 16, HALF), BF),
            pltpu.VMEM((2, 96, HALF), BF),
            pltpu.VMEM((16, 1536), BF),
            pltpu.VMEM((2, 4, 4, 48, 64), F32),
            pltpu.VMEM((12, 256, HALF), BF),
            pltpu.VMEM((256, 2304), F32),
            pltpu.VMEM((256, 2304), F32),
            pltpu.VMEM((12, 256, 2304), BF),
            pltpu.VMEM((12, 64, 256), F32),
            pltpu.VMEM((HALF, 128), F32),
            pltpu.VMEM((2, 256, HALF), BF),
            pltpu.VMEM((12, 64, 256), BF),
            pltpu.VMEM((12, 64, 256), BF),
            pltpu.VMEM((2, 4, 4, 96, 64), BF),
            pltpu.VMEM((4, 4, 96, 64), BF),
            pltpu.VMEM((2, 4, 4, 96, 64), F32),
            pltpu.VMEM((4, 4, 48, 64), BF),
            pltpu.VMEM((3, 4, 48, 64), BF),
            pltpu.VMEM((4, 48, 64), F32),
            pltpu.VMEM((4, 48, 64), BF),
            pltpu.VMEM((3, 48, 64), BF),
            pltpu.VMEM((48, 64), BF),
            pltpu.VMEM((8, 48, 64), BF),
            pltpu.VMEM((4, 4, 96, 64), BF),
            pltpu.VMEM((3, 4, 96, 64), BF),
            pltpu.VMEM((4, 96, 64), BF),
            pltpu.VMEM((3, 96, 64), BF),
            pltpu.VMEM((8, 16, 64), BF),
            pltpu.VMEM((7, 16, 64), BF),
            pltpu.SemaphoreType.DMA((136,)),
            pltpu.SemaphoreType.DMA((136,)),
            pltpu.SemaphoreType.DMA((8,)),
        ],
        compiler_params=pltpu.CompilerParams(
            collective_id=0, has_side_effects=True, vmem_limit_bytes=60 * MIB
        ),
        name="fused",
    )(*args)


def per_device(
    patch_tokens,
    queries,
    key_vectors,
    cotangent,
    value_weight,
    adapter_down,
    adapter_up,
    radius,
    tile_mask,
):
    att, gd, gu = fused(
        radius,
        tile_mask,
        queries.reshape(256, 1536),
        key_vectors.reshape(256, 1536),
        cotangent.reshape(256, 1536),
        patch_tokens.reshape(256, 3072),
        value_weight,
        adapter_down.T,
        adapter_up,
        jnp.asarray(distances()),
    )
    return att.reshape(16, 16, 1536), gd, gu


def solution(mesh):
    placed = (
        P("row", "col", None),
        P("row", "col", None),
        P("row", "col", None),
        P("row", "col", None),
        P(("row", "col"), None),
        P(),
        P(),
        P(),
        P("row", "col", None),
    )
    return jax.shard_map(
        per_device,
        mesh=mesh,
        in_specs=placed,
        out_specs=(P("row", "col", None), P(("row", "col"), None), P()),
        check_vma=False,
    )
```

```python
import jax
import jax.numpy as jnp
import numpy as np
from jax import lax
from jax.experimental import pallas as pl
from jax.experimental.pallas import tpu as pltpu
from jax.sharding import PartitionSpec as P

MESH = pl.DeviceIdType.MESH
BF = jnp.bfloat16
F32 = jnp.float32
HALF = 768
WIDE = 896
MIB = 2**20


def place():
    row = lax.axis_index("row")
    col = lax.axis_index("col")
    return row, col


def grid_place():
    row, col = place()
    y = lax.div(row, 4)
    x = lax.rem(lax.div(row, 2), 2) * 2 + lax.div(col, 8)
    return y, x, lax.rem(col, 8), lax.rem(row, 2)


def at_grid(y, x, z, c):
    y = lax.rem(y + 4, 4)
    x = lax.rem(x + 4, 4)
    z = lax.rem(z + 8, 8)
    return (y * 4 + lax.div(x, 2) * 2 + c, lax.rem(x, 2) * 8 + z)


def at_chip(k, h, col):
    return (lax.rem(k + 8, 8) * 2 + h, lax.rem(col + 16, 16))


def greet(targets):
    barrier = pltpu.get_barrier_semaphore()
    for target in targets:
        pl.semaphore_signal(barrier, inc=1, device_id=target, device_id_type=MESH)
    return lambda: pl.semaphore_wait(barrier, len(targets))


class Wire:
    def __init__(self, send, recv):
        self.send, self.recv, self.pending = send, recv, []

    def copy(self, src, dst, target, s, r):
        return pltpu.make_async_remote_copy(
            src_ref=src,
            dst_ref=dst,
            send_sem=self.send.at[s],
            recv_sem=self.recv.at[r],
            device_id=target,
            device_id_type=MESH,
        )

    def start(self, src, dst, target, s, r):
        copy = self.copy(src, dst, target, s, r)
        copy.start()
        self.pending.append(copy)

    def arrived(self, dst, r):
        row, col = place()
        self.copy(dst, dst, (row + 1 - 2 * lax.rem(row, 2), col), r, r).wait_recv()

    def drain(self):
        for copy in self.pending:
            copy.wait_send()
        self.pending = []


def chip_targets():
    row, col = place()
    k, c = lax.div(row, 2), lax.rem(row, 2)
    out = [at_chip(k, 1 - c, col)]
    for h in (0, 1):
        out += [at_chip(k + 1, h, col), at_chip(k - 1, h, col)]
        out += [at_chip(k, h, col + 1), at_chip(k, h, col - 1)]
    return out


def stretch(c):
    return pl.multiple_of(c * HALF, HALF)


def kernel(
    radius, mask, q, kv, cot, x, w, down, up, dist,
    att, gd, gu,
    q2, kwin, c2, keys_out, x2, wout, allow2, zbuf, wblk, wp, gun,
    vwin, s_one, s_two, p_ref, back, upt, att2,
    bs, br, gs, gr, keep, ux, uxr, ukeep, uy, uyr, uz, uzr, gx, gxr, gy, gyr, gz, gzr,
    send, recv, local,
):
    row, col = place()
    k, c = lax.div(row, 2), lax.rem(row, 2)
    y, xx, z, _ = grid_place()
    other = 1 - c
    mine = stretch(c)
    wire = Wire(send, recv)
    targets = chip_targets()
    for a in range(1, 8):
        targets += [at_grid(y, xx, z + a, 0), at_grid(y, xx, z + a, 1)]
    xt = [at_grid(y, xx + a, z, c) for a in (1, 2, 3)]
    yt = [at_grid(y + a, xx, z, c) for a in (1, 2, 3)]
    zt = [at_grid(y, xx, z + a, c) for a in range(1, 8)]
    xo = [at_grid(y, xx + a, z, other) for a in (1, 2, 3)]
    targets += xt + yt + xo
    targets += [at_chip(k, h, col + d) for d in (7, 8, 9) for h in (0, 1)]
    for h in (0, 1):
        for d in (1, -1):
            targets += [at_chip(k + 1, h, col + d), at_chip(k - 1, h, col + d)]
    sib = at_chip(k, other, col)
    theirs = stretch(other)

    locals_ = []

    def local_copy(src, dst):
        copy = pltpu.make_async_copy(src, dst, local.at[len(locals_)])
        copy.start()
        locals_.append(copy)
        return copy

    slot = c * 8 + z
    centre = (1 + c) * 3 + 1
    far = (3 - 3 * c) * 3 + 1
    step = 2 * c - 1

    crossing = ((0, 1, 7, 15), (1, -1, 8, 0))

    def side_sends(parts, win, rr, n, which):
        for h, target_core, src in parts:
            for i, d, hop, relay in crossing:
                spot, near = win.at[rr * 3 + 1 - d], win.at[rr * 3 + 1 + d]

                @pl.when((col != hop) & (col != relay))
                def _(h=h, i=i, d=d, src=src, target_core=target_core, spot=spot):
                    target = at_chip(k, target_core, col + d)
                    wire.copy(src, spot, target, n + 2 * i + h, n + 2 * i + which).start()

                @pl.when(col == hop)
                def _(h=h, i=i, src=src, target_core=target_core, near=near, relay=relay):
                    target = at_chip(k, target_core, jnp.int32(relay))
                    wire.copy(src, near, target, n + 2 * i + h, n + 2 * (1 - i) + which).start()

    def side_relay(win, n):
        for i, d, hop, relay in crossing:

            @pl.when(col == relay)
            def _(i=i, d=d, hop=hop):
                for t in (0, 1):
                    spot, near = win.at[(1 + t) * 3 + 1 - d], win.at[(1 + t) * 3 + 1 + d]
                    wire.arrived(near, n + 2 * (1 - i) + t)
                    m = n + 2 * i + t
                    wire.copy(near, spot, (row, jnp.int32(hop + d)), m, m).start()

    def side_arrivals(win, n):
        for i, edge in enumerate((0, 15)):

            @pl.when(col != edge)
            def _(i=i):
                wire.arrived(win.at[0], n + 2 * i)
                wire.arrived(win.at[0], n + 2 * i + 1)

        for m in range(4):
            wire.copy(win.at[0], win.at[0], sib, n + m, n + m).wait_send()

    def clear_edges(win):
        for edge, cc in ((0, 0), (15, 2)):

            @pl.when(col == edge)
            def _(cc=cc):
                for rr in (0, 3):
                    win[rr * 3 + cc] = jnp.zeros(win.shape[1:], win.dtype)

    def corner(win, m, rr):
        src = win.at[rr * 3 + 1]
        for i, d, _, edge in crossing:

            @pl.when(col != edge)
            def _(i=i, d=d):
                n = m + (2 if rr else 0) + i
                wire.copy(src, win.at[rr * 3 + 1 - d], at_chip(k, c, col + d), n, n).start()

    def corner_arrivals(win, m):
        for n in (m, m + 2):
            for i, edge in enumerate((0, 15)):

                @pl.when(col != edge)
                def _(n=n, i=i):
                    wire.arrived(win.at[0], n + i)

                @pl.when(col != 15 - edge)
                def _(n=n, i=i):
                    wire.copy(win.at[0], win.at[0], sib, n + i, n + i).wait_send()

    def keys_up():
        for h in (0, 1):
            wire.start(keys_out.at[h], kwin.at[far], at_chip(k + step, h, col), 16 + h, 16 + c)

    def keys_aside():
        parts = [(h, h, keys_out.at[h]) for h in (0, 1)]
        side_sends(parts, kwin, 1 + c, 18, c)

    met = greet(targets)
    own_x = local_copy(x, x2.at[c])
    own_k = local_copy(kv.at[:, pl.ds(mine, HALF)], kwin.at[centre, :, pl.ds(0, HALF)])
    for h in (0, 1):
        local_copy(kv.at[:, pl.ds(h * HALF, HALF)], keys_out.at[h, :, pl.ds(0, HALF)])
    local_copy(q.at[:, pl.ds(mine, HALF)], q2.at[c])
    local_copy(cot.at[:, pl.ds(mine, HALF)], c2.at[c])
    for n in range(9):
        r, t = row + n // 3 - 1, col + n % 3 - 1
        seen = (r >= 0) & (r < 16) & (t >= 0) & (t < 16) & (mask[0, 0, n] > 0)
        allow2[c, :, n * 256 : (n + 1) * 256] = jnp.full((8, 256), jnp.where(seen, 1.0, 0.0))
    r_out = lax.broadcasted_iota(jnp.int32, (16, 12), 0)
    r_in = lax.broadcasted_iota(jnp.int32, (16, 12), 1)
    wp[...] = jnp.dot(
        jnp.where(r_out == r_in, 1.0, 0.0).astype(BF), w[...], preferred_element_type=F32
    ).astype(BF)
    own_w = local_copy(wp.at[:, pl.ds(mine, HALF)], zbuf.at[slot])
    own_x.wait()
    low = lax.dot_general(
        x2[c], down[...], (((1,), (1,)), ((), ())), preferred_element_type=F32
    ).astype(BF)
    low = jnp.concatenate([low, jnp.zeros((256, 64), BF)], axis=1)
    for h in (0, 1):
        keys_out[h, :, HALF:WIDE] = low
    clear_edges(kwin)
    clear_edges(vwin)
    kwin[centre, :, HALF:WIDE] = low
    for copy in locals_[1:]:
        copy.wait()
    met()

    wire.start(wp.at[:, pl.ds(theirs, HALF)], zbuf.at[slot], sib, 0, 0)
    for a in range(1, 8):
        for h in (0, 1):
            hh = c if h == 0 else other
            wire.start(
                wp.at[:, pl.ds(stretch(hh), HALF)],
                zbuf.at[slot],
                at_grid(y, xx, z + a, hh),
                2 * a + h,
                2 * a + h,
            )
    keys_up()
    wire.start(keys_out.at[other], kwin.at[centre], sib, 22, 22)
    wire.start(q.at[:, pl.ds(theirs, HALF)], q2.at[c], sib, 30, 30)
    wire.start(cot.at[:, pl.ds(theirs, HALF)], c2.at[c], sib, 31, 31)
    wire.start(x, x2.at[c], sib, 32, 32)
    wire.start(allow2.at[c], allow2.at[c], sib, 33, 33)
    wire.arrived(zbuf.at[0], 0)
    for a in range(1, 8):
        for h in (0, 1):
            wire.arrived(zbuf.at[0], 2 * a + h)
    r_out = lax.broadcasted_iota(jnp.int32, (96, 128), 0)
    r_in = lax.broadcasted_iota(jnp.int32, (96, 128), 1)
    pick = jnp.where(lax.div(r_out, 12) * 16 + lax.rem(r_out, 12) == r_in, 1.0, 0.0).astype(BF)
    for cc in (0, 1):
        part = zbuf[pl.ds(cc * 8, 8)].reshape(128, HALF)
        wblk[cc] = jnp.dot(pick, part, preferred_element_type=F32).astype(BF)

    def x_part(i):
        i = lax.rem(i + 4, 4)
        return lax.div(i, 2), lax.rem(i, 2)

    def y_part(i):
        return lax.rem(i + 4, 4)

    def small(yi, xi):
        a, b = x_part(xi)
        return wout.at[y_part(yi), a, :, b]

    def small_half(yi, xi, j):
        a, b = x_part(xi)
        return wout.at[y_part(yi), a, j, b]

    own_copy = pltpu.make_async_copy(wblk, small(y, xx), local.at[7])
    own_copy.start()

    def corners(win, n, m):
        for rr, first in ((0, n + 1), (3, n)):
            wire.arrived(win.at[rr * 3 + 1], first)
            corner(win, m, rr)

    fx, fy = 1 - c, c
    ring = Wire(send, recv)
    one = [at_grid(y + d * fy, xx + d * fx, z, c) for d in (1, -1)]
    two = [at_grid(y + d * fx, xx + d * fy, z, c) for d in (1, -1)]
    w0 = 34
    at = (0, -1, 1, 2)

    def full(a, b):
        return small(y + a * fy + b * fx, xx + a * fx + b * fy)

    def half(a, b, j):
        return small_half(y + a * fy + b * fx, xx + a * fx + b * fy, j)

    def across(n, src):
        for i in (0, 1):
            m = w0 + 4 + 2 * n + i
            ring.start(src, full(at[n], 0), two[i], m, m)

    def pass_on(n):
        for i, d in enumerate((-1, 1)):
            ring.arrived(full(at[n], d), w0 + 4 + 2 * n + i)
            m = w0 + 12 + 2 * n + i
            ring.start(half(at[n], d, i), half(at[n], d, i), two[i], m, m)

    for i in (0, 1):
        ring.start(wblk, full(0, 0), one[i], w0 + i, w0 + i)
    across(0, wblk)
    keys_aside()
    for i, d in enumerate((-1, 1)):
        ring.arrived(full(d, 0), w0 + i)
        ring.start(half(d, 0, i), half(d, 0, i), one[i], w0 + 2 + i, w0 + 2 + i)
        across(1 + i, full(d, 0))
    corners(kwin, 16, 70)
    pass_on(0)
    for i in (0, 1):
        ring.arrived(half(2, 0, i), w0 + 2 + i)
    across(3, full(2, 0))
    side_relay(kwin, 18)
    pass_on(1)

    def heads(start, width):
        return pl.ds(pl.multiple_of(mine + start, 128), width)

    def keys_here():
        side_arrivals(kwin, 18)
        wire.arrived(q2.at[0], 30)
        wire.arrived(c2.at[0], 31)
        wire.arrived(allow2.at[0], 33)
        corner_arrivals(kwin, 70)

    back[...] = jnp.zeros_like(back)
    upt[...] = jnp.zeros_like(upt)

    def place_of(i):
        h, t = lax.div(i, 2), lax.rem(i, 2)
        return h, t, pl.ds(pl.multiple_of(h * 128, 128), 128)

    def score(i, to):
        h, t, lanes = place_of(i)
        keys = kwin[pl.ds(t * 3, 9), :, lanes].reshape(2304, 128)
        to[...] = lax.dot_general(
            q2[t, :, lanes], keys, (((1,), (1,)), ((), ())), preferred_element_type=F32
        )

    log_scale = 128**-0.5 * 1.4426950408889634

    def soften(i, s_ref):
        h, t, _ = place_of(i)
        reach = radius[c * 6 + h]
        limit = allow2[t, 0:1, :] * (reach * reach + 1).astype(F32) - 1.0
        for j in range(8):
            rows = slice(j * 32, (j + 1) * 32)
            s = jnp.where(dist[rows] <= limit, s_ref[rows], -1e30)
            e = jnp.exp2((s - jnp.max(s, axis=1, keepdims=True)) * log_scale)
            p_ref[i, rows] = (e * (1.0 / jnp.sum(e, axis=1, keepdims=True))).astype(BF)

    def gradient(i):
        h, t, lanes = place_of(i)
        vgt = jnp.dot(c2[t, :, lanes].T, p_ref[i], preferred_element_type=F32).astype(BF)
        bt = jnp.dot(up[:, heads(h * 128, 128)], vgt, preferred_element_type=F32)
        for n in range(9):
            back[t * 3 + n] += bt[:, n * 256 : (n + 1) * 256]
        lows = kwin[pl.ds(t * 3, 9), :, HALF:WIDE].reshape(2304, 128)
        upt[lanes] += jnp.dot(vgt, lows, preferred_element_type=F32)

    def probs(lo, hi):
        @pl.loop(lo, hi)
        def _(m):
            score(2 * m, s_one)
            score(2 * m + 1, s_two)
            soften(2 * m, s_one)
            soften(2 * m + 1, s_two)
            gradient(2 * m)
            gradient(2 * m + 1)

    def attend(lo, hi):
        for i in range(lo, hi):
            h, t = i // 2, i % 2
            lanes = slice(h * 128, (h + 1) * 128)
            vals = vwin[t * 3 : t * 3 + 9, :, lanes].reshape(2304, 128)
            att2[t, :, lanes] = jnp.dot(p_ref[i], vals, preferred_element_type=F32).astype(BF)

    pass_on(2)
    pass_on(3)
    for n in range(4):
        for i in (0, 1):
            ring.arrived(half(0, 2, i), w0 + 12 + 2 * n + i)
    own_copy.wait()

    wire.arrived(x2.at[0], 32)
    wire.arrived(kwin.at[0], 22)
    low2 = jnp.concatenate([kwin[4, :, HALF : HALF + 64], kwin[7, :, HALF : HALF + 64]], axis=0)

    @pl.loop(0, 3)
    def _(n):
        lanes = pl.ds(pl.multiple_of(n * 256, 256), 256)
        acc = jnp.dot(low2, up[:, heads(n * 256, 256)], preferred_element_type=F32)
        for yi in range(4):
            rows = wout[yi, :, :, :, :, lanes].reshape(768, 256)
            part = x2[:, :, yi * 768 : (yi + 1) * 768].reshape(512, 768)
            acc = acc + jnp.dot(part, rows, preferred_element_type=F32)
        acc = acc.astype(BF)
        vwin[4, :, lanes] = acc[:256]
        vwin[7, :, lanes] = acc[256:]

    v0 = 54
    wire.start(vwin.at[4], vwin.at[10], at_chip(k - 1, c, col), v0, v0)
    wire.start(vwin.at[7], vwin.at[1], at_chip(k + 1, c, col), v0 + 1, v0 + 1)
    for t in (0, 1):
        side_sends([(t, c, vwin.at[4 + 3 * t])], vwin, 1 + t, v0 + 2, t)

    keys_here()

    probs(0, 6)

    def values_here():
        side_arrivals(vwin, v0 + 2)
        corner_arrivals(vwin, 60)

    b0 = 78
    for n in range(12):
        rr, cc = n // 3, n % 3
        bs[n] = back[n].astype(BF)
        dk, h = ((-1, 1), (0, 0), (0, 1), (1, 0))[rr]
        slot = (0 if rr in (1, 2) else 6) + cc * 2
        if n in (4, 7):

            @pl.when(c != h)
            def _():
                wire.copy(bs.at[n], br.at[slot + c], sib, b0 + 12, b0 + slot + c).start()
        else:
            target = at_chip(k + dk, h, col + cc - 1)
            wire.start(bs.at[n], br.at[slot + c], target, b0 + n, b0 + slot + c)

    wire.arrived(vwin.at[10], v0)
    corner(vwin, 60, 3)
    wire.arrived(vwin.at[1], v0 + 1)
    corner(vwin, 60, 0)
    u0, e0 = 92, 120
    for a in range(4):
        for b in range(4):
            ux[a, b] = upt[(a * 4 + b) * 48 : (a * 4 + b + 1) * 48, 0:64].astype(BF)
    for i in range(3):
        wire.start(ux.at[lax.rem(xx + i + 1, 4)], uxr.at[i], xt[i], u0 + i, u0 + i)

    side_relay(vwin, v0 + 2)
    total = back[(1 + c) * 3 + 1]
    wire.arrived(br.at[0], b0 + 2 + other)
    total = total + br[2 + other].astype(F32)
    for slot in range(12):
        if slot not in (2, 3):
            wire.arrived(br.at[0], b0 + slot)
            total = total + br[slot].astype(F32)
    hi = total.astype(BF)
    lo = (total - hi.astype(F32)).astype(BF)
    both = jnp.concatenate([hi, lo], axis=0)

    for i in range(3):
        wire.arrived(uxr.at[0], u0 + i)
    for b in range(4):
        ua = upt[pl.ds(pl.multiple_of((xx * 4 + b) * 48, 16), 48), 0:64]
        for i in range(3):
            ua = ua + uxr[i, b].astype(F32)
        ukeep[b] = ua
        uy[b] = ua.astype(BF)
    for i in range(3):
        wire.start(uy.at[lax.rem(y + i + 1, 4)], uyr.at[i], yt[i], u0 + 3 + i, u0 + 3 + i)

    for i in range(8):
        part = x2[c, :, i * 384 : (i + 1) * 384]
        g = jnp.dot(both, part, preferred_element_type=F32)
        g = (g[:64] + g[64:]).T
        yi, xhi = i // 2, i % 2
        for cc in (0, 1):
            for xl in (0, 1):
                rows = g[(cc * 2 + xl) * 96 : (cc * 2 + xl + 1) * 96]
                keep[cc, xhi * 2 + xl, yi] = rows
                gs[cc, xhi * 2 + xl, yi] = rows.astype(BF)

    wire.start(gs.at[other], gr, sib, e0, e0)

    for i in range(3):
        wire.arrived(uyr.at[0], u0 + 3 + i)
    ua = ukeep[y]
    for i in range(3):
        ua = ua + uyr[i].astype(F32)
    uz[...] = ua.astype(BF)
    uzr[z] = ua.astype(BF)
    for i in range(7):
        wire.start(uz, uzr.at[z], zt[i], u0 + 6 + i, u0 + 6 + i)

    wire.arrived(gr, e0)
    for a in range(4):
        for b in range(4):
            full = keep[c, a, b] + gr[a, b].astype(F32)
            keep[0, a, b] = full
            gx[a, b] = full.astype(BF)
    for i in range(3):
        wire.start(gx.at[lax.rem(xx + i + 1, 4)], gxr.at[i], xt[i], e0 + 1 + i, e0 + 1 + i)
    values_here()
    attend(0, 4)

    scale = 65536**-0.5
    for i in range(7):
        wire.arrived(uz, u0 + 6 + i)
    ua = uzr[0].astype(F32)
    for i in range(1, 8):
        ua = ua + uzr[i].astype(F32)
    gun[c, xx, y] = ua * scale
    spot = gun.at[c, xx, y]
    for i in range(3):
        wire.start(spot, spot, yt[i], u0 + 13 + i, u0 + 13 + i)

    for i in range(3):
        wire.arrived(gxr.at[0], e0 + 1 + i)
    for b in range(4):
        acc = keep[0, xx, b]
        for i in range(3):
            acc = acc + gxr[i, b].astype(F32)
        keep[1, 0, b] = acc
        gy[b] = acc.astype(BF)
    for i in range(3):
        wire.start(gy.at[lax.rem(y + i + 1, 4)], gyr.at[i], yt[i], e0 + 4 + i, e0 + 4 + i)
    attend(4, 8)

    def att_part(p):
        return pl.ds(pl.multiple_of(mine + p * 512, 256), 512 if p == 0 else 256)

    def att_sends(p):
        lanes = slice(0, 512) if p == 0 else slice(512, HALF)
        m = e0 + 14 + p
        wire.start(att2.at[other, :, lanes], att.at[:, att_part(p)], sib, m, m)
        pltpu.make_async_copy(att2.at[c, :, lanes], att.at[:, att_part(p)], local.at[5 + p]).start()

    att_sends(0)

    for i in range(3):
        wire.arrived(spot, u0 + 13 + i)
    for i in range(3):
        for h, target in enumerate((xt[i], xo[i])):
            m = u0 + 16 + 2 * i + h
            wire.start(gun.at[c, xx], gun.at[c, xx], target, m, m)
    wire.start(gun.at[c, xx], gun.at[c, xx], sib, u0 + 22, u0 + 22)

    for i in range(3):
        wire.arrived(gyr.at[0], e0 + 4 + i)
    acc = keep[1, 0, y]
    for i in range(3):
        acc = acc + gyr[i].astype(F32)
    r_out = lax.broadcasted_iota(jnp.int32, (128, 96), 0)
    r_in = lax.broadcasted_iota(jnp.int32, (128, 96), 1)
    row_of = lax.div(r_out, 16) * 12 + lax.rem(r_out, 16)
    pick = jnp.where((row_of == r_in) & (lax.rem(r_out, 16) < 12), 1.0, 0.0).astype(BF)
    parts = jnp.dot(pick, acc.astype(BF), preferred_element_type=F32).astype(BF)
    for i in range(8):
        gz[i] = parts[i * 16 : (i + 1) * 16]
    for i in range(7):
        wire.start(gz.at[lax.rem(z + i + 1, 8)], gzr.at[i], zt[i], e0 + 7 + i, e0 + 7 + i)


    attend(8, 12)
    att_sends(1)

    for i in range(7):
        wire.arrived(gzr.at[0], e0 + 7 + i)
    acc = gz[z].astype(F32)
    for i in range(7):
        acc = acc + gzr[i].astype(F32)
    gd[...] = (acc * scale)[0:12]
    for i in range(7):
        wire.arrived(gun.at[c, xx], u0 + 16 + i)
    for cc in (0, 1):
        for i in (0, 2):
            lanes = pl.ds(cc * HALF + i * 192, 384)
            gu[:, lanes] = gun[cc, i : i + 2].reshape(384, 64).T
    for p in (0, 1):
        wire.arrived(att.at[:, att_part(p)], e0 + 14 + p)
        lanes = slice(0, 512) if p == 0 else slice(512, HALF)
        pltpu.make_async_copy(att2.at[c, :, lanes], att.at[:, att_part(p)], local.at[5 + p]).wait()
    wire.copy(bs.at[0], bs.at[0], sib, b0 + 12, b0 + 12).wait_send()
    ring.drain()
    wire.drain()


def distances():
    qp = np.arange(256)
    kp = np.arange(2304)
    kr = (kp // 768) * 16 + (kp % 256) // 16 - 16
    kc = (kp // 256 % 3) * 16 + kp % 16 - 16
    dr = kr[None] - (qp // 16)[:, None]
    dc = kc[None] - (qp % 16)[:, None]
    return (dr * dr + dc * dc).astype(np.float32)


def fused(*args):
    vm = pl.BlockSpec(memory_space=pltpu.VMEM)
    hb = pl.BlockSpec(memory_space=pl.ANY)
    return pl.pallas_call(
        kernel,
        out_shape=[
            jax.ShapeDtypeStruct((256, 1536), BF),
            jax.ShapeDtypeStruct((12, 64), F32),
            jax.ShapeDtypeStruct((64, 1536), F32),
        ],
        in_specs=[pl.BlockSpec(memory_space=pltpu.SMEM)] * 2 + [hb] * 4 + [vm] * 4,
        out_specs=[hb, vm, vm],
        scratch_shapes=[
            pltpu.VMEM((2, 256, HALF), BF),
            pltpu.VMEM((12, 256, WIDE), BF),
            pltpu.VMEM((2, 256, HALF), BF),
            pltpu.VMEM((2, 256, WIDE), BF),
            pltpu.VMEM((2, 256, 3072), BF),
            pltpu.VMEM((4, 2, 2, 2, 96, HALF), BF),
            pltpu.VMEM((2, 8, 2304), F32),
            pltpu.VMEM((16, 16, HALF), BF),
            pltpu.VMEM((2, 96, HALF), BF),
            pltpu.VMEM((16, 1536), BF),
            pltpu.VMEM((2, 4, 4, 48, 64), F32),
            pltpu.VMEM((12, 256, HALF), BF),
            pltpu.VMEM((256, 2304), F32),
            pltpu.VMEM((256, 2304), F32),
            pltpu.VMEM((12, 256, 2304), BF),
            pltpu.VMEM((12, 64, 256), F32),
            pltpu.VMEM((HALF, 128), F32),
            pltpu.VMEM((2, 256, HALF), BF),
            pltpu.VMEM((12, 64, 256), BF),
            pltpu.VMEM((12, 64, 256), BF),
            pltpu.VMEM((2, 4, 4, 96, 64), BF),
            pltpu.VMEM((4, 4, 96, 64), BF),
            pltpu.VMEM((2, 4, 4, 96, 64), F32),
            pltpu.VMEM((4, 4, 48, 64), BF),
            pltpu.VMEM((3, 4, 48, 64), BF),
            pltpu.VMEM((4, 48, 64), F32),
            pltpu.VMEM((4, 48, 64), BF),
            pltpu.VMEM((3, 48, 64), BF),
            pltpu.VMEM((48, 64), BF),
            pltpu.VMEM((8, 48, 64), BF),
            pltpu.VMEM((4, 4, 96, 64), BF),
            pltpu.VMEM((3, 4, 96, 64), BF),
            pltpu.VMEM((4, 96, 64), BF),
            pltpu.VMEM((3, 96, 64), BF),
            pltpu.VMEM((8, 16, 64), BF),
            pltpu.VMEM((7, 16, 64), BF),
            pltpu.SemaphoreType.DMA((138,)),
            pltpu.SemaphoreType.DMA((138,)),
            pltpu.SemaphoreType.DMA((8,)),
        ],
        compiler_params=pltpu.CompilerParams(
            collective_id=0, has_side_effects=True, vmem_limit_bytes=60 * MIB
        ),
        name="fused",
    )(*args)


def per_device(
    patch_tokens,
    queries,
    key_vectors,
    cotangent,
    value_weight,
    adapter_down,
    adapter_up,
    radius,
    tile_mask,
):
    att, gd, gu = fused(
        radius,
        tile_mask,
        queries.reshape(256, 1536),
        key_vectors.reshape(256, 1536),
        cotangent.reshape(256, 1536),
        patch_tokens.reshape(256, 3072),
        value_weight,
        adapter_down.T,
        adapter_up,
        jnp.asarray(distances()),
    )
    return att.reshape(16, 16, 1536), gd, gu


def solution(mesh):
    placed = (
        P("row", "col", None),
        P("row", "col", None),
        P("row", "col", None),
        P("row", "col", None),
        P(("row", "col"), None),
        P(),
        P(),
        P(),
        P("row", "col", None),
    )
    return jax.shard_map(
        per_device,
        mesh=mesh,
        in_specs=placed,
        out_specs=(P("row", "col", None), P(("row", "col"), None), P()),
        check_vma=False,
    )
```

```python
import jax
import jax.numpy as jnp
import numpy as np
from jax import lax
from jax.experimental import pallas as pl
from jax.experimental.pallas import tpu as pltpu
from jax.sharding import PartitionSpec as P

MESH = pl.DeviceIdType.MESH
BF = jnp.bfloat16
F32 = jnp.float32
HALF = 768
WIDE = 896
MIB = 2**20


def place():
    row = lax.axis_index("row")
    col = lax.axis_index("col")
    return row, col


def grid_place():
    row, col = place()
    y = lax.div(row, 4)
    x = lax.rem(lax.div(row, 2), 2) * 2 + lax.div(col, 8)
    return y, x, lax.rem(col, 8), lax.rem(row, 2)


def at_grid(y, x, z, c):
    y = lax.rem(y + 4, 4)
    x = lax.rem(x + 4, 4)
    z = lax.rem(z + 8, 8)
    return (y * 4 + lax.div(x, 2) * 2 + c, lax.rem(x, 2) * 8 + z)


def at_chip(k, h, col):
    return (lax.rem(k + 8, 8) * 2 + h, lax.rem(col + 16, 16))


def greet(targets):
    barrier = pltpu.get_barrier_semaphore()
    for target in targets:
        pl.semaphore_signal(barrier, inc=1, device_id=target, device_id_type=MESH)
    return lambda: pl.semaphore_wait(barrier, len(targets))


class Wire:
    def __init__(self, send, recv):
        self.send, self.recv, self.pending = send, recv, []

    def copy(self, src, dst, target, s, r):
        return pltpu.make_async_remote_copy(
            src_ref=src,
            dst_ref=dst,
            send_sem=self.send.at[s],
            recv_sem=self.recv.at[r],
            device_id=target,
            device_id_type=MESH,
        )

    def start(self, src, dst, target, s, r):
        copy = self.copy(src, dst, target, s, r)
        copy.start()
        self.pending.append(copy)

    def arrived(self, dst, r):
        row, col = place()
        self.copy(dst, dst, (row + 1 - 2 * lax.rem(row, 2), col), r, r).wait_recv()

    def drain(self):
        for copy in self.pending:
            copy.wait_send()
        self.pending = []


def chip_targets():
    row, col = place()
    k, c = lax.div(row, 2), lax.rem(row, 2)
    out = [at_chip(k, 1 - c, col)]
    for h in (0, 1):
        out += [at_chip(k + 1, h, col), at_chip(k - 1, h, col)]
        out += [at_chip(k, h, col + 1), at_chip(k, h, col - 1)]
    return out


def stretch(c):
    return pl.multiple_of(c * HALF, HALF)


def kernel(
    radius, mask, q, kv, cot, x, w, down, up, dist,
    att, gd, gu,
    q2, kwin, c2, keys_out, x2, wout, allow2, zbuf, wblk, wp, gun,
    vwin, s_one, s_two, p_ref, back, upt, att2,
    bs, br, gs, gr, keep, ux, uxr, ukeep, uy, uyr, uz, uzr, gx, gxr, gy, gyr, gz, gzr,
    send, recv, local,
):
    row, col = place()
    k, c = lax.div(row, 2), lax.rem(row, 2)
    y, xx, z, _ = grid_place()
    other = 1 - c
    mine = stretch(c)
    wire = Wire(send, recv)
    targets = chip_targets()
    for a in range(1, 8):
        targets += [at_grid(y, xx, z + a, 0), at_grid(y, xx, z + a, 1)]
    xt = [at_grid(y, xx + a, z, c) for a in (1, 2, 3)]
    yt = [at_grid(y + a, xx, z, c) for a in (1, 2, 3)]
    zt = [at_grid(y, xx, z + a, c) for a in range(1, 8)]
    xo = [at_grid(y, xx + a, z, other) for a in (1, 2, 3)]
    targets += xt + yt + xo
    targets += [at_chip(k, h, col + d) for d in (7, 8, 9) for h in (0, 1)]
    for h in (0, 1):
        for d in (1, -1):
            targets += [at_chip(k + 1, h, col + d), at_chip(k - 1, h, col + d)]
    sib = at_chip(k, other, col)
    theirs = stretch(other)

    locals_ = []

    def local_copy(src, dst):
        copy = pltpu.make_async_copy(src, dst, local.at[len(locals_)])
        copy.start()
        locals_.append(copy)
        return copy

    slot = c * 8 + z
    centre = (1 + c) * 3 + 1
    far = (3 - 3 * c) * 3 + 1
    step = 2 * c - 1

    crossing = ((0, 1, 7, 15), (1, -1, 8, 0))

    def side_sends(parts, win, rr, n, which):
        for h, target_core, src in parts:
            for i, d, hop, relay in crossing:
                spot, near = win.at[rr * 3 + 1 - d], win.at[rr * 3 + 1 + d]

                @pl.when((col != hop) & (col != relay))
                def _(h=h, i=i, d=d, src=src, target_core=target_core, spot=spot):
                    target = at_chip(k, target_core, col + d)
                    wire.copy(src, spot, target, n + 2 * i + h, n + 2 * i + which).start()

                @pl.when(col == hop)
                def _(h=h, i=i, src=src, target_core=target_core, near=near, relay=relay):
                    target = at_chip(k, target_core, jnp.int32(relay))
                    wire.copy(src, near, target, n + 2 * i + h, n + 2 * (1 - i) + which).start()

    def side_relay(win, n):
        for i, d, hop, relay in crossing:

            @pl.when(col == relay)
            def _(i=i, d=d, hop=hop):
                for t in (0, 1):
                    spot, near = win.at[(1 + t) * 3 + 1 - d], win.at[(1 + t) * 3 + 1 + d]
                    wire.arrived(near, n + 2 * (1 - i) + t)
                    m = n + 2 * i + t
                    wire.copy(near, spot, (row, jnp.int32(hop + d)), m, m).start()

    def side_arrivals(win, n):
        for i, edge in enumerate((0, 15)):

            @pl.when(col != edge)
            def _(i=i):
                wire.arrived(win.at[0], n + 2 * i)
                wire.arrived(win.at[0], n + 2 * i + 1)

        for m in range(4):
            wire.copy(win.at[0], win.at[0], sib, n + m, n + m).wait_send()

    def clear_edges(win):
        for edge, cc in ((0, 0), (15, 2)):

            @pl.when(col == edge)
            def _(cc=cc):
                for rr in (0, 3):
                    win[rr * 3 + cc] = jnp.zeros(win.shape[1:], win.dtype)

    def corner(win, m, rr):
        src = win.at[rr * 3 + 1]
        for i, d, _, edge in crossing:

            @pl.when(col != edge)
            def _(i=i, d=d):
                n = m + (2 if rr else 0) + i
                wire.copy(src, win.at[rr * 3 + 1 - d], at_chip(k, c, col + d), n, n).start()

    def corner_arrivals(win, m):
        for n in (m, m + 2):
            for i, edge in enumerate((0, 15)):

                @pl.when(col != edge)
                def _(n=n, i=i):
                    wire.arrived(win.at[0], n + i)

                @pl.when(col != 15 - edge)
                def _(n=n, i=i):
                    wire.copy(win.at[0], win.at[0], sib, n + i, n + i).wait_send()

    def keys_up():
        for h in (0, 1):
            wire.start(keys_out.at[h], kwin.at[far], at_chip(k + step, h, col), 16 + h, 16 + c)

    def keys_aside():
        parts = [(h, h, keys_out.at[h]) for h in (0, 1)]
        side_sends(parts, kwin, 1 + c, 18, c)

    met = greet(targets)
    own_x = local_copy(x, x2.at[c])
    own_k = local_copy(kv.at[:, pl.ds(mine, HALF)], kwin.at[centre, :, pl.ds(0, HALF)])
    for h in (0, 1):
        local_copy(kv.at[:, pl.ds(h * HALF, HALF)], keys_out.at[h, :, pl.ds(0, HALF)])
    local_copy(q.at[:, pl.ds(mine, HALF)], q2.at[c])
    local_copy(cot.at[:, pl.ds(mine, HALF)], c2.at[c])
    for n in range(9):
        r, t = row + n // 3 - 1, col + n % 3 - 1
        seen = (r >= 0) & (r < 16) & (t >= 0) & (t < 16) & (mask[0, 0, n] > 0)
        allow2[c, :, n * 256 : (n + 1) * 256] = jnp.full((8, 256), jnp.where(seen, 1.0, 0.0))
    r_out = lax.broadcasted_iota(jnp.int32, (16, 12), 0)
    r_in = lax.broadcasted_iota(jnp.int32, (16, 12), 1)
    wp[...] = jnp.dot(
        jnp.where(r_out == r_in, 1.0, 0.0).astype(BF), w[...], preferred_element_type=F32
    ).astype(BF)
    own_w = local_copy(wp.at[:, pl.ds(mine, HALF)], zbuf.at[slot])
    own_x.wait()
    low = lax.dot_general(
        x2[c], down[...], (((1,), (1,)), ((), ())), preferred_element_type=F32
    ).astype(BF)
    low = jnp.concatenate([low, jnp.zeros((256, 64), BF)], axis=1)
    for h in (0, 1):
        keys_out[h, :, HALF:WIDE] = low
    clear_edges(kwin)
    clear_edges(vwin)
    kwin[centre, :, HALF:WIDE] = low
    for copy in locals_[1:]:
        copy.wait()
    met()

    wire.start(wp.at[:, pl.ds(theirs, HALF)], zbuf.at[slot], sib, 0, 0)
    for a in range(1, 8):
        for h in (0, 1):
            hh = c if h == 0 else other
            wire.start(
                wp.at[:, pl.ds(stretch(hh), HALF)],
                zbuf.at[slot],
                at_grid(y, xx, z + a, hh),
                2 * a + h,
                2 * a + h,
            )
    keys_up()
    wire.start(keys_out.at[other], kwin.at[centre], sib, 22, 22)
    wire.start(q.at[:, pl.ds(theirs, HALF)], q2.at[c], sib, 30, 30)
    wire.start(cot.at[:, pl.ds(theirs, HALF)], c2.at[c], sib, 31, 31)
    wire.start(x, x2.at[c], sib, 32, 32)
    wire.start(allow2.at[c], allow2.at[c], sib, 33, 33)
    wire.arrived(zbuf.at[0], 0)
    for a in range(1, 8):
        for h in (0, 1):
            wire.arrived(zbuf.at[0], 2 * a + h)
    r_out = lax.broadcasted_iota(jnp.int32, (96, 128), 0)
    r_in = lax.broadcasted_iota(jnp.int32, (96, 128), 1)
    pick = jnp.where(lax.div(r_out, 12) * 16 + lax.rem(r_out, 12) == r_in, 1.0, 0.0).astype(BF)
    for cc in (0, 1):
        part = zbuf[pl.ds(cc * 8, 8)].reshape(128, HALF)
        wblk[cc] = jnp.dot(pick, part, preferred_element_type=F32).astype(BF)

    def x_part(i):
        i = lax.rem(i + 4, 4)
        return lax.div(i, 2), lax.rem(i, 2)

    def y_part(i):
        return lax.rem(i + 4, 4)

    def small(yi, xi):
        a, b = x_part(xi)
        return wout.at[y_part(yi), a, :, b]

    def small_half(yi, xi, j):
        a, b = x_part(xi)
        return wout.at[y_part(yi), a, j, b]

    own_copy = pltpu.make_async_copy(wblk, small(y, xx), local.at[7])
    own_copy.start()

    def corners(win, n, m):
        for rr, first in ((0, n + 1), (3, n)):
            wire.arrived(win.at[rr * 3 + 1], first)
            corner(win, m, rr)

    fx, fy = 1 - c, c
    ring = Wire(send, recv)
    one = [at_grid(y + d * fy, xx + d * fx, z, c) for d in (1, -1)]
    two = [at_grid(y + d * fx, xx + d * fy, z, c) for d in (1, -1)]
    w0 = 34
    at = (0, -1, 1, 2)

    def full(a, b):
        return small(y + a * fy + b * fx, xx + a * fx + b * fy)

    def half(a, b, j):
        return small_half(y + a * fy + b * fx, xx + a * fx + b * fy, j)

    def across(n, src):
        for i in (0, 1):
            m = w0 + 4 + 2 * n + i
            ring.start(src, full(at[n], 0), two[i], m, m)

    def pass_on(n):
        for i, d in enumerate((-1, 1)):
            ring.arrived(full(at[n], d), w0 + 4 + 2 * n + i)
            m = w0 + 12 + 2 * n + i
            ring.start(half(at[n], d, i), half(at[n], d, i), two[i], m, m)

    for i in (0, 1):
        ring.start(wblk, full(0, 0), one[i], w0 + i, w0 + i)
    across(0, wblk)
    keys_aside()
    for i, d in enumerate((-1, 1)):
        ring.arrived(full(d, 0), w0 + i)
        ring.start(half(d, 0, i), half(d, 0, i), one[i], w0 + 2 + i, w0 + 2 + i)
        across(1 + i, full(d, 0))
    corners(kwin, 16, 70)
    pass_on(0)
    for i in (0, 1):
        ring.arrived(half(2, 0, i), w0 + 2 + i)
    across(3, full(2, 0))
    side_relay(kwin, 18)
    pass_on(1)

    def heads(start, width):
        return pl.ds(pl.multiple_of(mine + start, 128), width)

    def keys_here():
        side_arrivals(kwin, 18)
        wire.arrived(q2.at[0], 30)
        wire.arrived(c2.at[0], 31)
        wire.arrived(allow2.at[0], 33)
        corner_arrivals(kwin, 70)

    back[...] = jnp.zeros_like(back)
    upt[...] = jnp.zeros_like(upt)

    def place_of(i):
        h, t = lax.div(i, 2), lax.rem(i, 2)
        return h, t, pl.ds(pl.multiple_of(h * 128, 128), 128)

    def score(i, to):
        h, t, lanes = place_of(i)
        keys = kwin[pl.ds(t * 3, 9), :, lanes].reshape(2304, 128)
        to[...] = lax.dot_general(
            q2[t, :, lanes], keys, (((1,), (1,)), ((), ())), preferred_element_type=F32
        )

    log_scale = 128**-0.5 * 1.4426950408889634

    def soften(i, s_ref):
        h, t, _ = place_of(i)
        reach = radius[c * 6 + h]
        limit = allow2[t, 0:1, :] * (reach * reach + 1).astype(F32) - 1.0
        for j in range(8):
            rows = slice(j * 32, (j + 1) * 32)
            s = jnp.where(dist[rows] <= limit, s_ref[rows], -1e30)
            e = jnp.exp2((s - jnp.max(s, axis=1, keepdims=True)) * log_scale)
            p_ref[i, rows] = (e * (1.0 / jnp.sum(e, axis=1, keepdims=True))).astype(BF)

    def gradient(i):
        h, t, lanes = place_of(i)
        vgt = jnp.dot(c2[t, :, lanes].T, p_ref[i], preferred_element_type=F32).astype(BF)
        bt = jnp.dot(up[:, heads(h * 128, 128)], vgt, preferred_element_type=F32)
        for n in range(9):
            back[t * 3 + n] += bt[:, n * 256 : (n + 1) * 256]
        lows = kwin[pl.ds(t * 3, 9), :, HALF:WIDE].reshape(2304, 128)
        upt[lanes] += jnp.dot(vgt, lows, preferred_element_type=F32)

    def probs(lo, hi):
        @pl.loop(lo, hi)
        def _(m):
            score(2 * m, s_one)
            score(2 * m + 1, s_two)
            soften(2 * m, s_one)
            soften(2 * m + 1, s_two)
            gradient(2 * m)
            gradient(2 * m + 1)

    def attend(lo, hi):
        for i in range(lo, hi):
            h, t = i // 2, i % 2
            lanes = slice(h * 128, (h + 1) * 128)
            vals = vwin[t * 3 : t * 3 + 9, :, lanes].reshape(2304, 128)
            att2[t, :, lanes] = jnp.dot(p_ref[i], vals, preferred_element_type=F32).astype(BF)

    pass_on(2)
    pass_on(3)
    for n in range(4):
        for i in (0, 1):
            ring.arrived(half(0, 2, i), w0 + 12 + 2 * n + i)
    own_copy.wait()

    wire.arrived(x2.at[0], 32)
    wire.arrived(kwin.at[0], 22)
    low2 = jnp.concatenate([kwin[4, :, HALF : HALF + 64], kwin[7, :, HALF : HALF + 64]], axis=0)

    @pl.loop(0, 3)
    def _(n):
        lanes = pl.ds(pl.multiple_of(n * 256, 256), 256)
        acc = jnp.dot(low2, up[:, heads(n * 256, 256)], preferred_element_type=F32)
        for yi in range(4):
            rows = wout[yi, :, :, :, :, lanes].reshape(768, 256)
            part = x2[:, :, yi * 768 : (yi + 1) * 768].reshape(512, 768)
            acc = acc + jnp.dot(part, rows, preferred_element_type=F32)
        acc = acc.astype(BF)
        vwin[4, :, lanes] = acc[:256]
        vwin[7, :, lanes] = acc[256:]

    v0 = 54
    wire.start(vwin.at[4], vwin.at[10], at_chip(k - 1, c, col), v0, v0)
    wire.start(vwin.at[7], vwin.at[1], at_chip(k + 1, c, col), v0 + 1, v0 + 1)
    for t in (0, 1):
        side_sends([(t, c, vwin.at[4 + 3 * t])], vwin, 1 + t, v0 + 2, t)

    keys_here()

    probs(0, 6)

    def values_here():
        side_arrivals(vwin, v0 + 2)
        corner_arrivals(vwin, 60)

    b0 = 78
    for n in range(12):
        rr, cc = n // 3, n % 3
        bs[n] = back[n].astype(BF)
        dk, h = ((-1, 1), (0, 0), (0, 1), (1, 0))[rr]
        slot = (0 if rr in (1, 2) else 6) + cc * 2
        if n in (4, 7):

            @pl.when(c != h)
            def _():
                wire.copy(bs.at[n], br.at[slot + c], sib, b0 + 12, b0 + slot + c).start()
        else:
            target = at_chip(k + dk, h, col + cc - 1)
            wire.start(bs.at[n], br.at[slot + c], target, b0 + n, b0 + slot + c)

    wire.arrived(vwin.at[10], v0)
    corner(vwin, 60, 3)
    wire.arrived(vwin.at[1], v0 + 1)
    corner(vwin, 60, 0)
    u0, e0 = 92, 120
    for a in range(4):
        for b in range(4):
            ux[a, b // 2, :, (b % 2) * 64 : (b % 2) * 64 + 64] = upt[(a * 4 + b) * 48 : (a * 4 + b + 1) * 48, 0:64].astype(BF)
    for i in range(3):
        wire.start(ux.at[lax.rem(xx + i + 1, 4)], uxr.at[i], xt[i], u0 + i, u0 + i)

    side_relay(vwin, v0 + 2)
    total = back[(1 + c) * 3 + 1]
    wire.arrived(br.at[0], b0 + 2 + other)
    total = total + br[2 + other].astype(F32)
    for slot in range(12):
        if slot not in (2, 3):
            wire.arrived(br.at[0], b0 + slot)
            total = total + br[slot].astype(F32)
    hi = total.astype(BF)
    lo = (total - hi.astype(F32)).astype(BF)
    both = jnp.concatenate([hi, lo], axis=0)

    for i in range(3):
        wire.arrived(uxr.at[0], u0 + i)
    for b in range(4):
        ua = upt[pl.ds(pl.multiple_of((xx * 4 + b) * 48, 16), 48), 0:64]
        for i in range(3):
            ua = ua + uxr[i, b // 2, :, (b % 2) * 64 : (b % 2) * 64 + 64].astype(F32)
        ukeep[b] = ua
        uy[b] = ua.astype(BF)
    for i in range(3):
        wire.start(uy.at[lax.rem(y + i + 1, 4)], uyr.at[i], yt[i], u0 + 3 + i, u0 + 3 + i)

    for i in range(8):
        part = x2[c, :, i * 384 : (i + 1) * 384]
        g = jnp.dot(both, part, preferred_element_type=F32)
        g = (g[:64] + g[64:]).T
        yi, xhi = i // 2, i % 2
        for cc in (0, 1):
            for xl in (0, 1):
                rows = g[(cc * 2 + xl) * 96 : (cc * 2 + xl + 1) * 96]
                keep[cc, xhi * 2 + xl, yi] = rows
                gs[cc, xhi * 2 + xl, yi] = rows.astype(BF)

    wire.start(gs.at[other], gr, sib, e0, e0)

    for i in range(3):
        wire.arrived(uyr.at[0], u0 + 3 + i)
    ua = ukeep[y]
    for i in range(3):
        ua = ua + uyr[i].astype(F32)
    uz[...] = ua.astype(BF)
    uzr[z] = ua.astype(BF)
    for i in range(7):
        wire.start(uz, uzr.at[z], zt[i], u0 + 6 + i, u0 + 6 + i)

    wire.arrived(gr, e0)
    for a in range(4):
        for b in range(4):
            full = keep[c, a, b] + gr[a, b].astype(F32)
            keep[0, a, b] = full
            gx[a, b // 2, :, (b % 2) * 64 : (b % 2) * 64 + 64] = full.astype(BF)
    for i in range(3):
        wire.start(gx.at[lax.rem(xx + i + 1, 4)], gxr.at[i], xt[i], e0 + 1 + i, e0 + 1 + i)
    values_here()
    attend(0, 4)

    scale = 65536**-0.5
    for i in range(7):
        wire.arrived(uz, u0 + 6 + i)
    ua = uzr[0].astype(F32)
    for i in range(1, 8):
        ua = ua + uzr[i].astype(F32)
    gun[c, xx, y] = ua * scale
    spot = gun.at[c, xx, y]
    for i in range(3):
        wire.start(spot, spot, yt[i], u0 + 13 + i, u0 + 13 + i)

    for i in range(3):
        wire.arrived(gxr.at[0], e0 + 1 + i)
    for b in range(4):
        acc = keep[0, xx, b]
        for i in range(3):
            acc = acc + gxr[i, b // 2, :, (b % 2) * 64 : (b % 2) * 64 + 64].astype(F32)
        keep[1, 0, b] = acc
        gy[b] = acc.astype(BF)
    for i in range(3):
        wire.start(gy.at[lax.rem(y + i + 1, 4)], gyr.at[i], yt[i], e0 + 4 + i, e0 + 4 + i)
    attend(4, 8)

    def att_part(p):
        return pl.ds(pl.multiple_of(mine + p * 512, 256), 512 if p == 0 else 256)

    def att_sends(p):
        lanes = slice(0, 512) if p == 0 else slice(512, HALF)
        m = e0 + 14 + p
        wire.start(att2.at[other, :, lanes], att.at[:, att_part(p)], sib, m, m)
        pltpu.make_async_copy(att2.at[c, :, lanes], att.at[:, att_part(p)], local.at[5 + p]).start()

    att_sends(0)

    for i in range(3):
        wire.arrived(spot, u0 + 13 + i)
    for i in range(3):
        for h, target in enumerate((xt[i], xo[i])):
            m = u0 + 16 + 2 * i + h
            wire.start(gun.at[c, xx], gun.at[c, xx], target, m, m)
    wire.start(gun.at[c, xx], gun.at[c, xx], sib, u0 + 22, u0 + 22)

    for i in range(3):
        wire.arrived(gyr.at[0], e0 + 4 + i)
    acc = keep[1, 0, y]
    for i in range(3):
        acc = acc + gyr[i].astype(F32)
    r_out = lax.broadcasted_iota(jnp.int32, (128, 96), 0)
    r_in = lax.broadcasted_iota(jnp.int32, (128, 96), 1)
    row_of = lax.div(r_out, 16) * 12 + lax.rem(r_out, 16)
    pick = jnp.where((row_of == r_in) & (lax.rem(r_out, 16) < 12), 1.0, 0.0).astype(BF)
    parts = jnp.dot(pick, acc.astype(BF), preferred_element_type=F32).astype(BF)
    for i in range(8):
        gz[i] = parts[i * 16 : (i + 1) * 16]
    for i in range(7):
        wire.start(gz.at[lax.rem(z + i + 1, 8)], gzr.at[i], zt[i], e0 + 7 + i, e0 + 7 + i)


    attend(8, 12)
    att_sends(1)

    for i in range(7):
        wire.arrived(gzr.at[0], e0 + 7 + i)
    acc = gz[z].astype(F32)
    for i in range(7):
        acc = acc + gzr[i].astype(F32)
    gd[...] = (acc * scale)[0:12]
    for i in range(7):
        wire.arrived(gun.at[c, xx], u0 + 16 + i)
    for cc in (0, 1):
        for i in (0, 2):
            lanes = pl.ds(cc * HALF + i * 192, 384)
            gu[:, lanes] = gun[cc, i : i + 2].reshape(384, 64).T
    for p in (0, 1):
        wire.arrived(att.at[:, att_part(p)], e0 + 14 + p)
        lanes = slice(0, 512) if p == 0 else slice(512, HALF)
        pltpu.make_async_copy(att2.at[c, :, lanes], att.at[:, att_part(p)], local.at[5 + p]).wait()
    wire.copy(bs.at[0], bs.at[0], sib, b0 + 12, b0 + 12).wait_send()
    ring.drain()
    wire.drain()


def distances():
    qp = np.arange(256)
    kp = np.arange(2304)
    kr = (kp // 768) * 16 + (kp % 256) // 16 - 16
    kc = (kp // 256 % 3) * 16 + kp % 16 - 16
    dr = kr[None] - (qp // 16)[:, None]
    dc = kc[None] - (qp % 16)[:, None]
    return (dr * dr + dc * dc).astype(np.float32)


def fused(*args):
    vm = pl.BlockSpec(memory_space=pltpu.VMEM)
    hb = pl.BlockSpec(memory_space=pl.ANY)
    return pl.pallas_call(
        kernel,
        out_shape=[
            jax.ShapeDtypeStruct((256, 1536), BF),
            jax.ShapeDtypeStruct((12, 64), F32),
            jax.ShapeDtypeStruct((64, 1536), F32),
        ],
        in_specs=[pl.BlockSpec(memory_space=pltpu.SMEM)] * 2 + [hb] * 4 + [vm] * 4,
        out_specs=[hb, vm, vm],
        scratch_shapes=[
            pltpu.VMEM((2, 256, HALF), BF),
            pltpu.VMEM((12, 256, WIDE), BF),
            pltpu.VMEM((2, 256, HALF), BF),
            pltpu.VMEM((2, 256, WIDE), BF),
            pltpu.VMEM((2, 256, 3072), BF),
            pltpu.VMEM((4, 2, 2, 2, 96, HALF), BF),
            pltpu.VMEM((2, 8, 2304), F32),
            pltpu.VMEM((16, 16, HALF), BF),
            pltpu.VMEM((2, 96, HALF), BF),
            pltpu.VMEM((16, 1536), BF),
            pltpu.VMEM((2, 4, 4, 48, 64), F32),
            pltpu.VMEM((12, 256, HALF), BF),
            pltpu.VMEM((256, 2304), F32),
            pltpu.VMEM((256, 2304), F32),
            pltpu.VMEM((12, 256, 2304), BF),
            pltpu.VMEM((12, 64, 256), F32),
            pltpu.VMEM((HALF, 128), F32),
            pltpu.VMEM((2, 256, HALF), BF),
            pltpu.VMEM((12, 64, 256), BF),
            pltpu.VMEM((12, 64, 256), BF),
            pltpu.VMEM((2, 4, 4, 96, 64), BF),
            pltpu.VMEM((4, 4, 96, 64), BF),
            pltpu.VMEM((2, 4, 4, 96, 64), F32),
            pltpu.VMEM((4, 2, 48, 128), BF),
            pltpu.VMEM((3, 2, 48, 128), BF),
            pltpu.VMEM((4, 48, 64), F32),
            pltpu.VMEM((4, 48, 64), BF),
            pltpu.VMEM((3, 48, 64), BF),
            pltpu.VMEM((48, 64), BF),
            pltpu.VMEM((8, 48, 64), BF),
            pltpu.VMEM((4, 2, 96, 128), BF),
            pltpu.VMEM((3, 2, 96, 128), BF),
            pltpu.VMEM((4, 96, 64), BF),
            pltpu.VMEM((3, 96, 64), BF),
            pltpu.VMEM((8, 16, 64), BF),
            pltpu.VMEM((7, 16, 64), BF),
            pltpu.SemaphoreType.DMA((138,)),
            pltpu.SemaphoreType.DMA((138,)),
            pltpu.SemaphoreType.DMA((8,)),
        ],
        compiler_params=pltpu.CompilerParams(
            collective_id=0, has_side_effects=True, vmem_limit_bytes=60 * MIB
        ),
        name="fused",
    )(*args)


def per_device(
    patch_tokens,
    queries,
    key_vectors,
    cotangent,
    value_weight,
    adapter_down,
    adapter_up,
    radius,
    tile_mask,
):
    att, gd, gu = fused(
        radius,
        tile_mask,
        queries.reshape(256, 1536),
        key_vectors.reshape(256, 1536),
        cotangent.reshape(256, 1536),
        patch_tokens.reshape(256, 3072),
        value_weight,
        adapter_down.T,
        adapter_up,
        jnp.asarray(distances()),
    )
    return att.reshape(16, 16, 1536), gd, gu


def solution(mesh):
    placed = (
        P("row", "col", None),
        P("row", "col", None),
        P("row", "col", None),
        P("row", "col", None),
        P(("row", "col"), None),
        P(),
        P(),
        P(),
        P("row", "col", None),
    )
    return jax.shard_map(
        per_device,
        mesh=mesh,
        in_specs=placed,
        out_specs=(P("row", "col", None), P(("row", "col"), None), P()),
        check_vma=False,
    )
```
